32 devices in a mesh: particle: 8 (over y, x, core), shard: 4 (over z).
Axes of the slice: x: 2, y: 2, z: 4, core: 2. Of those that a mesh axis runs over, the one named last changes fastest.
Arguments:
- pool: bfloat16 [4096, 1024], P('shard'), may hold values from -6 to 6
- batch_index: int32 [2048], P('shard'), may hold values from 0 to 1023
- kernel_scale: int32 [1], replicated, may hold values from 4194304 to 8388607
- cotangent: bfloat16 [8, 2048, 1024], P('particle', 'shard'), may hold values from -6 to 6
- weights: float32 [8, 1024, 2, 2048], P('particle', 'shard'), may hold values from -10 to 10
- first_moment: float32 [8, 1024, 2, 2048], P('particle', 'shard'), may hold values from -2 to 2
- second_moment: float32 [8, 1024, 2, 2048], P('particle', 'shard'), may hold values from 0.01 to 1
Outputs:
- new_weights: float32 [8, 1024, 2, 2048], P('particle', 'shard')
- new_first: float32 [8, 1024, 2, 2048], P('particle', 'shard')
- new_second: float32 [8, 1024, 2, 2048], P('particle', 'shard')
- transport: float32 [8, 1024, 2, 2048], P('particle', 'shard')
The draws below stay inside these ranges and needn't reach their ends.
Inputs may be any that keep to these rules, and one draw needn't show every extreme that they name: `batch_index`: each entry names a row of the pool block that the same index of shard holds.
All inputs are finite; a program needn't handle non-finite values.
Results may differ from the reference program's by a relative error of at most 0.015.
Values may be sent and summed in bfloat16 or wider, within the bound.
No kernel may reach another device: no remote copies, remote signals or barrier semaphores. Data moves between devices by JAX's collectives and lax.ppermute only.
A program may use at most 192 MiB of HBM per device.

```python
import math
import jax
import jax.numpy as jnp
from jax import lax

D = 1024
FF = 2048
TOK_DEV = 512
POOL_DEV = 1024
PARTICLES = 8
TOKENS = 2048
POOL = 4096
PARAMS = 4194304


def draw_weights(key, part):
    base_key, noise_key, spread_key = jax.random.split(jax.random.fold_in(key, 17), 3)
    shape_full = (PARTICLES, D, 2, FF)
    shape_base = (1, D, 2, FF)
    row_pos = (jnp.arange(D, dtype=jnp.float32) + 0.5) / D - 0.5
    rise = jnp.exp(0.5 * jnp.log(3.0) * row_pos)[None, :, None, None]
    spread = jnp.exp(jax.random.uniform(spread_key, (PARTICLES, 1, 1, 1), jnp.float32, jnp.log(0.3), jnp.log(1.2)))
    base_part = jax.random.truncated_normal(base_key, -3.0, 3.0, shape_base, jnp.float32)
    noise_part = jax.random.truncated_normal(noise_key, -3.0, 3.0, shape_full, jnp.float32)
    return (base_part + spread * rise * noise_part).astype(jnp.float32)


def place_ends(entries, rng, low, largest):
    longest = entries.shape.index(max(entries.shape))
    spots = []
    for shift in (0, 1):
        where = [jax.random.randint(jax.random.fold_in(rng, axis), (), 0, length) for axis, length in enumerate(entries.shape)]
        where[longest] = (where[longest] + shift) % entries.shape[longest]
        spots.append(tuple(where))
    return entries.at[spots[0]].set(low).at[spots[1]].set(largest)


def levels(rng, dims, shards, least, top_value):
    factor_of = 1.0
    for axis_at, shards_of in shards:
        heights = jax.random.uniform(jax.random.fold_in(jax.random.fold_in(rng, 6), axis_at), (shards_of,), jnp.float32, least / len(shards), top_value / len(shards))
        factor_of = factor_of * jnp.repeat(jnp.exp(heights), dims[axis_at] // shards_of).reshape((-1,) + (1,) * (len(dims) - 1 - axis_at))
    return factor_of


def scatter_about(rng, shape, width, limit, cuts=(), held_as=jnp.bfloat16):
    array = jax.random.normal(rng, shape, jnp.float32) * width
    if len(cuts) > 0:
        array = levels(rng, shape, cuts, -0.22, 0.18) * array
    return jnp.clip(array, min=-limit, max=limit).astype(held_as)


def setup_inputs(seed: int = 0) -> dict:
    splits = jax.random.split(jax.random.key(seed), 8)
    pool = scatter_about(splits[0], (POOL, D), 1.0, 6.0, ((0, 4),))
    batch_index = place_ends(jax.random.randint(splits[1], (TOKENS,), 0, POOL_DEV), jax.random.fold_in(splits[1], 1), 0, POOL_DEV - 1).astype(jnp.int32)
    kernel_scale = jax.random.randint(splits[2], (1,), PARAMS, 2 * PARAMS).astype(jnp.int32)
    cotangent = scatter_about(splits[3], (PARTICLES, TOKENS, D), 1.0, 6.0, ((0, 8), (1, 4)))
    weights = draw_weights(jax.random.fold_in(splits[7], 71), 0)
    first_moment = scatter_about(splits[5], (PARTICLES, D, 2, FF), 0.3, 2.0, ((0, 8), (1, 4)), jnp.float32)
    second_moment = jnp.clip(jnp.exp(math.log(1.0) - 4.6051702 * jax.random.uniform(splits[6], (PARTICLES, D, 2, FF), jnp.float32) ** levels(splits[6], (PARTICLES, D, 2, FF), ((0, 8), (1, 4)), -0.2, 0.2)), 0.01, 1.0)
    return dict(pool=pool, batch_index=batch_index, kernel_scale=kernel_scale, cotangent=cotangent, weights=weights, first_moment=first_moment, second_moment=second_moment)


def gelu_pair(up_proj):
    cdf_part = 0.5 * (1.0 + jax.scipy.special.erf(up_proj * 0.7071067811865476))
    density = jnp.exp(-0.5 * up_proj * up_proj) * 0.3989422804014327
    return (up_proj * cdf_part, cdf_part + up_proj * density)

def reference(pool, batch_index, kernel_scale, cotangent, weights, first_moment, second_moment):
    offsets = jnp.arange(TOKENS, dtype=jnp.int32) // TOK_DEV * POOL_DEV
    picked = pool[(batch_index + offsets).astype(jnp.int32)].astype(jnp.float32)
    normed = (picked * lax.rsqrt(lax.optimization_barrier(jnp.mean(picked * picked, axis=1, keepdims=True)) + 1e-06)).astype(jnp.bfloat16)
    grad_scale = 1.0 / (TOKENS * D)

    def particle_score(particle_pair):
        particle_w, upstream = particle_pair
        wb_rows = particle_w.astype(jnp.bfloat16)
        up_proj = jnp.dot(normed, wb_rows[:, 0, :], preferred_element_type=jnp.float32) * D ** (-0.5)
        back_proj = jnp.dot(upstream, wb_rows[:, 1, :], preferred_element_type=jnp.float32) * FF ** (-0.5)
        act_full, gelu_slope = gelu_pair(up_proj)
        activation = act_full.astype(jnp.bfloat16)
        up_grad = (back_proj * gelu_slope).astype(jnp.bfloat16)
        g_up = jnp.dot(normed.T, up_grad, preferred_element_type=jnp.float32) * (D ** (-0.5) * grad_scale)
        g_down = jnp.dot(upstream.T, activation, preferred_element_type=jnp.float32) * (FF ** (-0.5) * grad_scale)
        return (-jnp.stack([g_up, g_down], axis=1)).astype(jnp.bfloat16)
    scores = lax.map(particle_score, (weights, cotangent))
    inverse_band = 1.0 / kernel_scale[0].astype(jnp.float32)
    repulse = 2.0 * inverse_band
    rounded_w = lax.optimization_barrier(weights.astype(jnp.bfloat16)).astype(jnp.float32)

    def distance_row(own_row):
        offset_sq = own_row[None] - rounded_w
        return lax.optimization_barrier(jnp.sum(offset_sq * offset_sq, axis=(1, 2, 3)))
    distances = lax.map(distance_row, rounded_w)
    kernel = jnp.exp(-distances * inverse_band)
    pushed_field = scores.astype(jnp.float32) - repulse * rounded_w

    def weighted_row(kernel_row):
        term_rows = (kernel_row[:, None, None, None] * pushed_field).astype(jnp.bfloat16)
        return lax.optimization_barrier(jnp.sum(lax.optimization_barrier(term_rows).astype(jnp.float32), axis=0))
    weighted = lax.map(weighted_row, kernel)
    kernel_total = lax.optimization_barrier(jnp.sum(kernel, axis=1))[:, None, None, None]
    transport = PARAMS / PARTICLES * (weighted + repulse * kernel_total * rounded_w)
    new_first = 0.9 * first_moment - 0.1 * transport
    new_second = 0.999 * second_moment + 0.001 * transport * transport
    new_weights = weights - 0.01 * new_first / (jnp.sqrt(new_second) + 1e-08)
    return (new_weights, new_first, new_second, transport)
```

```python
import functools

import jax
import jax.numpy as jnp
from jax import lax
from jax.experimental import pallas as pl
from jax.experimental.pallas import tpu as pltpu
from jax.sharding import PartitionSpec as P

BF = jnp.bfloat16
F32 = jnp.float32
AXES = ("particle", "shard")
LANES = 128
BLOCK = 256
MIB = 1024 * 1024
NT = (((1,), (1,)), ((), ()))

COL, CORE, SHARD, PROC, PIECE = range(5)


def any_spec():
    return pl.BlockSpec(memory_space=pl.ANY)


def smem_spec():
    return pl.BlockSpec(memory_space=pltpu.SMEM)


def params(mib):
    return pltpu.CompilerParams(vmem_limit_bytes=mib * MIB)


def run_copies(copies):
    for copy in copies:
        copy.start()
    for copy in copies:
        copy.wait()


def slice_index(ids, column, core, shard, columns):
    return 2 * lax.rem(column - shard + columns * 16, columns) + core


def split_kernel(shards, ids, w, *out):
    _, rows, piece = out[0].shape
    tiles = piece // LANES
    stride = 2 * shards * tiles
    for r in range(shards):
        first = lax.rem(ids[SHARD] - r + shards, shards) * tiles
        for kind in range(2):
            for j in range(tiles):
                part = w[pl.ds(2 * (first + j) + kind, rows, stride=stride), :]
                out[r][kind, :, j * LANES : (j + 1) * LANES] = part.astype(BF)


def slice_kernel(ids, w, out):
    particles, _, rows, cols = out.shape
    tiles = cols // LANES
    stride = 2 * particles * tiles
    for p in range(particles):
        first = slice_index(ids, p // 2, p % 2, ids[SHARD], particles // 2) * tiles
        for kind in range(2):
            for j in range(tiles):
                part = w[pl.ds(2 * (first + j) + kind, rows, stride=stride), :]
                out[p, kind, :, j * LANES : (j + 1) * LANES] = part.astype(BF)


def up_kernel(shards, scale, ids, tokens, *refs):
    pieces = refs[:shards]
    act_t, slope_t, down_t, normed, up_w, down_w, up_t = refs[shards:]
    width, part = up_w.shape
    rows = width // shards

    @pl.when(pl.program_id(0) == 0)
    def _():
        for r in range(shards):
            at = pl.multiple_of(lax.rem(ids[PIECE] + r, shards) * rows, rows)
            up_w[pl.ds(at, rows), :] = pieces[r][0]
            down_w[pl.ds(at, rows), :] = pieces[r][1]
        for i in range(width // LANES):
            span = slice(i * LANES, (i + 1) * LANES)
            up_t[:, span] = up_w[span, :].astype(F32).T.astype(BF)
            down_t[:, span] = down_w[span, :].astype(F32).T.astype(BF)

    block = tokens[...].reshape(normed.shape)
    normed[...] = block
    u = lax.dot_general(up_t[...], block, NT, preferred_element_type=F32) * scale
    cdf = 0.5 * (1.0 + lax.erf(u * 0.7071067811865476))
    density = jnp.exp(-0.5 * u * u) * 0.3989422804014327
    act_t[...] = (u * cdf).astype(BF)
    slope_t[...] = (cdf + u * density).astype(BF)


def grad_kernel(shards, particles, up_scale, down_scale, back_scale, pick, ids, normed, act_t, slope_t, down_t, *refs):
    n_in = len(refs) - particles - 8
    sources, out = refs[:n_in], refs[n_in : n_in + particles]
    c, n, act, slope, grad, down, score, sems = refs[n_in + particles :]
    part, tokens = act.shape
    width = c.shape[1]
    chunk = tokens // shards
    first = [
        pltpu.make_async_copy(down_t, down, sems.at[2 * shards]),
        pltpu.make_async_copy(slope_t, slope, sems.at[2 * shards + 1]),
    ]
    later = [
        pltpu.make_async_copy(act_t, act, sems.at[2 * shards + 2]),
        pltpu.make_async_copy(normed, n, sems.at[2 * shards + 3]),
    ]
    for copy in first:
        copy.start()
    pick(ids, sources, c, sems)
    for copy in later:
        copy.start()
    for copy in first:
        copy.wait()

    def back(i, carry):
        for turn in range(2):
            here = c.at[pl.ds(0, chunk // 2), :]
            pltpu.make_async_copy(here, here, sems.at[2 * i + turn]).wait()
        at = pl.multiple_of(i * chunk, chunk)
        b = lax.dot_general(down[...], c[pl.ds(at, chunk), :], NT, preferred_element_type=F32)
        grad[:, pl.ds(at, chunk)] = (b * (slope[:, pl.ds(at, chunk)].astype(F32) * back_scale)).astype(BF)
        return carry

    lax.fori_loop(0, shards, back, 0)
    for copy in later:
        copy.wait()

    def gradient(j, carry):
        at = pl.multiple_of(j * BLOCK, BLOCK)
        g = jnp.dot(grad[...], n[:, pl.ds(at, BLOCK)], preferred_element_type=F32)
        score[0, pl.ds(at, BLOCK), :] = (g * up_scale).T.astype(BF)
        g = jnp.dot(act[...], c[:, pl.ds(at, BLOCK)], preferred_element_type=F32)
        score[1, pl.ds(at, BLOCK), :] = (g * down_scale).T.astype(BF)
        return carry

    lax.fori_loop(0, width // BLOCK, gradient, 0)
    rows = width // shards
    ratio = particles // shards
    cols = part // ratio
    mine = 2 * ids[COL] + ids[PROC]
    copies = []
    for t in range(particles):
        u = lax.rem(mine + ratio * ids[PIECE] - t + particles, particles)
        row = pl.multiple_of(lax.div(u, ratio) * rows, rows)
        col = pl.multiple_of(lax.rem(u, ratio) * cols, cols)
        copies.append(pltpu.make_async_copy(score.at[:, pl.ds(row, rows), pl.ds(col, cols)], out[t], sems.at[t]))
    run_copies(copies)


def distance_kernel(whole, out):
    particles, _, rows, cols = whole.shape
    pairs = [(i, j) for i in range(particles) for j in range(i)]
    tiles = cols // LANES

    def body(g, acc):
        kind = lax.div(g, rows // 16)
        row = pl.multiple_of(lax.rem(g, rows // 16) * 16, 16)
        for tile in range(tiles):
            w = [whole[p, kind, pl.ds(row, 16), tile * LANES : (tile + 1) * LANES].astype(F32) for p in range(particles)]
            new = []
            for a, (i, j) in zip(acc, pairs):
                d = w[i] - w[j]
                d = d * d
                new.append(a + (d[:8] + d[8:]))
            acc = tuple(new)
        return acc

    acc = lax.fori_loop(0, 2 * rows // 16, body, tuple(jnp.zeros((8, LANES), F32) for _ in pairs))
    for i, a in enumerate(acc):
        out[i] = a


def stein_kernel(shards, particles, ids, coef, whole, *refs):
    sources, out = refs[:particles], refs[particles : 2 * particles]
    scores, field, sems = refs[2 * particles :]
    columns = particles // 2
    ratio = particles // shards
    _, _, rows, cols = whole.shape
    e = slice_index(ids, ids[COL], ids[CORE], ids[SHARD], columns)
    u = ids[SHARD] * ratio + lax.rem(e, ratio) + particles * shards - ratio * lax.div(e, ratio)
    run_copies(
        [pltpu.make_async_copy(sources[t], scores.at[lax.rem(u + t, particles)], sems.at[t]) for t in range(particles)]
    )
    repulse = coef[particles * particles + particles]
    groups = rows // 16
    tiles = cols // LANES

    def body(g, carry):
        kind = lax.div(g, groups)
        row = pl.multiple_of(lax.rem(g, groups) * 16, 16)
        for tile in range(tiles):
            at = (kind, pl.ds(row, 16), slice(tile * LANES, (tile + 1) * LANES))
            w = [whole[(p,) + at].astype(F32) for p in range(particles)]
            pushed = [scores[(p,) + at].astype(F32) - repulse * w[p] for p in range(particles)]
            for i in range(particles):
                total = coef[particles * particles + i] * w[i]
                for j in range(particles):
                    total = total + coef[i * particles + j] * pushed[j]
                field[(i,) + at] = total.astype(BF)
        return carry

    lax.fori_loop(0, 2 * groups, body, 0)
    copies = []
    for k in range(columns):
        for x in range(2):
            column = lax.rem(ids[COL] + k, columns)
            core = ids[CORE] if x == 0 else 1 - ids[CORE]
            i = 2 * k + x
            copies.append(pltpu.make_async_copy(field.at[2 * column + core], out[i], sems.at[i]))
    run_copies(copies)


def adam_kernel(particles, ids, w, first, second, *refs):
    sources = refs[:particles]
    new_w, new_first, new_second, transport, field, sems = refs[particles:]
    columns = particles // 2
    _, _, hidden = field.shape
    width = hidden // particles
    step = pl.program_id(0)

    @pl.when(step == 0)
    def _():
        copies = []
        for k in range(columns):
            for x in range(2):
                column = lax.rem(ids[COL] - k + columns, columns)
                core = ids[CORE] if x == 0 else 1 - ids[CORE]
                at = pl.multiple_of(slice_index(ids, column, core, ids[SHARD], columns) * width, width)
                i = 2 * k + x
                copies.append(pltpu.make_async_copy(sources[i], field.at[:, :, pl.ds(at, width)], sems.at[i]))
        run_copies(copies)

    lane_tiles = hidden // LANES
    rows = w.shape[0] // (2 * lane_tiles)
    base = pl.multiple_of(step * rows, rows)
    for kind in range(2):
        for tile in range(lane_tiles):
            part = field[kind, pl.ds(base, rows), tile * LANES : (tile + 1) * LANES]
            transport[pl.ds(2 * tile + kind, rows, stride=2 * lane_tiles), :] = part.astype(F32)
    t = transport[...]
    m = 0.9 * first[...] - 0.1 * t
    v = 0.999 * second[...] + 0.001 * t * t
    new_first[...] = m
    new_second[...] = v
    new_w[...] = w[...] - 0.01 * m / (jnp.sqrt(v) + 1e-08)


def local(pool, batch_index, kernel_scale, cotangent, weights, first_moment, second_moment):
    shards = lax.axis_size("shard")
    particles = lax.axis_size("particle")
    columns, half = particles // 2, shards // 2
    tok_rows = batch_index.shape[0]
    width = pool.shape[1]
    _, rows, _, hidden = weights.shape
    part, cols = hidden // shards, hidden // particles
    tokens = tok_rows * shards
    blocks = tokens // BLOCK
    lane_tiles = hidden // LANES

    own = lax.axis_index("particle")
    shard = lax.axis_index("shard")
    core, column = own % 2, own // 2
    proc = shard // half
    piece = 2 * (shard % half) + core
    ids = jnp.stack([column, core, shard, proc, piece]).astype(jnp.int32)
    devices = [(m, c, s) for m in range(columns) for c in range(2) for s in range(shards)]

    def dev(m, c, s):
        return (2 * (m % columns) + c) * shards + s

    def move(x, pairs):
        if all(a == b for a, b in pairs) and len(pairs) == len(devices):
            return x
        return lax.ppermute(x, AXES, pairs)

    def swap_of(among):
        return [(dev(m, c, s), dev(m, 1 - c, s)) for m, c, s in devices if s in among]

    def flat(x):
        return x[0].reshape(rows, 2, lane_tiles, LANES).transpose(0, 2, 1, 3).reshape(-1, LANES)

    def unflat(x):
        return x.reshape(rows, lane_tiles, 2, LANES).transpose(0, 2, 1, 3).reshape(1, rows, 2, hidden)

    everyone = range(shards)
    half_rows = tok_rows // 2
    if shards == 4:
        mine = lax.dynamic_slice(cotangent[0], (core * half_rows, 0), (half_rows, width))
        give = lax.dynamic_slice(cotangent[0], ((1 - core) * half_rows, 0), (half_rows, width))
        other = move(give, swap_of(everyone))
        is_own = core == proc
        here = jnp.where(is_own, mine, other)
        away = jnp.where(is_own, other, mine)

    share = tok_rows // particles
    index = lax.dynamic_slice(batch_index, (own * share,), (share,))
    picked = jnp.take(pool, index, axis=0).astype(F32)
    normed = (picked * lax.rsqrt(jnp.mean(picked * picked, axis=1, keepdims=True) + 1e-06)).astype(BF)
    normed = lax.all_to_all(jnp.broadcast_to(normed[None], (shards, share, width)), "shard", 0, 0, tiled=True)
    normed = lax.all_gather(normed[None], "particle", axis=0, tiled=True)

    w_flat = flat(weights)
    steps = max(rows // 64, 1)
    lines = w_flat.shape[0] // steps
    w_spec = pl.BlockSpec((lines, LANES), lambda i: (i, 0))
    prepared = pl.pallas_call(
        functools.partial(split_kernel, shards),
        grid=(steps,),
        out_shape=[jax.ShapeDtypeStruct((2, rows, part), BF)] * shards,
        in_specs=[smem_spec(), w_spec],
        out_specs=[pl.BlockSpec((2, rows // steps, part), lambda i: (0, i, 0))] * shards,
        compiler_params=params(8),
        name="split",
    )(ids, w_flat)

    if shards == 4:
        here, away, w_late, *prepared = lax.optimization_barrier((here, away, w_flat, *prepared))
    else:
        w_late, *prepared = lax.optimization_barrier((w_flat, *prepared))
    w_routes = []
    for r in range(shards):
        pairs = []
        for m, c, s in devices:
            q = (s - r) % shards
            pairs.append((dev(m, c, s), dev(m, q % 2, c * half + q // 2)))
        w_routes.append(pairs)

    if shards == 4:
        inner, edge = (1, 2), (0, 3)
        far = [(dev(m, c, s), dev(m, c, 1 if s == 3 else 2)) for m, c, s in devices if s in edge]
        near = [(dev(m, c, s), dev(m, c, 3 - s)) for m, c, s in devices if s in inner]
        outward = [(dev(m, c, s), dev(m, c, s ^ 1)) for m, c, s in devices if s in inner]
        pair_c = move(here, [(dev(m, c, s), dev(m, c, s ^ 1)) for m, c, s in devices])
        near_c, far_c = move(away, near), move(away, far)
        w_pieces = [move(x, route) for x, route in zip(prepared[:2], w_routes[:2])]
        near_c, far_c, pair_c, w_pieces[0], w_pieces[1], prepared[2], prepared[3] = lax.optimization_barrier(
            (near_c, far_c, pair_c, *w_pieces, *prepared[2:])
        )
        w_pieces += [move(x, route) for x, route in zip(prepared[2:], w_routes[2:])]
        cross = jnp.concatenate([near_c, far_c])
        cross = jnp.where(jnp.logical_or(shard == 1, shard == 2), cross, move(cross, outward))
        got = jnp.concatenate([here, pair_c])
        sources = [got, cross, move(got, swap_of(everyone)), move(cross, swap_of(everyone))]

        def pick(ids, refs, held, sems):
            s, core = ids[SHARD], ids[CORE]
            low = s < 2
            place = [s, s + 1 - 2 * lax.rem(s, 2), jnp.where(low, 2, 1), jnp.where(low, 3, 0)]
            for i, ref in enumerate(refs):
                turn = core if i < 2 else 1 - core
                for k in range(2):
                    at = 2 * place[2 * (i % 2) + k] + turn
                    to = pl.multiple_of(at * half_rows, half_rows)
                    pltpu.make_async_copy(
                        ref.at[pl.ds(k * half_rows, half_rows), :], held.at[pl.ds(to, half_rows), :], sems.at[at]
                    ).start()
    else:
        full = lax.all_gather(cotangent[0], "shard", axis=0, tiled=True)
        sources = [jnp.where(core == proc, full, move(full, swap_of(everyone)))]
        w_pieces = [move(x, route) for x, route in zip(prepared, w_routes)]

        def pick(ids, refs, held, sems):
            for i in range(2 * shards):
                span = pl.ds(i * half_rows, half_rows)
                pltpu.make_async_copy(refs[0].at[span, :], held.at[span, :], sems.at[i]).start()

    slices = pl.pallas_call(
        slice_kernel,
        grid=(steps,),
        out_shape=jax.ShapeDtypeStruct((particles, 2, rows, cols), BF),
        in_specs=[smem_spec(), w_spec],
        out_specs=pl.BlockSpec((particles, 2, rows // steps, cols), lambda i: (0, 0, i, 0)),
        compiler_params=params(8),
        name="slices",
    )(ids, w_late)
    whole = lax.all_to_all(slices, "particle", 0, 0, tiled=True)
    per = BLOCK // share
    halves = tok_rows // BLOCK
    act_t, slope_t, down_t, normed = pl.pallas_call(
        functools.partial(up_kernel, shards, width ** (-0.5)),
        grid=(blocks,),
        out_shape=[
            jax.ShapeDtypeStruct((part, tokens), BF),
            jax.ShapeDtypeStruct((part, tokens), BF),
            jax.ShapeDtypeStruct((part, width), BF),
            jax.ShapeDtypeStruct((tokens, width), BF),
        ],
        in_specs=[smem_spec(), pl.BlockSpec((per, 1, share, width), lambda i: (i % halves, i // halves, 0, 0))]
        + [pl.BlockSpec((2, rows, part), lambda i: (0, 0, 0))] * shards,
        out_specs=[
            pl.BlockSpec((part, BLOCK), lambda i: (0, i)),
            pl.BlockSpec((part, BLOCK), lambda i: (0, i)),
            pl.BlockSpec((part, width), lambda i: (0, 0)),
            pl.BlockSpec((BLOCK, width), lambda i: (i, 0)),
        ],
        scratch_shapes=[pltpu.VMEM((width, part), BF), pltpu.VMEM((width, part), BF), pltpu.VMEM((part, width), BF)],
        compiler_params=params(24),
        name="up",
    )(ids, normed, *w_pieces)

    grad_scale = 1.0 / (tokens * width)
    held = 2 * (2 * tokens * width + 3 * tokens * part + 3 * width * part)
    scores = pl.pallas_call(
        functools.partial(
            grad_kernel,
            shards,
            particles,
            -(width ** (-0.5)) * grad_scale,
            -(hidden ** (-0.5)) * grad_scale,
            hidden ** (-0.5),
            pick,
        ),
        out_shape=[jax.ShapeDtypeStruct((2, rows, cols), BF)] * particles,
        in_specs=[smem_spec()] + [any_spec()] * (4 + len(sources)),
        out_specs=[any_spec()] * particles,
        scratch_shapes=[
            pltpu.VMEM((tokens, width), BF),
            pltpu.VMEM((tokens, width), BF),
            pltpu.VMEM((part, tokens), BF),
            pltpu.VMEM((part, tokens), BF),
            pltpu.VMEM((part, tokens), BF),
            pltpu.VMEM((part, width), BF),
            pltpu.VMEM((2, width, part), BF),
            pltpu.SemaphoreType.DMA((2 * shards + 4,)),
        ],
        compiler_params=params(held // MIB + 8),
        name="grads",
    )(ids, normed, act_t, slope_t, down_t, *sources)

    whole, *scores = lax.optimization_barrier((whole, *scores))
    pair_list = [(i, j) for i in range(particles) for j in range(i)]
    partial = pl.pallas_call(
        distance_kernel,
        out_shape=jax.ShapeDtypeStruct((len(pair_list), 8, LANES), F32),
        in_specs=[pl.BlockSpec(memory_space=pltpu.VMEM)],
        out_specs=pl.BlockSpec(memory_space=pltpu.VMEM),
        compiler_params=params(8),
        name="distances",
    )(whole)
    sums = jnp.sum(partial, axis=(1, 2))
    sums = jnp.pad(sums, (0, -len(pair_list) % LANES))
    for axis, count in (("particle", particles), ("shard", shards)):
        copies = jnp.broadcast_to(sums[None, None], (count, 1, sums.shape[0]))
        sums = jnp.sum(lax.all_to_all(copies, axis, 0, 0, tiled=True), axis=(0, 1))
    lookup = [
        [pair_list.index((max(i, j), min(i, j))) if i != j else len(pair_list) for j in range(particles)]
        for i in range(particles)
    ]
    table = jnp.concatenate([sums[: len(pair_list)], jnp.zeros((1,), F32)])
    distances = table[jnp.array(lookup, jnp.int32)]
    inverse_band = 1.0 / kernel_scale[0].astype(F32)
    repulse = 2.0 * inverse_band
    kernel = jnp.exp(-distances * inverse_band)
    scale = 2 * width * hidden / particles
    coef = jnp.concatenate(
        [(scale * kernel).reshape(-1), scale * repulse * jnp.sum(kernel, axis=1), repulse[None]]
    )

    ratio = particles // shards
    arrived = []
    for t in range(particles):
        pairs = []
        for m, c, s in devices:
            mine, q = 2 * m + s // half, 2 * (s % half) + c
            u = (mine + ratio * q - t) % particles
            z, e = u // ratio, q * ratio + u % ratio
            pairs.append((dev(m, c, s), dev(e // 2 + z, e % 2, z)))
        arrived.append(move(scores[t], pairs))

    fields = pl.pallas_call(
        functools.partial(stein_kernel, shards, particles),
        out_shape=[jax.ShapeDtypeStruct((2, rows, cols), BF)] * particles,
        in_specs=[smem_spec(), smem_spec(), pl.BlockSpec(memory_space=pltpu.VMEM)] + [any_spec()] * particles,
        out_specs=[any_spec()] * particles,
        scratch_shapes=[
            pltpu.VMEM((particles, 2, rows, cols), BF),
            pltpu.VMEM((particles, 2, rows, cols), BF),
            pltpu.SemaphoreType.DMA((particles,)),
        ],
        compiler_params=params(12),
        name="stein",
    )(ids, coef, whole, *arrived)

    back = []
    for k in range(columns):
        for x in range(2):
            pairs = [(dev(m, c, s), dev(m + k, c ^ x, s)) for m, c, s in devices]
            back.append(move(fields[2 * k + x], pairs))

    steps = max(rows // 32, 1)
    flat_rows = rows * 2 * lane_tiles
    state_spec = pl.BlockSpec((flat_rows // steps, LANES), lambda i: (i, 0))
    outs = pl.pallas_call(
        functools.partial(adam_kernel, particles),
        grid=(steps,),
        out_shape=[jax.ShapeDtypeStruct((flat_rows, LANES), F32)] * 4,
        in_specs=[smem_spec()] + [state_spec] * 3 + [any_spec()] * particles,
        out_specs=[state_spec] * 4,
        scratch_shapes=[pltpu.VMEM((2, rows, hidden), BF), pltpu.SemaphoreType.DMA((particles,))],
        compiler_params=params(16),
        name="adam",
    )(ids, w_flat, flat(first_moment), flat(second_moment), *back)
    return tuple(unflat(x) for x in outs)


def solution(mesh):
    state = P("particle", "shard", None, None)
    return jax.shard_map(
        local,
        mesh=mesh,
        in_specs=(P("shard", None), P("shard"), P(), P("particle", "shard", None), state, state, state),
        out_specs=(state, state, state, state),
        check_vma=False,
    )
```

```python
import functools

import jax
import jax.numpy as jnp
from jax import lax
from jax.experimental import pallas as pl
from jax.experimental.pallas import tpu as pltpu
from jax.sharding import PartitionSpec as P

BF = jnp.bfloat16
F32 = jnp.float32
AXES = ("particle", "shard")
LANES = 128
BLOCK = 256
MIB = 1024 * 1024
NT = (((1,), (1,)), ((), ()))

COL, CORE, SHARD, PROC, PIECE = range(5)


def any_spec():
    return pl.BlockSpec(memory_space=pl.ANY)


def smem_spec():
    return pl.BlockSpec(memory_space=pltpu.SMEM)


def params(mib):
    return pltpu.CompilerParams(vmem_limit_bytes=mib * MIB)


def run_copies(copies):
    for copy in copies:
        copy.start()
    for copy in copies:
        copy.wait()


def slice_index(ids, column, core, shard, columns):
    return 2 * lax.rem(column - shard + columns * 16, columns) + core


def prep_kernel(shards, ids, w, *out):
    _, rows, piece = out[0].shape
    tiles = piece // LANES
    stride = 2 * shards * tiles
    for r in range(shards):
        first = lax.rem(ids[SHARD] - r + shards, shards) * tiles
        for kind in range(2):
            for j in range(tiles):
                part = w[pl.ds(2 * (first + j) + kind, rows, stride=stride), :]
                out[r][kind, :, j * LANES : (j + 1) * LANES] = part.astype(BF)
    particles, _, _, cols = out[shards].shape
    tiles = cols // LANES
    for p in range(particles):
        first = slice_index(ids, p // 2, p % 2, ids[SHARD], particles // 2) * tiles
        for kind in range(2):
            for j in range(tiles):
                part = w[pl.ds(2 * (first + j) + kind, rows, stride=stride), :]
                out[shards][p, kind, :, j * LANES : (j + 1) * LANES] = part.astype(BF)


def up_kernel(shards, scale, ids, tokens, *refs):
    pieces = refs[:shards]
    act_t, slope_t, down_t, normed, up_w, down_w, up_t = refs[shards:]
    width, part = up_w.shape
    rows = width // shards

    @pl.when(pl.program_id(0) == 0)
    def _():
        for r in range(shards):
            at = pl.multiple_of(lax.rem(ids[PIECE] + r, shards) * rows, rows)
            up_w[pl.ds(at, rows), :] = pieces[r][0]
            down_w[pl.ds(at, rows), :] = pieces[r][1]
        for i in range(width // LANES):
            span = slice(i * LANES, (i + 1) * LANES)
            up_t[:, span] = up_w[span, :].astype(F32).T.astype(BF)
            down_t[:, span] = down_w[span, :].astype(F32).T.astype(BF)

    block = tokens[...].reshape(normed.shape)
    normed[...] = block
    u = lax.dot_general(up_t[...], block, NT, preferred_element_type=F32) * scale
    cdf = 0.5 * (1.0 + lax.erf(u * 0.7071067811865476))
    density = jnp.exp(-0.5 * u * u) * 0.3989422804014327
    act_t[...] = (u * cdf).astype(BF)
    slope_t[...] = (cdf + u * density).astype(BF)


def grad_kernel(shards, particles, up_scale, down_scale, back_scale, pick, ids, normed, act_t, slope_t, down_t, *refs):
    n_in = len(refs) - particles - 8
    sources, out = refs[:n_in], refs[n_in : n_in + particles]
    c, n, act, slope, grad, down, score, sems = refs[n_in + particles :]
    part, tokens = act.shape
    width = c.shape[1]
    chunk = tokens // shards
    first = [
        pltpu.make_async_copy(down_t, down, sems.at[2 * shards]),
        pltpu.make_async_copy(slope_t, slope, sems.at[2 * shards + 1]),
    ]
    later = [
        pltpu.make_async_copy(act_t, act, sems.at[2 * shards + 2]),
        pltpu.make_async_copy(normed, n, sems.at[2 * shards + 3]),
    ]
    for copy in first:
        copy.start()
    pick(ids, sources, c, sems)
    for copy in later:
        copy.start()
    for copy in first:
        copy.wait()

    def back(i, carry):
        for turn in range(2):
            here = c.at[pl.ds(0, chunk // 2), :]
            pltpu.make_async_copy(here, here, sems.at[2 * i + turn]).wait()
        at = pl.multiple_of(i * chunk, chunk)
        b = lax.dot_general(down[...], c[pl.ds(at, chunk), :], NT, preferred_element_type=F32)
        grad[:, pl.ds(at, chunk)] = (b * (slope[:, pl.ds(at, chunk)].astype(F32) * back_scale)).astype(BF)
        return carry

    lax.fori_loop(0, shards, back, 0)
    for copy in later:
        copy.wait()

    def gradient(j, carry):
        at = pl.multiple_of(j * BLOCK, BLOCK)
        g = jnp.dot(grad[...], n[:, pl.ds(at, BLOCK)], preferred_element_type=F32)
        score[0, pl.ds(at, BLOCK), :] = (g * up_scale).T.astype(BF)
        g = jnp.dot(act[...], c[:, pl.ds(at, BLOCK)], preferred_element_type=F32)
        score[1, pl.ds(at, BLOCK), :] = (g * down_scale).T.astype(BF)
        return carry

    lax.fori_loop(0, width // BLOCK, gradient, 0)
    rows = width // shards
    ratio = particles // shards
    cols = part // ratio
    mine = 2 * ids[COL] + ids[PROC]
    copies = []
    for t in range(particles):
        u = lax.rem(mine + ratio * ids[PIECE] - t + particles, particles)
        row = pl.multiple_of(lax.div(u, ratio) * rows, rows)
        col = pl.multiple_of(lax.rem(u, ratio) * cols, cols)
        copies.append(pltpu.make_async_copy(score.at[:, pl.ds(row, rows), pl.ds(col, cols)], out[t], sems.at[t]))
    run_copies(copies)


def distance_kernel(whole, out):
    particles, _, rows, cols = whole.shape
    pairs = [(i, j) for i in range(particles) for j in range(i)]
    tiles = cols // LANES

    def body(g, acc):
        kind = lax.div(g, rows // 16)
        row = pl.multiple_of(lax.rem(g, rows // 16) * 16, 16)
        for tile in range(tiles):
            w = [whole[p, kind, pl.ds(row, 16), tile * LANES : (tile + 1) * LANES].astype(F32) for p in range(particles)]
            new = []
            for a, (i, j) in zip(acc, pairs):
                d = w[i] - w[j]
                d = d * d
                new.append(a + (d[:8] + d[8:]))
            acc = tuple(new)
        return acc

    acc = lax.fori_loop(0, 2 * rows // 16, body, tuple(jnp.zeros((8, LANES), F32) for _ in pairs))
    for i, a in enumerate(acc):
        out[i] = a


def stein_kernel(shards, particles, ids, coef, whole, *refs):
    sources, out = refs[:particles], refs[particles : 2 * particles]
    scores, field, sems = refs[2 * particles :]
    columns = particles // 2
    ratio = particles // shards
    _, _, rows, cols = whole.shape
    e = slice_index(ids, ids[COL], ids[CORE], ids[SHARD], columns)
    u = ids[SHARD] * ratio + lax.rem(e, ratio) + particles * shards - ratio * lax.div(e, ratio)
    run_copies(
        [pltpu.make_async_copy(sources[t], scores.at[lax.rem(u + t, particles)], sems.at[t]) for t in range(particles)]
    )
    repulse = coef[particles * particles + particles]
    groups = rows // 16
    tiles = cols // LANES

    def body(g, carry):
        kind = lax.div(g, groups)
        row = pl.multiple_of(lax.rem(g, groups) * 16, 16)
        for tile in range(tiles):
            at = (kind, pl.ds(row, 16), slice(tile * LANES, (tile + 1) * LANES))
            w = [whole[(p,) + at].astype(F32) for p in range(particles)]
            pushed = [scores[(p,) + at].astype(F32) - repulse * w[p] for p in range(particles)]
            for i in range(particles):
                total = coef[particles * particles + i] * w[i]
                for j in range(particles):
                    total = total + coef[i * particles + j] * pushed[j]
                field[(i,) + at] = total.astype(BF)
        return carry

    lax.fori_loop(0, 2 * groups, body, 0)
    copies = []
    for k in range(columns):
        for x in range(2):
            column = lax.rem(ids[COL] + k, columns)
            core = ids[CORE] if x == 0 else 1 - ids[CORE]
            i = 2 * k + x
            copies.append(pltpu.make_async_copy(field.at[2 * column + core], out[i], sems.at[i]))
    run_copies(copies)


def adam_kernel(particles, ids, w, first, second, *refs):
    sources = refs[:particles]
    new_w, new_first, new_second, transport, field, sems = refs[particles:]
    columns = particles // 2
    _, _, hidden = field.shape
    width = hidden // particles
    step = pl.program_id(0)

    @pl.when(step == 0)
    def _():
        copies = []
        for k in range(columns):
            for x in range(2):
                column = lax.rem(ids[COL] - k + columns, columns)
                core = ids[CORE] if x == 0 else 1 - ids[CORE]
                at = pl.multiple_of(slice_index(ids, column, core, ids[SHARD], columns) * width, width)
                i = 2 * k + x
                copies.append(pltpu.make_async_copy(sources[i], field.at[:, :, pl.ds(at, width)], sems.at[i]))
        run_copies(copies)

    lane_tiles = hidden // LANES
    rows = w.shape[0] // (2 * lane_tiles)
    base = pl.multiple_of(step * rows, rows)
    for kind in range(2):
        for tile in range(lane_tiles):
            part = field[kind, pl.ds(base, rows), tile * LANES : (tile + 1) * LANES]
            transport[pl.ds(2 * tile + kind, rows, stride=2 * lane_tiles), :] = part.astype(F32)
    t = transport[...]
    m = 0.9 * first[...] - 0.1 * t
    v = 0.999 * second[...] + 0.001 * t * t
    new_first[...] = m
    new_second[...] = v
    new_w[...] = w[...] - 0.01 * m / (jnp.sqrt(v) + 1e-08)


def local(pool, batch_index, kernel_scale, cotangent, weights, first_moment, second_moment):
    shards = lax.axis_size("shard")
    particles = lax.axis_size("particle")
    columns, half = particles // 2, shards // 2
    tok_rows = batch_index.shape[0]
    width = pool.shape[1]
    _, rows, _, hidden = weights.shape
    part, cols = hidden // shards, hidden // particles
    tokens = tok_rows * shards
    blocks = tokens // BLOCK
    lane_tiles = hidden // LANES

    own = lax.axis_index("particle")
    shard = lax.axis_index("shard")
    core, column = own % 2, own // 2
    proc = shard // half
    piece = 2 * (shard % half) + core
    ids = jnp.stack([column, core, shard, proc, piece]).astype(jnp.int32)
    devices = [(m, c, s) for m in range(columns) for c in range(2) for s in range(shards)]

    def dev(m, c, s):
        return (2 * (m % columns) + c) * shards + s

    def move(x, pairs):
        if all(a == b for a, b in pairs) and len(pairs) == len(devices):
            return x
        return lax.ppermute(x, AXES, pairs)

    def swap_of(among):
        return [(dev(m, c, s), dev(m, 1 - c, s)) for m, c, s in devices if s in among]

    def flat(x):
        return x[0].reshape(rows, 2, lane_tiles, LANES).transpose(0, 2, 1, 3).reshape(-1, LANES)

    def unflat(x):
        return x.reshape(rows, lane_tiles, 2, LANES).transpose(0, 2, 1, 3).reshape(1, rows, 2, hidden)

    everyone = range(shards)
    half_rows = tok_rows // 2
    if shards == 4:
        mine = lax.dynamic_slice(cotangent[0], (core * half_rows, 0), (half_rows, width))
        give = lax.dynamic_slice(cotangent[0], ((1 - core) * half_rows, 0), (half_rows, width))
        other = move(give, swap_of(everyone))
        is_own = core == proc
        here = jnp.where(is_own, mine, other)
        away = jnp.where(is_own, other, mine)

    share = tok_rows // particles
    index = lax.dynamic_slice(batch_index, (own * share,), (share,))
    picked = jnp.take(pool, index, axis=0).astype(F32)
    normed = (picked * lax.rsqrt(jnp.mean(picked * picked, axis=1, keepdims=True) + 1e-06)).astype(BF)
    normed = jnp.stack(
        [move(normed, [(dev(m, c, s), dev(m, c, (s + k) % shards)) for m, c, s in devices]) for k in range(shards)]
    )
    normed = lax.all_gather(normed[None], "particle", axis=0, tiled=True)

    w_flat = flat(weights)
    steps = max(rows // 64, 1)
    lines = w_flat.shape[0] // steps
    *prepared, slices = pl.pallas_call(
        functools.partial(prep_kernel, shards),
        grid=(steps,),
        out_shape=[jax.ShapeDtypeStruct((2, rows, part), BF)] * shards
        + [jax.ShapeDtypeStruct((particles, 2, rows, cols), BF)],
        in_specs=[smem_spec(), pl.BlockSpec((lines, LANES), lambda i: (i, 0))],
        out_specs=[pl.BlockSpec((2, rows // steps, part), lambda i: (0, i, 0))] * shards
        + [pl.BlockSpec((particles, 2, rows // steps, cols), lambda i: (0, 0, i, 0))],
        compiler_params=params(56),
        name="prep",
    )(ids, w_flat)

    w_routes = []
    for r in range(shards):
        pairs = []
        for m, c, s in devices:
            q = (s - r) % shards
            pairs.append((dev(m, c, s), dev(m, q % 2, c * half + q // 2)))
        w_routes.append(pairs)

    if shards == 4:
        here, away, slices, *prepared = lax.optimization_barrier((here, away, slices, *prepared))
    whole = lax.all_to_all(slices, "particle", 0, 0, tiled=True)
    pair_list = [(i, j) for i in range(particles) for j in range(i)]
    partial = pl.pallas_call(
        distance_kernel,
        out_shape=jax.ShapeDtypeStruct((len(pair_list), 8, LANES), F32),
        in_specs=[pl.BlockSpec(memory_space=pltpu.VMEM)],
        out_specs=pl.BlockSpec(memory_space=pltpu.VMEM),
        compiler_params=params(8),
        name="distances",
    )(whole)
    sums = jnp.sum(partial, axis=(1, 2))
    sums = jnp.pad(sums, (0, -len(pair_list) % LANES))
    for axis, count in (("particle", particles), ("shard", shards)):
        copies = jnp.broadcast_to(sums[None, None], (count, 1, sums.shape[0]))
        sums = jnp.sum(lax.all_to_all(copies, axis, 0, 0, tiled=True), axis=(0, 1))
    if shards == 4:
        inner, edge = (1, 2), (0, 3)
        far = [(dev(m, c, s), dev(m, c, 1 if s == 3 else 2)) for m, c, s in devices if s in edge]
        near = [(dev(m, c, s), dev(m, c, 3 - s)) for m, c, s in devices if s in inner]
        outward = [(dev(m, c, s), dev(m, c, s ^ 1)) for m, c, s in devices if s in inner]
        pair = [(dev(m, c, s), dev(m, c, s ^ 1)) for m, c, s in devices]
        got = [move(away, near), move(away, far), move(here, pair)]
        w_pieces = [move(x, route) for x, route in zip(prepared[:2], w_routes[:2])]
        got, w_pieces, last, sums, normed = lax.optimization_barrier((got, w_pieces, prepared[2:], sums, normed))
        near_c, far_c, pair_c = got
        near_o, far_o = move(near_c, outward), move(far_c, outward)
        w_pieces = w_pieces + [move(x, route) for x, route in zip(last, w_routes[2:])]
        is_inner = jnp.logical_or(shard == 1, shard == 2)
        got = [here, pair_c, jnp.where(is_inner, near_c, near_o), jnp.where(is_inner, far_c, far_o)]
        got, w_pieces = lax.optimization_barrier((got, w_pieces))
        sources = got + [move(x, swap_of(everyone)) for x in got]

        def pick(ids, refs, held, sems):
            s, core = ids[SHARD], ids[CORE]
            low = s < 2
            place = [s, s + 1 - 2 * lax.rem(s, 2), jnp.where(low, 2, 1), jnp.where(low, 3, 0)]
            for i, ref in enumerate(refs):
                at = 2 * place[i % 4] + (core if i < 4 else 1 - core)
                to = pl.multiple_of(at * half_rows, half_rows)
                pltpu.make_async_copy(ref, held.at[pl.ds(to, half_rows), :], sems.at[at]).start()
    else:
        full = lax.all_gather(cotangent[0], "shard", axis=0, tiled=True)
        sources = [jnp.where(core == proc, full, move(full, swap_of(everyone)))]
        w_pieces = [move(x, route) for x, route in zip(prepared, w_routes)]

        def pick(ids, refs, held, sems):
            for i in range(2 * shards):
                span = pl.ds(i * half_rows, half_rows)
                pltpu.make_async_copy(refs[0].at[span, :], held.at[span, :], sems.at[i]).start()

    lookup = [
        [pair_list.index((max(i, j), min(i, j))) if i != j else len(pair_list) for j in range(particles)]
        for i in range(particles)
    ]
    table = jnp.concatenate([sums[: len(pair_list)], jnp.zeros((1,), F32)])
    distances = table[jnp.array(lookup, jnp.int32)]
    inverse_band = 1.0 / kernel_scale[0].astype(F32)
    repulse = 2.0 * inverse_band
    kernel = jnp.exp(-distances * inverse_band)
    scale = 2 * width * hidden / particles
    coef = jnp.concatenate(
        [(scale * kernel).reshape(-1), scale * repulse * jnp.sum(kernel, axis=1), repulse[None]]
    )

    per = BLOCK // share
    halves = tok_rows // BLOCK
    act_t, slope_t, down_t, normed = pl.pallas_call(
        functools.partial(up_kernel, shards, width ** (-0.5)),
        grid_spec=pltpu.PrefetchScalarGridSpec(
            num_scalar_prefetch=1,
            grid=(blocks,),
            in_specs=[
                pl.BlockSpec(
                    (per, 1, share, width),
                    lambda i, ids: (i % halves, lax.rem(ids[SHARD] - i // halves + shards, shards), 0, 0),
                )
            ]
            + [pl.BlockSpec((2, rows, part), lambda i, ids: (0, 0, 0))] * shards,
            out_specs=[
                pl.BlockSpec((part, BLOCK), lambda i, ids: (0, i)),
                pl.BlockSpec((part, BLOCK), lambda i, ids: (0, i)),
                pl.BlockSpec((part, width), lambda i, ids: (0, 0)),
                pl.BlockSpec((BLOCK, width), lambda i, ids: (i, 0)),
            ],
            scratch_shapes=[
                pltpu.VMEM((width, part), BF),
                pltpu.VMEM((width, part), BF),
                pltpu.VMEM((part, width), BF),
            ],
        ),
        out_shape=[
            jax.ShapeDtypeStruct((part, tokens), BF),
            jax.ShapeDtypeStruct((part, tokens), BF),
            jax.ShapeDtypeStruct((part, width), BF),
            jax.ShapeDtypeStruct((tokens, width), BF),
        ],
        compiler_params=params(56),
        name="up",
    )(ids, normed, *w_pieces)

    grad_scale = 1.0 / (tokens * width)
    scores = pl.pallas_call(
        functools.partial(
            grad_kernel,
            shards,
            particles,
            -(width ** (-0.5)) * grad_scale,
            -(hidden ** (-0.5)) * grad_scale,
            hidden ** (-0.5),
            pick,
        ),
        out_shape=[jax.ShapeDtypeStruct((2, rows, cols), BF)] * particles,
        in_specs=[smem_spec()] + [any_spec()] * (4 + len(sources)),
        out_specs=[any_spec()] * particles,
        scratch_shapes=[
            pltpu.VMEM((tokens, width), BF),
            pltpu.VMEM((tokens, width), BF),
            pltpu.VMEM((part, tokens), BF),
            pltpu.VMEM((part, tokens), BF),
            pltpu.VMEM((part, tokens), BF),
            pltpu.VMEM((part, width), BF),
            pltpu.VMEM((2, width, part), BF),
            pltpu.SemaphoreType.DMA((2 * shards + 4,)),
        ],
        compiler_params=params(56),
        name="grads",
    )(ids, normed, act_t, slope_t, down_t, *sources)

    ratio = particles // shards
    arrived = []
    for t in range(particles):
        pairs = []
        for m, c, s in devices:
            mine, q = 2 * m + s // half, 2 * (s % half) + c
            u = (mine + ratio * q - t) % particles
            z, e = u // ratio, q * ratio + u % ratio
            pairs.append((dev(m, c, s), dev(e // 2 + z, e % 2, z)))
        arrived.append(move(scores[t], pairs))

    fields = pl.pallas_call(
        functools.partial(stein_kernel, shards, particles),
        out_shape=[jax.ShapeDtypeStruct((2, rows, cols), BF)] * particles,
        in_specs=[smem_spec(), smem_spec(), pl.BlockSpec(memory_space=pltpu.VMEM)] + [any_spec()] * particles,
        out_specs=[any_spec()] * particles,
        scratch_shapes=[
            pltpu.VMEM((particles, 2, rows, cols), BF),
            pltpu.VMEM((particles, 2, rows, cols), BF),
            pltpu.SemaphoreType.DMA((particles,)),
        ],
        compiler_params=params(12),
        name="stein",
    )(ids, coef, whole, *arrived)

    back = []
    for k in range(columns):
        for x in range(2):
            pairs = [(dev(m, c, s), dev(m + k, c ^ x, s)) for m, c, s in devices]
            back.append(move(fields[2 * k + x], pairs))

    steps = max(rows // 32, 1)
    flat_rows = rows * 2 * lane_tiles
    state_spec = pl.BlockSpec((flat_rows // steps, LANES), lambda i: (i, 0))
    outs = pl.pallas_call(
        functools.partial(adam_kernel, particles),
        grid=(steps,),
        out_shape=[jax.ShapeDtypeStruct((flat_rows, LANES), F32)] * 4,
        in_specs=[smem_spec()] + [state_spec] * 3 + [any_spec()] * particles,
        out_specs=[state_spec] * 4,
        scratch_shapes=[pltpu.VMEM((2, rows, hidden), BF), pltpu.SemaphoreType.DMA((particles,))],
        compiler_params=params(56),
        name="adam",
    )(ids, w_flat, flat(first_moment), flat(second_moment), *back)
    return tuple(unflat(x) for x in outs)


def solution(mesh):
    state = P("particle", "shard", None, None)
    return jax.shard_map(
        local,
        mesh=mesh,
        in_specs=(P("shard", None), P("shard"), P(), P("particle", "shard", None), state, state, state),
        out_specs=(state, state, state, state),
        check_vma=False,
    )
```

```python
import functools

import jax
import jax.numpy as jnp
from jax import lax
from jax.experimental import pallas as pl
from jax.experimental.pallas import tpu as pltpu
from jax.sharding import PartitionSpec as P

BF = jnp.bfloat16
F32 = jnp.float32
AXES = ("particle", "shard")
LANES = 128
BLOCK = 256
MIB = 1024 * 1024
NT = (((1,), (1,)), ((), ()))

COL, CORE, SHARD, PROC, PIECE = range(5)


def any_spec():
    return pl.BlockSpec(memory_space=pl.ANY)


def smem_spec():
    return pl.BlockSpec(memory_space=pltpu.SMEM)


def params(mib):
    return pltpu.CompilerParams(vmem_limit_bytes=mib * MIB)


def run_copies(copies):
    for copy in copies:
        copy.start()
    for copy in copies:
        copy.wait()


def slice_index(ids, column, core, shard, columns):
    return 2 * lax.rem(column - shard + columns * 16, columns) + core


def prep_kernel(shards, ids, w, *out):
    _, rows, piece = out[0].shape
    tiles = piece // LANES
    stride = 2 * shards * tiles
    for r in range(shards):
        first = lax.rem(ids[SHARD] - r + shards, shards) * tiles
        for kind in range(2):
            for j in range(tiles):
                part = w[pl.ds(2 * (first + j) + kind, rows, stride=stride), :]
                out[r][kind, :, j * LANES : (j + 1) * LANES] = part.astype(BF)
    particles, _, _, cols = out[shards].shape
    tiles = cols // LANES
    for p in range(particles):
        first = slice_index(ids, p // 2, p % 2, ids[SHARD], particles // 2) * tiles
        for kind in range(2):
            for j in range(tiles):
                part = w[pl.ds(2 * (first + j) + kind, rows, stride=stride), :]
                out[shards][p, kind, :, j * LANES : (j + 1) * LANES] = part.astype(BF)


def up_kernel(shards, scale, ids, tokens, *refs):
    pieces = refs[:shards]
    act_t, slope_t, down_t, up_w, down_w, up_t = refs[shards:]
    width, part = up_w.shape
    rows = width // shards

    @pl.when(pl.program_id(0) == 0)
    def _():
        for r in range(shards):
            at = pl.multiple_of(lax.rem(ids[PIECE] + r, shards) * rows, rows)
            up_w[pl.ds(at, rows), :] = pieces[r][0]
            down_w[pl.ds(at, rows), :] = pieces[r][1]
        for i in range(width // LANES):
            span = slice(i * LANES, (i + 1) * LANES)
            up_t[:, span] = up_w[span, :].astype(F32).T.astype(BF)
            down_t[:, span] = down_w[span, :].astype(F32).T.astype(BF)

    u = lax.dot_general(up_t[...], tokens[...], NT, preferred_element_type=F32) * scale
    cdf = 0.5 * (1.0 + lax.erf(u * 0.7071067811865476))
    density = jnp.exp(-0.5 * u * u) * 0.3989422804014327
    act_t[...] = (u * cdf).astype(BF)
    slope_t[...] = (cdf + u * density).astype(BF)


def grad_kernel(shards, particles, up_scale, down_scale, back_scale, pick, ids, normed, act_t, slope_t, down_t, *refs):
    n_in = len(refs) - particles - 8
    sources, out = refs[:n_in], refs[n_in : n_in + particles]
    c, n, act, slope, grad, down, score, sems = refs[n_in + particles :]
    part, tokens = act.shape
    width = c.shape[1]
    chunk = tokens // shards
    first = [
        pltpu.make_async_copy(down_t, down, sems.at[1]),
        pltpu.make_async_copy(slope_t, slope, sems.at[2]),
    ]
    later = [
        pltpu.make_async_copy(act_t, act, sems.at[3]),
        pltpu.make_async_copy(normed, n, sems.at[4]),
    ]
    for copy in first:
        copy.start()
    pick(ids, sources, c, sems.at[0])
    for copy in later:
        copy.start()
    for copy in first:
        copy.wait()
    pltpu.make_async_copy(c, c, sems.at[0]).wait()

    def back(i, carry):
        at = pl.multiple_of(i * chunk, chunk)
        b = lax.dot_general(down[...], c[pl.ds(at, chunk), :], NT, preferred_element_type=F32)
        grad[:, pl.ds(at, chunk)] = (b * (slope[:, pl.ds(at, chunk)].astype(F32) * back_scale)).astype(BF)
        return carry

    lax.fori_loop(0, shards, back, 0)
    for copy in later:
        copy.wait()

    def gradient(j, carry):
        at = pl.multiple_of(j * BLOCK, BLOCK)
        g = jnp.dot(grad[...], n[:, pl.ds(at, BLOCK)], preferred_element_type=F32)
        score[0, pl.ds(at, BLOCK), :] = (g * up_scale).T.astype(BF)
        g = jnp.dot(act[...], c[:, pl.ds(at, BLOCK)], preferred_element_type=F32)
        score[1, pl.ds(at, BLOCK), :] = (g * down_scale).T.astype(BF)
        return carry

    lax.fori_loop(0, width // BLOCK, gradient, 0)
    rows = width // shards
    ratio = particles // shards
    cols = part // ratio
    mine = 2 * ids[COL] + ids[PROC]
    copies = []
    for t in range(particles):
        u = lax.rem(mine + ratio * ids[PIECE] - t + particles, particles)
        row = pl.multiple_of(lax.div(u, ratio) * rows, rows)
        col = pl.multiple_of(lax.rem(u, ratio) * cols, cols)
        copies.append(pltpu.make_async_copy(score.at[:, pl.ds(row, rows), pl.ds(col, cols)], out[t], sems.at[t]))
    run_copies(copies)


def distance_kernel(whole, out):
    particles, _, rows, cols = whole.shape
    pairs = [(i, j) for i in range(particles) for j in range(i)]
    tiles = cols // LANES

    def body(g, acc):
        kind = lax.div(g, rows // 16)
        row = pl.multiple_of(lax.rem(g, rows // 16) * 16, 16)
        for tile in range(tiles):
            w = [whole[p, kind, pl.ds(row, 16), tile * LANES : (tile + 1) * LANES].astype(F32) for p in range(particles)]
            new = []
            for a, (i, j) in zip(acc, pairs):
                d = w[i] - w[j]
                d = d * d
                new.append(a + (d[:8] + d[8:]))
            acc = tuple(new)
        return acc

    acc = lax.fori_loop(0, 2 * rows // 16, body, tuple(jnp.zeros((8, LANES), F32) for _ in pairs))
    for i, a in enumerate(acc):
        out[i] = a


def stein_kernel(shards, particles, ids, coef, whole, *refs):
    sources, out = refs[:particles], refs[particles : 2 * particles]
    scores, field, sems = refs[2 * particles :]
    columns = particles // 2
    ratio = particles // shards
    _, _, rows, cols = whole.shape
    e = slice_index(ids, ids[COL], ids[CORE], ids[SHARD], columns)
    u = ids[SHARD] * ratio + lax.rem(e, ratio) + particles * shards - ratio * lax.div(e, ratio)
    run_copies(
        [pltpu.make_async_copy(sources[t], scores.at[lax.rem(u + t, particles)], sems.at[t]) for t in range(particles)]
    )
    repulse = coef[particles * particles + particles]
    groups = rows // 16
    tiles = cols // LANES

    def body(g, carry):
        kind = lax.div(g, groups)
        row = pl.multiple_of(lax.rem(g, groups) * 16, 16)
        for tile in range(tiles):
            at = (kind, pl.ds(row, 16), slice(tile * LANES, (tile + 1) * LANES))
            w = [whole[(p,) + at].astype(F32) for p in range(particles)]
            pushed = [scores[(p,) + at].astype(F32) - repulse * w[p] for p in range(particles)]
            for i in range(particles):
                total = coef[particles * particles + i] * w[i]
                for j in range(particles):
                    total = total + coef[i * particles + j] * pushed[j]
                field[(i,) + at] = total.astype(BF)
        return carry

    lax.fori_loop(0, 2 * groups, body, 0)
    copies = []
    for k in range(columns):
        for x in range(2):
            column = lax.rem(ids[COL] + k, columns)
            core = ids[CORE] if x == 0 else 1 - ids[CORE]
            i = 2 * k + x
            copies.append(pltpu.make_async_copy(field.at[2 * column + core], out[i], sems.at[i]))
    run_copies(copies)


def adam_kernel(particles, ids, w, first, second, *refs):
    sources = refs[:particles]
    new_w, new_first, new_second, transport, field, sems = refs[particles:]
    columns = particles // 2
    _, _, hidden = field.shape
    width = hidden // particles
    step = pl.program_id(0)

    @pl.when(step == 0)
    def _():
        copies = []
        for k in range(columns):
            for x in range(2):
                column = lax.rem(ids[COL] - k + columns, columns)
                core = ids[CORE] if x == 0 else 1 - ids[CORE]
                at = pl.multiple_of(slice_index(ids, column, core, ids[SHARD], columns) * width, width)
                i = 2 * k + x
                copies.append(pltpu.make_async_copy(sources[i], field.at[:, :, pl.ds(at, width)], sems.at[i]))
        run_copies(copies)

    lane_tiles = hidden // LANES
    rows = w.shape[0] // (2 * lane_tiles)
    base = pl.multiple_of(step * rows, rows)
    for kind in range(2):
        for tile in range(lane_tiles):
            part = field[kind, pl.ds(base, rows), tile * LANES : (tile + 1) * LANES]
            transport[pl.ds(2 * tile + kind, rows, stride=2 * lane_tiles), :] = part.astype(F32)
    t = transport[...]
    m = 0.9 * first[...] - 0.1 * t
    v = 0.999 * second[...] + 0.001 * t * t
    new_first[...] = m
    new_second[...] = v
    new_w[...] = w[...] - 0.01 * m / (jnp.sqrt(v) + 1e-08)


def local(pool, batch_index, kernel_scale, cotangent, weights, first_moment, second_moment):
    shards = lax.axis_size("shard")
    particles = lax.axis_size("particle")
    columns, half = particles // 2, shards // 2
    tok_rows = batch_index.shape[0]
    width = pool.shape[1]
    _, rows, _, hidden = weights.shape
    part, cols = hidden // shards, hidden // particles
    tokens = tok_rows * shards
    blocks = tokens // BLOCK
    lane_tiles = hidden // LANES

    own = lax.axis_index("particle")
    shard = lax.axis_index("shard")
    core, column = own % 2, own // 2
    proc = shard // half
    piece = 2 * (shard % half) + core
    ids = jnp.stack([column, core, shard, proc, piece]).astype(jnp.int32)
    devices = [(m, c, s) for m in range(columns) for c in range(2) for s in range(shards)]

    def dev(m, c, s):
        return (2 * (m % columns) + c) * shards + s

    def move(x, pairs):
        if all(a == b for a, b in pairs) and len(pairs) == len(devices):
            return x
        return lax.ppermute(x, AXES, pairs)

    def swap_of(among):
        return [(dev(m, c, s), dev(m, 1 - c, s)) for m, c, s in devices if s in among]

    def flat(x):
        return x[0].reshape(rows, 2, lane_tiles, LANES).transpose(0, 2, 1, 3).reshape(-1, LANES)

    def unflat(x):
        return x.reshape(rows, lane_tiles, 2, LANES).transpose(0, 2, 1, 3).reshape(1, rows, 2, hidden)

    everyone = range(shards)
    half_rows = tok_rows // 2
    share = tok_rows // particles
    index = lax.dynamic_slice(batch_index, (own * share,), (share,))
    picked = jnp.take(pool, index, axis=0).astype(F32)
    normed = (picked * lax.rsqrt(jnp.mean(picked * picked, axis=1, keepdims=True) + 1e-06)).astype(BF)
    normed = jnp.stack(
        [move(normed, [(dev(m, c, s), dev(m, c, (s + k) % shards)) for m, c, s in devices]) for k in range(shards)]
    )
    normed = lax.all_gather(normed[None], "particle", axis=0, tiled=True).reshape(tokens, width)

    w_flat = flat(weights)
    steps = max(rows // 64, 1)
    lines = w_flat.shape[0] // steps
    *prepared, slices = pl.pallas_call(
        functools.partial(prep_kernel, shards),
        grid=(steps,),
        out_shape=[jax.ShapeDtypeStruct((2, rows, part), BF)] * shards
        + [jax.ShapeDtypeStruct((particles, 2, rows, cols), BF)],
        in_specs=[smem_spec(), pl.BlockSpec((lines, LANES), lambda i: (i, 0))],
        out_specs=[pl.BlockSpec((2, rows // steps, part), lambda i: (0, i, 0))] * shards
        + [pl.BlockSpec((particles, 2, rows // steps, cols), lambda i: (0, 0, i, 0))],
        compiler_params=params(56),
        name="prep",
    )(ids, w_flat)

    w_routes = []
    for r in range(shards):
        pairs = []
        for m, c, s in devices:
            q = (s - r) % shards
            pairs.append((dev(m, c, s), dev(m, q % 2, c * half + q // 2)))
        w_routes.append(pairs)

    whole = lax.all_to_all(slices, "particle", 0, 0, tiled=True)

    def gather_row(ids, which, turn):
        k = lax.rem(ids[SHARD] - which + shards, shards)
        return (turn * (particles // 2) * shards + k) * share

    def place(ids, ref, held, sem, which, turn, start=0):
        row = gather_row(ids, which, turn)
        for i in range(particles // 2):
            to = pl.multiple_of(row + i * shards * share, share)
            pltpu.make_async_copy(
                ref.at[pl.ds(start + i * share, share), :], held.at[pl.ds(to, share), :], sem
            ).start()

    if shards == 4:
        cot = cotangent[0]
        inner = jnp.logical_or(shard == 1, shard == 2)
        flip = jnp.where(jnp.logical_or(inner, core == proc), 0, 1)
        first_routes, second_routes = [], []
        for e in range(2):
            one, two = [], []
            for m, c, s in devices:
                at_home, is_inner = c == s // half, s in (1, 2)
                if not at_home:
                    to, turn = (3 - s, e) if is_inner else (1 if s == 3 else 2, 1 - e)
                    one.append((dev(m, c, s), dev(m, c ^ turn, to)))
                elif is_inner:
                    one.append((dev(m, c, s), dev(m, c ^ e, s ^ 1)))
                else:
                    two.append((dev(m, c, s), dev(m, c ^ e, s ^ 1)))
                if is_inner:
                    two.append((dev(m, c, s), dev(m, c, s ^ 1)))
            first_routes.append(one)
            second_routes.append(two)
        halves = [
            lax.dynamic_slice(cot, (((core + e + flip) % 2) * half_rows, 0), (half_rows, width)) for e in range(2)
        ]
        alpha = [move(x, route) for x, route in zip(halves, first_routes)]
        own_c = move(cot, [(dev(m, c, s), dev(m, 1 - c, s)) for m, c, s in devices if c == s // half])
        w_pieces = [move(x, route) for x, route in zip(prepared[:2], w_routes[:2])]
        alpha, own_c, w_pieces, last = lax.optimization_barrier((alpha, own_c, w_pieces, prepared[2:]))
        beta = [move(jnp.where(inner, a, x), route) for a, x, route in zip(alpha, halves, second_routes)]
        w_pieces = w_pieces + [move(x, route) for x, route in zip(last, w_routes[2:])]
        alpha_x = [move(x, swap_of(everyone)) for x in alpha]
        beta, alpha_x, w_pieces, whole = lax.optimization_barrier((beta, alpha_x, w_pieces, whole))
        beta_x = [move(x, swap_of(everyone)) for x in beta]
        sources = [cot, own_c, *alpha, *alpha_x, *beta, *beta_x]

        def pick(ids, refs, held, sem):
            s, core, proc = ids[SHARD], ids[CORE], ids[PROC]
            low = s < 2
            near, far, pair = jnp.where(low, 2, 1), jnp.where(low, 3, 0), s + 1 - 2 * lax.rem(s, 2)
            side = lax.rem(core + proc, 2)
            is_inner = jnp.logical_or(s == 1, s == 2)

            def own(ref):
                for turn in range(2):
                    place(ids, ref, held, sem, s, turn, turn * half_rows)

            def others(main, main_x, rest, rest_x):
                for e in range(2):
                    same = side == e
                    place(ids, main[e], held, sem, jnp.where(same, near, far), core)
                    place(ids, main_x[e], held, sem, jnp.where(same, far, near), 1 - core)

                    @pl.when(same)
                    def _():
                        place(ids, rest[e], held, sem, pair, core)
                        place(ids, rest_x[1 - e], held, sem, pair, 1 - core)

            @pl.when(side == 0)
            def _():
                own(refs[0])

            @pl.when(side == 1)
            def _():
                own(refs[1])

            @pl.when(is_inner)
            def _():
                others(refs[2:4], refs[4:6], refs[6:8], refs[8:10])

            @pl.when(jnp.logical_not(is_inner))
            def _():
                others(refs[6:8], refs[8:10], refs[2:4], refs[4:6])
    else:
        full = lax.all_gather(cotangent[0], "shard", axis=0, tiled=True)
        sources = [jnp.where(core == proc, full, move(full, swap_of(everyone)))]
        w_pieces = [move(x, route) for x, route in zip(prepared, w_routes)]

        def pick(ids, refs, held, sem):
            def one(which, carry):
                for turn in range(2):
                    start = pl.multiple_of(which * tok_rows + turn * half_rows, half_rows)
                    place(ids, refs[0], held, sem, which, turn, start)
                return carry

            lax.fori_loop(0, shards, one, 0)

    act_t, slope_t, down_t = pl.pallas_call(
        functools.partial(up_kernel, shards, width ** (-0.5)),
        grid=(blocks,),
        out_shape=[
            jax.ShapeDtypeStruct((part, tokens), BF),
            jax.ShapeDtypeStruct((part, tokens), BF),
            jax.ShapeDtypeStruct((part, width), BF),
        ],
        in_specs=[smem_spec(), pl.BlockSpec((BLOCK, width), lambda i: (i, 0))]
        + [pl.BlockSpec((2, rows, part), lambda i: (0, 0, 0))] * shards,
        out_specs=[
            pl.BlockSpec((part, BLOCK), lambda i: (0, i)),
            pl.BlockSpec((part, BLOCK), lambda i: (0, i)),
            pl.BlockSpec((part, width), lambda i: (0, 0)),
        ],
        scratch_shapes=[pltpu.VMEM((width, part), BF), pltpu.VMEM((width, part), BF), pltpu.VMEM((part, width), BF)],
        compiler_params=params(24),
        name="up",
    )(ids, normed, *w_pieces)

    grad_scale = 1.0 / (tokens * width)
    scores = pl.pallas_call(
        functools.partial(
            grad_kernel,
            shards,
            particles,
            -(width ** (-0.5)) * grad_scale,
            -(hidden ** (-0.5)) * grad_scale,
            hidden ** (-0.5),
            pick,
        ),
        out_shape=[jax.ShapeDtypeStruct((2, rows, cols), BF)] * particles,
        in_specs=[smem_spec()] + [any_spec()] * (4 + len(sources)),
        out_specs=[any_spec()] * particles,
        scratch_shapes=[
            pltpu.VMEM((tokens, width), BF),
            pltpu.VMEM((tokens, width), BF),
            pltpu.VMEM((part, tokens), BF),
            pltpu.VMEM((part, tokens), BF),
            pltpu.VMEM((part, tokens), BF),
            pltpu.VMEM((part, width), BF),
            pltpu.VMEM((2, width, part), BF),
            pltpu.SemaphoreType.DMA((particles + 5,)),
        ],
        compiler_params=params(56),
        name="grads",
    )(ids, normed, act_t, slope_t, down_t, *sources)

    ratio = particles // shards
    arrived = []
    for t in range(particles):
        pairs = []
        for m, c, s in devices:
            mine, q = 2 * m + s // half, 2 * (s % half) + c
            u = (mine + ratio * q - t) % particles
            z, e = u // ratio, q * ratio + u % ratio
            pairs.append((dev(m, c, s), dev(e // 2 + z, e % 2, z)))
        arrived.append(move(scores[t], pairs))

    whole, arrived[0] = lax.optimization_barrier((whole, arrived[0]))
    pair_list = [(i, j) for i in range(particles) for j in range(i)]
    partial = pl.pallas_call(
        distance_kernel,
        out_shape=jax.ShapeDtypeStruct((len(pair_list), 8, LANES), F32),
        in_specs=[pl.BlockSpec(memory_space=pltpu.VMEM)],
        out_specs=pl.BlockSpec(memory_space=pltpu.VMEM),
        compiler_params=params(8),
        name="distances",
    )(whole)
    sums = jnp.sum(partial, axis=(1, 2))
    sums = jnp.pad(sums, (0, -len(pair_list) % LANES))
    for axis, count in (("particle", particles), ("shard", shards)):
        copies = jnp.broadcast_to(sums[None, None], (count, 1, sums.shape[0]))
        sums = jnp.sum(lax.all_to_all(copies, axis, 0, 0, tiled=True), axis=(0, 1))
    lookup = [
        [pair_list.index((max(i, j), min(i, j))) if i != j else len(pair_list) for j in range(particles)]
        for i in range(particles)
    ]
    table = jnp.concatenate([sums[: len(pair_list)], jnp.zeros((1,), F32)])
    distances = table[jnp.array(lookup, jnp.int32)]
    inverse_band = 1.0 / kernel_scale[0].astype(F32)
    repulse = 2.0 * inverse_band
    kernel = jnp.exp(-distances * inverse_band)
    scale = 2 * width * hidden / particles
    coef = jnp.concatenate(
        [(scale * kernel).reshape(-1), scale * repulse * jnp.sum(kernel, axis=1), repulse[None]]
    )

    fields = pl.pallas_call(
        functools.partial(stein_kernel, shards, particles),
        out_shape=[jax.ShapeDtypeStruct((2, rows, cols), BF)] * particles,
        in_specs=[smem_spec(), smem_spec(), pl.BlockSpec(memory_space=pltpu.VMEM)] + [any_spec()] * particles,
        out_specs=[any_spec()] * particles,
        scratch_shapes=[
            pltpu.VMEM((particles, 2, rows, cols), BF),
            pltpu.VMEM((particles, 2, rows, cols), BF),
            pltpu.SemaphoreType.DMA((particles,)),
        ],
        compiler_params=params(12),
        name="stein",
    )(ids, coef, whole, *arrived)

    back = []
    for k in range(columns):
        for x in range(2):
            pairs = [(dev(m, c, s), dev(m + k, c ^ x, s)) for m, c, s in devices]
            back.append(move(fields[2 * k + x], pairs))

    steps = max(rows // 32, 1)
    flat_rows = rows * 2 * lane_tiles
    state_spec = pl.BlockSpec((flat_rows // steps, LANES), lambda i: (i, 0))
    outs = pl.pallas_call(
        functools.partial(adam_kernel, particles),
        grid=(steps,),
        out_shape=[jax.ShapeDtypeStruct((flat_rows, LANES), F32)] * 4,
        in_specs=[smem_spec()] + [state_spec] * 3 + [any_spec()] * particles,
        out_specs=[state_spec] * 4,
        scratch_shapes=[pltpu.VMEM((2, rows, hidden), BF), pltpu.SemaphoreType.DMA((particles,))],
        compiler_params=params(56),
        name="adam",
    )(ids, w_flat, flat(first_moment), flat(second_moment), *back)
    return tuple(unflat(x) for x in outs)


def solution(mesh):
    state = P("particle", "shard", None, None)
    return jax.shard_map(
        local,
        mesh=mesh,
        in_specs=(P("shard", None), P("shard"), P(), P("particle", "shard", None), state, state, state),
        out_specs=(state, state, state, state),
        check_vma=False,
    )
```

```python
import functools

import jax
import jax.numpy as jnp
from jax import lax
from jax.experimental import pallas as pl
from jax.experimental.pallas import tpu as pltpu
from jax.sharding import PartitionSpec as P

BF = jnp.bfloat16
F32 = jnp.float32
AXES = ("particle", "shard")
LANES = 128
BLOCK = 256
MIB = 1024 * 1024
NT = (((1,), (1,)), ((), ()))

COL, CORE, SHARD, PROC, PIECE = range(5)


def any_spec():
    return pl.BlockSpec(memory_space=pl.ANY)


def smem_spec():
    return pl.BlockSpec(memory_space=pltpu.SMEM)


def params(mib):
    return pltpu.CompilerParams(vmem_limit_bytes=mib * MIB)


def cost(mib, flops=0):
    return pl.CostEstimate(flops=int(flops), bytes_accessed=int(mib * MIB), transcendentals=0)


def run_copies(copies):
    for copy in copies:
        copy.start()
    for copy in copies:
        copy.wait()


def slice_index(ids, column, core, shard, columns):
    return 2 * lax.rem(column - shard + columns * 16, columns) + core


def prep_kernel(shards, ids, w, *out):
    pieces, slices = out[:shards], out[shards]
    _, rows, piece = pieces[0].shape
    particles, _, _, cols = slices.shape
    columns = particles // 2
    tiles, per_slice = piece // LANES, cols // LANES
    for r in range(shards):
        q = lax.rem(ids[SHARD] - r + shards, shards)
        for j in range(tiles):
            e = q * (tiles // per_slice) + j // per_slice
            column = lax.rem(lax.div(e, 2) + ids[SHARD], columns)
            p = 2 * column + lax.rem(e, 2)
            at, within = j * LANES, j % per_slice * LANES
            for kind in range(2):
                line = 2 * (q * tiles + j) + kind
                part = w[pl.ds(line, rows, stride=2 * shards * tiles), :].astype(BF)
                pieces[r][kind, :, at : at + LANES] = part
                slices[p, kind, :, within : within + LANES] = part


def up_kernel(shards, scale, ids, tokens, *refs):
    pieces = refs[:shards]
    act_t, slope_t, down_t, up_w, down_w, up_t = refs[shards:]
    width, part = up_w.shape
    rows = width // shards

    @pl.when(pl.program_id(0) == 0)
    def _():
        for r in range(shards):
            at = pl.multiple_of(lax.rem(ids[PIECE] + r, shards) * rows, rows)
            up_w[pl.ds(at, rows), :] = pieces[r][0]
            down_w[pl.ds(at, rows), :] = pieces[r][1]
        for i in range(width // LANES):
            span = slice(i * LANES, (i + 1) * LANES)
            up_t[:, span] = up_w[span, :].astype(F32).T.astype(BF)
            down_t[:, span] = down_w[span, :].astype(F32).T.astype(BF)

    u = lax.dot_general(up_t[...], tokens[...], NT, preferred_element_type=F32) * scale
    cdf = 0.5 * (1.0 + lax.erf(u * 0.7071067811865476))
    density = jnp.exp(-0.5 * u * u) * 0.3989422804014327
    act_t[...] = (u * cdf).astype(BF)
    slope_t[...] = (cdf + u * density).astype(BF)


def grad_kernel(shards, particles, up_scale, down_scale, back_scale, pick, ids, normed, act_t, slope_t, down_t, *refs):
    n_in = len(refs) - particles - 8
    sources, out = refs[:n_in], refs[n_in : n_in + particles]
    c, n, act, slope, grad, down, score, sems = refs[n_in + particles :]
    part, tokens = act.shape
    width = c.shape[1]
    chunk = tokens // shards
    first = [
        pltpu.make_async_copy(down_t, down, sems.at[1]),
        pltpu.make_async_copy(slope_t, slope, sems.at[2]),
    ]
    later = [
        pltpu.make_async_copy(act_t, act, sems.at[3]),
        pltpu.make_async_copy(normed, n, sems.at[4]),
    ]
    for copy in first:
        copy.start()
    pick(ids, sources, c, sems.at[0])
    for copy in later:
        copy.start()
    for copy in first:
        copy.wait()
    pltpu.make_async_copy(c, c, sems.at[0]).wait()

    def back(i, carry):
        at = pl.multiple_of(i * chunk, chunk)
        b = lax.dot_general(down[...], c[pl.ds(at, chunk), :], NT, preferred_element_type=F32)
        grad[:, pl.ds(at, chunk)] = (b * (slope[:, pl.ds(at, chunk)].astype(F32) * back_scale)).astype(BF)
        return carry

    lax.fori_loop(0, shards, back, 0)
    for copy in later:
        copy.wait()

    def gradient(j, carry):
        at = pl.multiple_of(j * BLOCK, BLOCK)
        g = jnp.dot(grad[...], n[:, pl.ds(at, BLOCK)], preferred_element_type=F32)
        score[0, pl.ds(at, BLOCK), :] = (g * up_scale).T.astype(BF)
        g = jnp.dot(act[...], c[:, pl.ds(at, BLOCK)], preferred_element_type=F32)
        score[1, pl.ds(at, BLOCK), :] = (g * down_scale).T.astype(BF)
        return carry

    lax.fori_loop(0, width // BLOCK, gradient, 0)
    rows = width // shards
    ratio = particles // shards
    cols = part // ratio
    mine = 2 * ids[COL] + ids[PROC]
    copies = []
    for t in range(particles):
        u = lax.rem(mine + ratio * ids[PIECE] - t + particles, particles)
        row = pl.multiple_of(lax.div(u, ratio) * rows, rows)
        col = pl.multiple_of(lax.rem(u, ratio) * cols, cols)
        copies.append(pltpu.make_async_copy(score.at[:, pl.ds(row, rows), pl.ds(col, cols)], out[t], sems.at[t]))
    run_copies(copies)


def distance_kernel(whole, out):
    particles, _, rows, cols = whole.shape
    pairs = [(i, j) for i in range(particles) for j in range(i)]
    tiles = cols // LANES

    def body(g, acc):
        kind = lax.div(g, rows // 16)
        row = pl.multiple_of(lax.rem(g, rows // 16) * 16, 16)
        for tile in range(tiles):
            w = [whole[p, kind, pl.ds(row, 16), tile * LANES : (tile + 1) * LANES].astype(F32) for p in range(particles)]
            new = []
            for a, (i, j) in zip(acc, pairs):
                d = w[i] - w[j]
                d = d * d
                new.append(a + (d[:8] + d[8:]))
            acc = tuple(new)
        return acc

    acc = lax.fori_loop(0, 2 * rows // 16, body, tuple(jnp.zeros((8, LANES), F32) for _ in pairs))
    lane = lax.broadcasted_iota(jnp.int32, (8, LANES), 1)
    row = jnp.zeros((8, LANES), F32)
    for i, a in enumerate(acc):
        total = jnp.sum(jnp.sum(a, axis=0, keepdims=True), axis=1, keepdims=True)
        row = row + jnp.where(lane == i, total, 0.0)
    out[...] = row


def stein_kernel(shards, particles, ids, coef, whole, *refs):
    sources, out = refs[:particles], refs[particles : 2 * particles]
    scores, field, sems = refs[2 * particles :]
    columns = particles // 2
    ratio = particles // shards
    _, _, rows, cols = whole.shape
    e = slice_index(ids, ids[COL], ids[CORE], ids[SHARD], columns)
    u = ids[SHARD] * ratio + lax.rem(e, ratio) + particles * shards - ratio * lax.div(e, ratio)
    run_copies(
        [pltpu.make_async_copy(sources[t], scores.at[lax.rem(u + t, particles)], sems.at[t]) for t in range(particles)]
    )
    repulse = coef[particles * particles + particles]
    groups = rows // 16
    tiles = cols // LANES

    def body(g, carry):
        kind = lax.div(g, groups)
        row = pl.multiple_of(lax.rem(g, groups) * 16, 16)
        for tile in range(tiles):
            at = (kind, pl.ds(row, 16), slice(tile * LANES, (tile + 1) * LANES))
            w = [whole[(p,) + at].astype(F32) for p in range(particles)]
            pushed = [scores[(p,) + at].astype(F32) - repulse * w[p] for p in range(particles)]
            for i in range(particles):
                total = coef[particles * particles + i] * w[i]
                for j in range(particles):
                    total = total + coef[i * particles + j] * pushed[j]
                field[(i,) + at] = total.astype(BF)
        return carry

    lax.fori_loop(0, 2 * groups, body, 0)
    copies = []
    for k in range(columns):
        for x in range(2):
            column = lax.rem(ids[COL] + k, columns)
            core = ids[CORE] if x == 0 else 1 - ids[CORE]
            i = 2 * k + x
            copies.append(pltpu.make_async_copy(field.at[2 * column + core], out[i], sems.at[i]))
    run_copies(copies)


def adam_kernel(particles, ids, w, first, second, *refs):
    sources = refs[:particles]
    new_w, new_first, new_second, transport, field, sems = refs[particles:]
    columns = particles // 2
    _, _, hidden = field.shape
    width = hidden // particles
    step = pl.program_id(0)

    @pl.when(step == 0)
    def _():
        copies = []
        for k in range(columns):
            for x in range(2):
                column = lax.rem(ids[COL] - k + columns, columns)
                core = ids[CORE] if x == 0 else 1 - ids[CORE]
                at = pl.multiple_of(slice_index(ids, column, core, ids[SHARD], columns) * width, width)
                i = 2 * k + x
                copies.append(pltpu.make_async_copy(sources[i], field.at[:, :, pl.ds(at, width)], sems.at[i]))
        run_copies(copies)

    lane_tiles = hidden // LANES
    rows = w.shape[0] // (2 * lane_tiles)
    base = pl.multiple_of(step * rows, rows)
    for kind in range(2):
        for tile in range(lane_tiles):
            part = field[kind, pl.ds(base, rows), tile * LANES : (tile + 1) * LANES]
            transport[pl.ds(2 * tile + kind, rows, stride=2 * lane_tiles), :] = part.astype(F32)
    t = transport[...]
    m = 0.9 * first[...] - 0.1 * t
    v = 0.999 * second[...] + 0.001 * t * t
    new_first[...] = m
    new_second[...] = v
    new_w[...] = w[...] - 0.01 * m / (jnp.sqrt(v) + 1e-08)


def local(pool, batch_index, kernel_scale, cotangent, weights, first_moment, second_moment):
    shards = lax.axis_size("shard")
    particles = lax.axis_size("particle")
    columns, half = particles // 2, shards // 2
    tok_rows = batch_index.shape[0]
    width = pool.shape[1]
    _, rows, _, hidden = weights.shape
    part, cols = hidden // shards, hidden // particles
    tokens = tok_rows * shards
    blocks = tokens // BLOCK
    lane_tiles = hidden // LANES

    own = lax.axis_index("particle")
    shard = lax.axis_index("shard")
    core, column = own % 2, own // 2
    proc = shard // half
    piece = 2 * (shard % half) + core
    ids = jnp.stack([column, core, shard, proc, piece]).astype(jnp.int32)
    devices = [(m, c, s) for m in range(columns) for c in range(2) for s in range(shards)]

    def dev(m, c, s):
        return (2 * (m % columns) + c) * shards + s

    def move(x, pairs):
        if all(a == b for a, b in pairs) and len(pairs) == len(devices):
            return x
        return lax.ppermute(x, AXES, pairs)

    def swap_of(among):
        return [(dev(m, c, s), dev(m, 1 - c, s)) for m, c, s in devices if s in among]

    def flat(x):
        return x[0].reshape(rows, 2, lane_tiles, LANES).transpose(0, 2, 1, 3).reshape(-1, LANES)

    def unflat(x):
        return x.reshape(rows, lane_tiles, 2, LANES).transpose(0, 2, 1, 3).reshape(1, rows, 2, hidden)

    everyone = range(shards)
    half_rows = tok_rows // 2
    share = tok_rows // particles
    index = lax.dynamic_slice(batch_index, (own * share,), (share,))
    picked = jnp.take(pool, index, axis=0).astype(F32)
    normed = (picked * lax.rsqrt(jnp.mean(picked * picked, axis=1, keepdims=True) + 1e-06)).astype(BF)

    def gather_tokens(x):
        shifted = [[(dev(m, c, s), dev(m, c, (s + k) % shards)) for m, c, s in devices] for k in range(shards)]
        x = jnp.stack([move(x, pairs) for pairs in shifted])
        return lax.all_gather(x[None], "particle", axis=0, tiled=True)

    w_flat = flat(weights)
    steps = max(rows // 64, 1)
    lines = w_flat.shape[0] // steps
    *prepared, slices = pl.pallas_call(
        functools.partial(prep_kernel, shards),
        grid=(steps,),
        out_shape=[jax.ShapeDtypeStruct((2, rows, part), BF)] * shards
        + [jax.ShapeDtypeStruct((particles, 2, rows, cols), BF)],
        in_specs=[smem_spec(), pl.BlockSpec((lines, LANES), lambda i: (i, 0))],
        out_specs=[pl.BlockSpec((2, rows // steps, part), lambda i: (0, i, 0))] * shards
        + [pl.BlockSpec((particles, 2, rows // steps, cols), lambda i: (0, 0, i, 0))],
        compiler_params=params(56),
        cost_estimate=cost(16),
        name="prep",
    )(ids, w_flat)

    w_routes = []
    for r in range(shards):
        pairs = []
        for m, c, s in devices:
            q = (s - r) % shards
            pairs.append((dev(m, c, s), dev(m, q % 2, c * half + q // 2)))
        w_routes.append(pairs)

    whole = lax.all_to_all(slices, "particle", 0, 0, tiled=True)

    pair_list = [(i, j) for i in range(particles) for j in range(i)]
    hops = []
    for count, stride in ((particles, shards), (shards, 1)):
        hop = 1
        while hop < count:
            hops.append([(d, d + ((d // stride % count ^ hop) - d // stride % count) * stride) for d in range(len(devices))])
            hop *= 2

    def pair_sums(whole):
        return pl.pallas_call(
            distance_kernel,
            out_shape=jax.ShapeDtypeStruct((8, LANES), F32),
            in_specs=[pl.BlockSpec(memory_space=pltpu.VMEM)],
            out_specs=pl.BlockSpec(memory_space=pltpu.VMEM),
            compiler_params=params(8),
            cost_estimate=cost(4),
            name="distances",
        )(whole)

    def add_over(sums, steps):
        for step in steps:
            sums = sums + move(sums, hops[step])
        return sums

    def gather_row(ids, which, turn):
        k = lax.rem(ids[SHARD] - which + shards, shards)
        return (turn * (particles // 2) * shards + k) * share

    def place(ids, ref, held, sem, which, turn, start=0):
        row = gather_row(ids, which, turn)
        for i in range(particles // 2):
            to = pl.multiple_of(row + i * shards * share, share)
            pltpu.make_async_copy(
                ref.at[pl.ds(start + i * share, share), :], held.at[pl.ds(to, share), :], sem
            ).start()

    if shards == 4:
        cot = cotangent[0]
        inner = jnp.logical_or(shard == 1, shard == 2)
        flip = jnp.where(jnp.logical_or(inner, core == proc), 0, 1)
        first_routes, second_routes = [], []
        for e in range(2):
            one, two = [], []
            for m, c, s in devices:
                at_home, is_inner = c == s // half, s in (1, 2)
                if not at_home:
                    to, turn = (3 - s, e) if is_inner else (1 if s == 3 else 2, 1 - e)
                    one.append((dev(m, c, s), dev(m, c ^ turn, to)))
                elif is_inner:
                    one.append((dev(m, c, s), dev(m, c ^ e, s ^ 1)))
                else:
                    two.append((dev(m, c, s), dev(m, c ^ e, s ^ 1)))
                if is_inner:
                    two.append((dev(m, c, s), dev(m, c, s ^ 1)))
            first_routes.append(one)
            second_routes.append(two)
        halves = [
            lax.dynamic_slice(cot, (((core + e + flip) % 2) * half_rows, 0), (half_rows, width)) for e in range(2)
        ]
        alpha = [move(x, route) for x, route in zip(halves, first_routes)]
        own_c = move(cot, [(dev(m, c, s), dev(m, 1 - c, s)) for m, c, s in devices if c == s // half])
        normed = gather_tokens(normed)
        alpha, own_c, prepared = lax.optimization_barrier((alpha, own_c, prepared))
        w_pieces = [move(x, route) for x, route in zip(prepared, w_routes)]
        hand_on = [jnp.where(inner, a, x) for a, x in zip(alpha, halves)]
        alpha_x = [move(x, swap_of(everyone)) for x in alpha]
        beta = [move(hand_on[0], second_routes[0])]
        hand_on[1], *w_pieces[:2] = lax.optimization_barrier((hand_on[1], *w_pieces[:2]))
        beta.append(move(hand_on[1], second_routes[1]))
        whole, alpha_x, beta[0] = lax.optimization_barrier((whole, alpha_x, beta[0]))
        sums = add_over(pair_sums(whole), range(len(hops) - 3))
        w_pieces, normed, sums = lax.optimization_barrier((w_pieces, normed, sums))
        beta_x = [move(x, swap_of(everyone)) for x in beta]
        sources = [cot, own_c, *alpha, *alpha_x, *beta, *beta_x]

        def pick(ids, refs, held, sem):
            s, core, proc = ids[SHARD], ids[CORE], ids[PROC]
            low = s < 2
            near, far, pair = jnp.where(low, 2, 1), jnp.where(low, 3, 0), s + 1 - 2 * lax.rem(s, 2)
            side = lax.rem(core + proc, 2)
            is_inner = jnp.logical_or(s == 1, s == 2)

            def own(ref):
                for turn in range(2):
                    place(ids, ref, held, sem, s, turn, turn * half_rows)

            def others(main, main_x, rest, rest_x):
                for e in range(2):
                    same = side == e
                    place(ids, main[e], held, sem, jnp.where(same, near, far), core)
                    place(ids, main_x[e], held, sem, jnp.where(same, far, near), 1 - core)

                    @pl.when(same)
                    def _():
                        place(ids, rest[e], held, sem, pair, core)
                        place(ids, rest_x[1 - e], held, sem, pair, 1 - core)

            @pl.when(side == 0)
            def _():
                own(refs[0])

            @pl.when(side == 1)
            def _():
                own(refs[1])

            @pl.when(is_inner)
            def _():
                others(refs[2:4], refs[4:6], refs[6:8], refs[8:10])

            @pl.when(jnp.logical_not(is_inner))
            def _():
                others(refs[6:8], refs[8:10], refs[2:4], refs[4:6])
    else:
        full = lax.all_gather(cotangent[0], "shard", axis=0, tiled=True)
        sources = [jnp.where(core == proc, full, move(full, swap_of(everyone)))]
        w_pieces = [move(x, route) for x, route in zip(prepared, w_routes)]
        normed = gather_tokens(normed)
        sums = add_over(pair_sums(whole), range(len(hops) - 3))

        def pick(ids, refs, held, sem):
            def one(which, carry):
                for turn in range(2):
                    start = pl.multiple_of(which * tok_rows + turn * half_rows, half_rows)
                    place(ids, refs[0], held, sem, which, turn, start)
                return carry

            lax.fori_loop(0, shards, one, 0)

    normed = normed.reshape(tokens, width)
    act_t, slope_t, down_t = pl.pallas_call(
        functools.partial(up_kernel, shards, width ** (-0.5)),
        grid=(blocks,),
        out_shape=[
            jax.ShapeDtypeStruct((part, tokens), BF),
            jax.ShapeDtypeStruct((part, tokens), BF),
            jax.ShapeDtypeStruct((part, width), BF),
        ],
        in_specs=[smem_spec(), pl.BlockSpec((BLOCK, width), lambda i: (i, 0))]
        + [pl.BlockSpec((2, rows, part), lambda i: (0, 0, 0))] * shards,
        out_specs=[
            pl.BlockSpec((part, BLOCK), lambda i: (0, i)),
            pl.BlockSpec((part, BLOCK), lambda i: (0, i)),
            pl.BlockSpec((part, width), lambda i: (0, 0)),
        ],
        scratch_shapes=[pltpu.VMEM((width, part), BF), pltpu.VMEM((width, part), BF), pltpu.VMEM((part, width), BF)],
        compiler_params=params(56),
        cost_estimate=cost(24, 2 * tokens * width * part),
        name="up",
    )(ids, normed, *w_pieces)

    sums = add_over(sums, [-3])
    sums, act_t, slope_t = lax.optimization_barrier((sums, act_t, slope_t))
    grad_scale = 1.0 / (tokens * width)
    scores = pl.pallas_call(
        functools.partial(
            grad_kernel,
            shards,
            particles,
            -(width ** (-0.5)) * grad_scale,
            -(hidden ** (-0.5)) * grad_scale,
            hidden ** (-0.5),
            pick,
        ),
        out_shape=[jax.ShapeDtypeStruct((2, rows, cols), BF)] * particles,
        in_specs=[smem_spec()] + [any_spec()] * (4 + len(sources)),
        out_specs=[any_spec()] * particles,
        scratch_shapes=[
            pltpu.VMEM((tokens, width), BF),
            pltpu.VMEM((tokens, width), BF),
            pltpu.VMEM((part, tokens), BF),
            pltpu.VMEM((part, tokens), BF),
            pltpu.VMEM((part, tokens), BF),
            pltpu.VMEM((part, width), BF),
            pltpu.VMEM((2, width, part), BF),
            pltpu.SemaphoreType.DMA((particles + 5,)),
        ],
        compiler_params=params(56),
        cost_estimate=cost(32, 6 * tokens * width * part),
        name="grads",
    )(ids, normed, act_t, slope_t, down_t, *sources)

    sums = add_over(sums, [-2])
    sums, *scores = lax.optimization_barrier((sums, *scores))

    ratio = particles // shards
    arrived = []
    for t in range(particles):
        pairs = []
        for m, c, s in devices:
            mine, q = 2 * m + s // half, 2 * (s % half) + c
            u = (mine + ratio * q - t) % particles
            z, e = u // ratio, q * ratio + u % ratio
            pairs.append((dev(m, c, s), dev(e // 2 + z, e % 2, z)))
        arrived.append(move(scores[t], pairs))

    rest = move(sums, hops[-1])
    sums, rest, *arrived[:4] = lax.optimization_barrier((sums, rest, *arrived[:4]))
    sums = sums + rest
    sums = sums[0]
    lookup = [
        [pair_list.index((max(i, j), min(i, j))) if i != j else len(pair_list) for j in range(particles)]
        for i in range(particles)
    ]
    table = jnp.concatenate([sums[: len(pair_list)], jnp.zeros((1,), F32)])
    distances = table[jnp.array(lookup, jnp.int32)]
    inverse_band = 1.0 / kernel_scale[0].astype(F32)
    repulse = 2.0 * inverse_band
    kernel = jnp.exp(-distances * inverse_band)
    scale = 2 * width * hidden / particles
    coef = jnp.concatenate(
        [(scale * kernel).reshape(-1), scale * repulse * jnp.sum(kernel, axis=1), repulse[None]]
    )

    fields = pl.pallas_call(
        functools.partial(stein_kernel, shards, particles),
        out_shape=[jax.ShapeDtypeStruct((2, rows, cols), BF)] * particles,
        in_specs=[smem_spec(), smem_spec(), pl.BlockSpec(memory_space=pltpu.VMEM)] + [any_spec()] * particles,
        out_specs=[any_spec()] * particles,
        scratch_shapes=[
            pltpu.VMEM((particles, 2, rows, cols), BF),
            pltpu.VMEM((particles, 2, rows, cols), BF),
            pltpu.SemaphoreType.DMA((particles,)),
        ],
        compiler_params=params(12),
        cost_estimate=cost(12),
        name="stein",
    )(ids, coef, whole, *arrived)

    back = []
    for k in range(columns):
        for x in range(2):
            pairs = [(dev(m, c, s), dev(m + k, c ^ x, s)) for m, c, s in devices]
            back.append(move(fields[2 * k + x], pairs))

    steps = max(rows // 32, 1)
    flat_rows = rows * 2 * lane_tiles
    state_spec = pl.BlockSpec((flat_rows // steps, LANES), lambda i: (i, 0))
    outs = pl.pallas_call(
        functools.partial(adam_kernel, particles),
        grid=(steps,),
        out_shape=[jax.ShapeDtypeStruct((flat_rows, LANES), F32)] * 4,
        in_specs=[smem_spec()] + [state_spec] * 3 + [any_spec()] * particles,
        out_specs=[state_spec] * 4,
        scratch_shapes=[pltpu.VMEM((2, rows, hidden), BF), pltpu.SemaphoreType.DMA((particles,))],
        compiler_params=params(56),
        cost_estimate=cost(32),
        name="adam",
    )(ids, w_flat, flat(first_moment), flat(second_moment), *back)
    return tuple(unflat(x) for x in outs)


def solution(mesh):
    state = P("particle", "shard", None, None)
    return jax.shard_map(
        local,
        mesh=mesh,
        in_specs=(P("shard", None), P("shard"), P(), P("particle", "shard", None), state, state, state),
        out_specs=(state, state, state, state),
        check_vma=False,
    )
```

```python
import functools

import jax
import jax.numpy as jnp
from jax import lax
from jax.experimental import pallas as pl
from jax.experimental.pallas import tpu as pltpu
from jax.sharding import PartitionSpec as P

BF = jnp.bfloat16
F32 = jnp.float32
AXES = ("particle", "shard")
LANES = 128
BLOCK = 256
MIB = 1024 * 1024
NT = (((1,), (1,)), ((), ()))

COL, CORE, SHARD, PROC, PIECE = range(5)


def any_spec():
    return pl.BlockSpec(memory_space=pl.ANY)


def smem_spec():
    return pl.BlockSpec(memory_space=pltpu.SMEM)


def params(mib):
    return pltpu.CompilerParams(vmem_limit_bytes=mib * MIB)


def run_copies(copies):
    for copy in copies:
        copy.start()
    for copy in copies:
        copy.wait()


def slice_index(ids, column, core, shard, columns):
    return 2 * lax.rem(column - shard + columns * 16, columns) + core


def prep_kernel(shards, batches, ids, w, *out):
    pieces, slices = out[:-1], out[-1]
    _, rows, piece = pieces[0].shape
    particles, _, _, cols = slices.shape
    columns = particles // 2
    ratio = particles // shards
    tiles, per_slice = piece // LANES, cols // batches // LANES
    stride = 2 * shards * batches * tiles
    for r in range(shards):
        q = lax.rem(ids[SHARD] - r + shards, shards)
        for batch in range(batches):
            for j in range(tiles):
                e = q * ratio + j // per_slice
                column = lax.rem(lax.div(e, 2) + ids[SHARD], columns)
                p = 2 * column + lax.rem(e, 2)
                at, within = j * LANES, (batch * per_slice + j % per_slice) * LANES
                for kind in range(2):
                    line = 2 * ((q * batches + batch) * tiles + j) + kind
                    part = w[pl.ds(line, rows, stride=stride), :].astype(BF)
                    pieces[batch * shards + r][kind, :, at : at + LANES] = part
                    slices[p, kind, :, within : within + LANES] = part


def up_kernel(shards, scale, ids, tokens, *refs):
    pieces = refs[:shards]
    act_t, slope_t, down_t, up_w, down_w, up_t = refs[shards:]
    width, part = up_w.shape
    rows = width // shards

    @pl.when(pl.program_id(0) == 0)
    def _():
        for r in range(shards):
            at = pl.multiple_of(lax.rem(ids[PIECE] + r, shards) * rows, rows)
            up_w[pl.ds(at, rows), :] = pieces[r][0]
            down_w[pl.ds(at, rows), :] = pieces[r][1]
        for i in range(width // LANES):
            span = slice(i * LANES, (i + 1) * LANES)
            up_t[:, span] = up_w[span, :].astype(F32).T.astype(BF)
            down_t[:, span] = down_w[span, :].astype(F32).T.astype(BF)

    u = lax.dot_general(up_t[...], tokens[...], NT, preferred_element_type=F32) * scale
    cdf = 0.5 * (1.0 + lax.erf(u * 0.7071067811865476))
    density = jnp.exp(-0.5 * u * u) * 0.3989422804014327
    act_t[...] = (u * cdf).astype(BF)
    slope_t[...] = (cdf + u * density).astype(BF)


def grad_kernel(shards, particles, up_scale, down_scale, back_scale, pick, ids, normed, act_t, slope_t, down_t, *refs):
    n_in = len(refs) - particles - 8
    sources, out = refs[:n_in], refs[n_in : n_in + particles]
    c, n, act, slope, grad, down, score, sems = refs[n_in + particles :]
    part, tokens = act.shape
    width = c.shape[1]
    chunk = tokens // shards
    first = [
        pltpu.make_async_copy(down_t, down, sems.at[1]),
        pltpu.make_async_copy(slope_t, slope, sems.at[2]),
    ]
    later = [
        pltpu.make_async_copy(act_t, act, sems.at[3]),
        pltpu.make_async_copy(normed, n, sems.at[4]),
    ]
    for copy in first:
        copy.start()
    pick(ids, sources, c, sems.at[0])
    for copy in later:
        copy.start()
    for copy in first:
        copy.wait()
    pltpu.make_async_copy(c, c, sems.at[0]).wait()

    def back(i, carry):
        at = pl.multiple_of(i * chunk, chunk)
        b = lax.dot_general(down[...], c[pl.ds(at, chunk), :], NT, preferred_element_type=F32)
        grad[:, pl.ds(at, chunk)] = (b * (slope[:, pl.ds(at, chunk)].astype(F32) * back_scale)).astype(BF)
        return carry

    lax.fori_loop(0, shards, back, 0)
    for copy in later:
        copy.wait()

    def gradient(j, carry):
        at = pl.multiple_of(j * BLOCK, BLOCK)
        g = jnp.dot(grad[...], n[:, pl.ds(at, BLOCK)], preferred_element_type=F32)
        score[0, pl.ds(at, BLOCK), :] = (g * up_scale).T.astype(BF)
        g = jnp.dot(act[...], c[:, pl.ds(at, BLOCK)], preferred_element_type=F32)
        score[1, pl.ds(at, BLOCK), :] = (g * down_scale).T.astype(BF)
        return carry

    lax.fori_loop(0, width // BLOCK, gradient, 0)
    rows = width // shards
    ratio = particles // shards
    cols = part // ratio
    mine = 2 * ids[COL] + ids[PROC]
    copies = []
    for t in range(particles):
        u = lax.rem(mine + ratio * ids[PIECE] - t + particles, particles)
        row = pl.multiple_of(lax.div(u, ratio) * rows, rows)
        col = pl.multiple_of(lax.rem(u, ratio) * cols, cols)
        copies.append(pltpu.make_async_copy(score.at[:, pl.ds(row, rows), pl.ds(col, cols)], out[t], sems.at[t]))
    run_copies(copies)


def distance_kernel(whole, out):
    particles, _, rows, cols = whole.shape
    pairs = [(i, j) for i in range(particles) for j in range(i)]
    tiles = cols // LANES

    def body(g, acc):
        kind = lax.div(g, rows // 16)
        row = pl.multiple_of(lax.rem(g, rows // 16) * 16, 16)
        for tile in range(tiles):
            w = [whole[p, kind, pl.ds(row, 16), tile * LANES : (tile + 1) * LANES].astype(F32) for p in range(particles)]
            new = []
            for a, (i, j) in zip(acc, pairs):
                d = w[i] - w[j]
                d = d * d
                new.append(a + (d[:8] + d[8:]))
            acc = tuple(new)
        return acc

    acc = lax.fori_loop(0, 2 * rows // 16, body, tuple(jnp.zeros((8, LANES), F32) for _ in pairs))
    lane = lax.broadcasted_iota(jnp.int32, (8, LANES), 1)
    row = jnp.zeros((8, LANES), F32)
    for i, a in enumerate(acc):
        total = jnp.sum(jnp.sum(a, axis=0, keepdims=True), axis=1, keepdims=True)
        row = row + jnp.where(lane == i, total, 0.0)
    out[...] = row


def stein_kernel(shards, particles, ids, coef, whole, *refs):
    sources, out = refs[:particles], refs[particles : 2 * particles]
    scores, field, sems = refs[2 * particles :]
    columns = particles // 2
    ratio = particles // shards
    _, _, rows, cols = whole.shape
    e = slice_index(ids, ids[COL], ids[CORE], ids[SHARD], columns)
    u = ids[SHARD] * ratio + lax.rem(e, ratio) + particles * shards - ratio * lax.div(e, ratio)
    run_copies(
        [pltpu.make_async_copy(sources[t], scores.at[lax.rem(u + t, particles)], sems.at[t]) for t in range(particles)]
    )
    repulse = coef[particles * particles + particles]
    groups = rows // 16
    tiles = cols // LANES

    def body(g, carry):
        kind = lax.div(g, groups)
        row = pl.multiple_of(lax.rem(g, groups) * 16, 16)
        for tile in range(tiles):
            at = (kind, pl.ds(row, 16), slice(tile * LANES, (tile + 1) * LANES))
            w = [whole[(p,) + at].astype(F32) for p in range(particles)]
            pushed = [scores[(p,) + at].astype(F32) - repulse * w[p] for p in range(particles)]
            for i in range(particles):
                total = coef[particles * particles + i] * w[i]
                for j in range(particles):
                    total = total + coef[i * particles + j] * pushed[j]
                field[(i,) + at] = total.astype(BF)
        return carry

    lax.fori_loop(0, 2 * groups, body, 0)
    copies = []
    for k in range(columns):
        for x in range(2):
            column = lax.rem(ids[COL] + k, columns)
            core = ids[CORE] if x == 0 else 1 - ids[CORE]
            i = 2 * k + x
            copies.append(pltpu.make_async_copy(field.at[2 * column + core], out[i], sems.at[i]))
    run_copies(copies)


def adam_kernel(shards, particles, batches, ids, w, first, second, *refs):
    sources = refs[: batches * particles]
    new_w, new_first, new_second, transport, field, sems = refs[batches * particles :]
    columns = particles // 2
    _, _, hidden = field.shape
    ratio = particles // shards
    piece = hidden // shards // batches
    width = piece // ratio
    step = pl.program_id(0)

    @pl.when(step == 0)
    def _():
        copies = []
        for k in range(columns):
            for x in range(2):
                column = lax.rem(ids[COL] - k + columns, columns)
                core = ids[CORE] if x == 0 else 1 - ids[CORE]
                e = slice_index(ids, column, core, ids[SHARD], columns)
                for batch in range(batches):
                    at = (lax.div(e, ratio) * batches + batch) * piece + lax.rem(e, ratio) * width
                    at = pl.multiple_of(at, width)
                    i = batch * particles + 2 * k + x
                    copies.append(pltpu.make_async_copy(sources[i], field.at[:, :, pl.ds(at, width)], sems.at[i]))
        run_copies(copies)

    lane_tiles = hidden // LANES
    rows = w.shape[0] // (2 * lane_tiles)
    base = pl.multiple_of(step * rows, rows)
    for kind in range(2):
        for tile in range(lane_tiles):
            part = field[kind, pl.ds(base, rows), tile * LANES : (tile + 1) * LANES]
            transport[pl.ds(2 * tile + kind, rows, stride=2 * lane_tiles), :] = part.astype(F32)
    t = transport[...]
    m = 0.9 * first[...] - 0.1 * t
    v = 0.999 * second[...] + 0.001 * t * t
    new_first[...] = m
    new_second[...] = v
    new_w[...] = w[...] - 0.01 * m / (jnp.sqrt(v) + 1e-08)


def local(pool, batch_index, kernel_scale, cotangent, weights, first_moment, second_moment):
    shards = lax.axis_size("shard")
    particles = lax.axis_size("particle")
    columns, half = particles // 2, shards // 2
    tok_rows = batch_index.shape[0]
    width = pool.shape[1]
    _, rows, _, hidden = weights.shape
    batches = 2 if hidden // particles >= 2 * LANES else 1
    part, cols = hidden // shards // batches, hidden // particles
    tokens = tok_rows * shards
    blocks = tokens // BLOCK
    lane_tiles = hidden // LANES

    own = lax.axis_index("particle")
    shard = lax.axis_index("shard")
    core, column = own % 2, own // 2
    proc = shard // half
    piece = 2 * (shard % half) + core
    ids = jnp.stack([column, core, shard, proc, piece]).astype(jnp.int32)
    devices = [(m, c, s) for m in range(columns) for c in range(2) for s in range(shards)]

    def dev(m, c, s):
        return (2 * (m % columns) + c) * shards + s

    def move(x, pairs):
        if all(a == b for a, b in pairs) and len(pairs) == len(devices):
            return x
        return lax.ppermute(x, AXES, pairs)

    def swap_of(among):
        return [(dev(m, c, s), dev(m, 1 - c, s)) for m, c, s in devices if s in among]

    def flat(x):
        return x[0].reshape(rows, 2, lane_tiles, LANES).transpose(0, 2, 1, 3).reshape(-1, LANES)

    def unflat(x):
        return x.reshape(rows, lane_tiles, 2, LANES).transpose(0, 2, 1, 3).reshape(1, rows, 2, hidden)

    everyone = range(shards)
    half_rows = tok_rows // 2
    share = tok_rows // particles
    index = lax.dynamic_slice(batch_index, (own * share,), (share,))
    picked = jnp.take(pool, index, axis=0).astype(F32)
    normed = (picked * lax.rsqrt(jnp.mean(picked * picked, axis=1, keepdims=True) + 1e-06)).astype(BF)

    def shift_tokens(x):
        shifted = [[(dev(m, c, s), dev(m, c, (s + k) % shards)) for m, c, s in devices] for k in range(shards)]
        return jnp.stack([move(x, pairs) for pairs in shifted])

    w_flat = flat(weights)
    steps = max(rows // 64, 1)
    lines = w_flat.shape[0] // steps
    *prepared, slices = pl.pallas_call(
        functools.partial(prep_kernel, shards, batches),
        grid=(steps,),
        out_shape=[jax.ShapeDtypeStruct((2, rows, part), BF)] * (batches * shards)
        + [jax.ShapeDtypeStruct((particles, 2, rows, cols), BF)],
        in_specs=[smem_spec(), pl.BlockSpec((lines, LANES), lambda i: (i, 0))],
        out_specs=[pl.BlockSpec((2, rows // steps, part), lambda i: (0, i, 0))] * (batches * shards)
        + [pl.BlockSpec((particles, 2, rows // steps, cols), lambda i: (0, 0, i, 0))],
        compiler_params=params(56),
        name="prep",
    )(ids, w_flat)

    w_routes = []
    for r in range(shards):
        pairs = []
        for m, c, s in devices:
            q = (s - r) % shards
            pairs.append((dev(m, c, s), dev(m, q % 2, c * half + q // 2)))
        w_routes.append(pairs)

    whole = lax.all_to_all(slices, "particle", 0, 0, tiled=True)

    pair_list = [(i, j) for i in range(particles) for j in range(i)]
    hops = []
    for count, stride in ((particles, shards), (shards, 1)):
        hop = 1
        while hop < count:
            hops.append([(d, d + ((d // stride % count ^ hop) - d // stride % count) * stride) for d in range(len(devices))])
            hop *= 2

    def pair_sums(whole):
        return pl.pallas_call(
            distance_kernel,
            out_shape=jax.ShapeDtypeStruct((8, LANES), F32),
            in_specs=[pl.BlockSpec(memory_space=pltpu.VMEM)],
            out_specs=pl.BlockSpec(memory_space=pltpu.VMEM),
            compiler_params=params(8),
                name="distances",
        )(whole)

    def add_over(sums, steps):
        for step in steps:
            sums = sums + move(sums, hops[step])
        return sums

    def gather_row(ids, which, turn):
        k = lax.rem(ids[SHARD] - which + shards, shards)
        return (turn * (particles // 2) * shards + k) * share

    def place(ids, ref, held, sem, which, turn, start=0):
        row = gather_row(ids, which, turn)
        for i in range(particles // 2):
            to = pl.multiple_of(row + i * shards * share, share)
            pltpu.make_async_copy(
                ref.at[pl.ds(start + i * share, share), :], held.at[pl.ds(to, share), :], sem
            ).start()

    if shards == 4:
        cot = cotangent[0]
        inner = jnp.logical_or(shard == 1, shard == 2)
        flip = jnp.where(jnp.logical_or(inner, core == proc), 0, 1)
        first_routes, second_routes = [], []
        for e in range(2):
            one, two = [], []
            for m, c, s in devices:
                at_home, is_inner = c == s // half, s in (1, 2)
                if not at_home:
                    to, turn = (3 - s, e) if is_inner else (1 if s == 3 else 2, 1 - e)
                    one.append((dev(m, c, s), dev(m, c ^ turn, to)))
                elif is_inner:
                    one.append((dev(m, c, s), dev(m, c ^ e, s ^ 1)))
                else:
                    two.append((dev(m, c, s), dev(m, c ^ e, s ^ 1)))
                if is_inner:
                    two.append((dev(m, c, s), dev(m, c, s ^ 1)))
            first_routes.append(one)
            second_routes.append(two)
        halves = [
            lax.dynamic_slice(cot, (((core + e + flip) % 2) * half_rows, 0), (half_rows, width)) for e in range(2)
        ]
        alpha = [move(x, route) for x, route in zip(halves, first_routes)]
        own_c = move(cot, [(dev(m, c, s), dev(m, 1 - c, s)) for m, c, s in devices if c == s // half])
        normed = shift_tokens(normed)
        alpha, own_c, prepared, normed = lax.optimization_barrier((alpha, own_c, prepared, normed))
        normed = lax.all_gather(normed[None], "particle", axis=0, tiled=True)
        w_pieces = [move(x, w_routes[i % shards]) for i, x in enumerate(prepared)]
        beta = [move(jnp.where(inner, a, x), route) for a, x, route in zip(alpha, halves, second_routes)]
        alpha_x = [move(x, swap_of(everyone)) for x in alpha]
        beta, alpha_x, w_pieces[:shards], normed = lax.optimization_barrier((beta, alpha_x, w_pieces[:shards], normed))
        beta_x = [move(x, swap_of(everyone)) for x in beta]
        sources = [cot, own_c, *alpha, *alpha_x, *beta, *beta_x]

        def pick(ids, refs, held, sem):
            s, core, proc = ids[SHARD], ids[CORE], ids[PROC]
            low = s < 2
            near, far, pair = jnp.where(low, 2, 1), jnp.where(low, 3, 0), s + 1 - 2 * lax.rem(s, 2)
            side = lax.rem(core + proc, 2)
            is_inner = jnp.logical_or(s == 1, s == 2)

            def own(ref):
                for turn in range(2):
                    place(ids, ref, held, sem, s, turn, turn * half_rows)

            def others(main, main_x, rest, rest_x):
                for e in range(2):
                    same = side == e
                    place(ids, main[e], held, sem, jnp.where(same, near, far), core)
                    place(ids, main_x[e], held, sem, jnp.where(same, far, near), 1 - core)

                    @pl.when(same)
                    def _():
                        place(ids, rest[e], held, sem, pair, core)
                        place(ids, rest_x[1 - e], held, sem, pair, 1 - core)

            @pl.when(side == 0)
            def _():
                own(refs[0])

            @pl.when(side == 1)
            def _():
                own(refs[1])

            @pl.when(is_inner)
            def _():
                others(refs[2:4], refs[4:6], refs[6:8], refs[8:10])

            @pl.when(jnp.logical_not(is_inner))
            def _():
                others(refs[6:8], refs[8:10], refs[2:4], refs[4:6])
    else:
        full = lax.all_gather(cotangent[0], "shard", axis=0, tiled=True)
        sources = [jnp.where(core == proc, full, move(full, swap_of(everyone)))]
        w_pieces = [move(x, w_routes[i % shards]) for i, x in enumerate(prepared)]
        normed = lax.all_gather(shift_tokens(normed)[None], "particle", axis=0, tiled=True)

        def pick(ids, refs, held, sem):
            def one(which, carry):
                for turn in range(2):
                    start = pl.multiple_of(which * tok_rows + turn * half_rows, half_rows)
                    place(ids, refs[0], held, sem, which, turn, start)
                return carry

            lax.fori_loop(0, shards, one, 0)

    normed = normed.reshape(tokens, width)
    grad_scale = 1.0 / (tokens * width)
    ratio = particles // shards
    score_routes = []
    for t in range(particles):
        pairs = []
        for m, c, s in devices:
            mine, q = 2 * m + s // half, 2 * (s % half) + c
            u = (mine + ratio * q - t) % particles
            z, e = u // ratio, q * ratio + u % ratio
            pairs.append((dev(m, c, s), dev(e // 2 + z, e % 2, z)))
        score_routes.append(pairs)

    def up(pieces):
        return pl.pallas_call(
            functools.partial(up_kernel, shards, width ** (-0.5)),
            grid=(blocks,),
            out_shape=[
                jax.ShapeDtypeStruct((part, tokens), BF),
                jax.ShapeDtypeStruct((part, tokens), BF),
                jax.ShapeDtypeStruct((part, width), BF),
            ],
            in_specs=[smem_spec(), pl.BlockSpec((BLOCK, width), lambda i: (i, 0))]
            + [pl.BlockSpec((2, rows, part), lambda i: (0, 0, 0))] * shards,
            out_specs=[
                pl.BlockSpec((part, BLOCK), lambda i: (0, i)),
                pl.BlockSpec((part, BLOCK), lambda i: (0, i)),
                pl.BlockSpec((part, width), lambda i: (0, 0)),
            ],
            scratch_shapes=[
                pltpu.VMEM((width, part), BF),
                pltpu.VMEM((width, part), BF),
                pltpu.VMEM((part, width), BF),
            ],
            compiler_params=params(56),
            name="up",
        )(ids, normed, *pieces)

    def gradients(act_t, slope_t, down_t):
        return pl.pallas_call(
            functools.partial(
                grad_kernel,
                shards,
                particles,
                -(width ** (-0.5)) * grad_scale,
                -(hidden ** (-0.5)) * grad_scale,
                hidden ** (-0.5),
                pick,
            ),
            out_shape=[jax.ShapeDtypeStruct((2, rows, cols // batches), BF)] * particles,
            in_specs=[smem_spec()] + [any_spec()] * (4 + len(sources)),
            out_specs=[any_spec()] * particles,
            scratch_shapes=[
                pltpu.VMEM((tokens, width), BF),
                pltpu.VMEM((tokens, width), BF),
                pltpu.VMEM((part, tokens), BF),
                pltpu.VMEM((part, tokens), BF),
                pltpu.VMEM((part, tokens), BF),
                pltpu.VMEM((part, width), BF),
                pltpu.VMEM((2, width, part), BF),
                pltpu.SemaphoreType.DMA((particles + 5,)),
            ],
            compiler_params=params(56),
            name="grads",
        )(ids, normed, act_t, slope_t, down_t, *sources)

    arrived, sums = [], None
    for batch in range(batches):
        act_t, slope_t, down_t = up(w_pieces[batch * shards : (batch + 1) * shards])
        if batch == 0:
            whole, act_t = lax.optimization_barrier((whole, act_t))
            sums = add_over(pair_sums(whole), range(len(hops) - 3))
        else:
            sums = add_over(sums, [-3])
            sums, act_t = lax.optimization_barrier((sums, act_t))
        scores = gradients(act_t, slope_t, down_t)
        sums, *scores = lax.optimization_barrier((sums, *scores))
        arrived.append([move(x, route) for x, route in zip(scores, score_routes)])
    if batches == 1:
        sums = add_over(sums, [-3])
    sums = add_over(sums, [-2])
    rest = move(sums, hops[-1])
    sums, rest, arrived[0] = lax.optimization_barrier((sums, rest, arrived[0]))
    sums = sums + rest
    sums = sums[0]
    lookup = [
        [pair_list.index((max(i, j), min(i, j))) if i != j else len(pair_list) for j in range(particles)]
        for i in range(particles)
    ]
    table = jnp.concatenate([sums[: len(pair_list)], jnp.zeros((1,), F32)])
    distances = table[jnp.array(lookup, jnp.int32)]
    inverse_band = 1.0 / kernel_scale[0].astype(F32)
    repulse = 2.0 * inverse_band
    kernel = jnp.exp(-distances * inverse_band)
    scale = 2 * width * hidden / particles
    coef = jnp.concatenate(
        [(scale * kernel).reshape(-1), scale * repulse * jnp.sum(kernel, axis=1), repulse[None]]
    )

    back = []
    for batch in range(batches):
        fields = pl.pallas_call(
            functools.partial(stein_kernel, shards, particles),
            grid=(1,),
            out_shape=[jax.ShapeDtypeStruct((2, rows, cols // batches), BF)] * particles,
            in_specs=[
                smem_spec(),
                smem_spec(),
                pl.BlockSpec((particles, 2, rows, cols // batches), lambda i, batch=batch: (0, 0, 0, batch)),
            ]
            + [any_spec()] * particles,
            out_specs=[any_spec()] * particles,
            scratch_shapes=[
                pltpu.VMEM((particles, 2, rows, cols // batches), BF),
                pltpu.VMEM((particles, 2, rows, cols // batches), BF),
                pltpu.SemaphoreType.DMA((particles,)),
            ],
            compiler_params=params(12),
            name="stein",
        )(ids, coef, whole, *arrived[batch])
        for k in range(columns):
            for x in range(2):
                pairs = [(dev(m, c, s), dev(m + k, c ^ x, s)) for m, c, s in devices]
                back.append(move(fields[2 * k + x], pairs))

    steps = max(rows // 32, 1)
    flat_rows = rows * 2 * lane_tiles
    state_spec = pl.BlockSpec((flat_rows // steps, LANES), lambda i: (i, 0))
    outs = pl.pallas_call(
        functools.partial(adam_kernel, shards, particles, batches),
        grid=(steps,),
        out_shape=[jax.ShapeDtypeStruct((flat_rows, LANES), F32)] * 4,
        in_specs=[smem_spec()] + [state_spec] * 3 + [any_spec()] * len(back),
        out_specs=[state_spec] * 4,
        scratch_shapes=[pltpu.VMEM((2, rows, hidden), BF), pltpu.SemaphoreType.DMA((len(back),))],
        compiler_params=params(56),
        name="adam",
    )(ids, w_flat, flat(first_moment), flat(second_moment), *back)
    return tuple(unflat(x) for x in outs)


def solution(mesh):
    state = P("particle", "shard", None, None)
    return jax.shard_map(
        local,
        mesh=mesh,
        in_specs=(P("shard", None), P("shard"), P(), P("particle", "shard", None), state, state, state),
        out_specs=(state, state, state, state),
        check_vma=False,
    )
```

```python
import functools

import jax
import jax.numpy as jnp
from jax import lax
from jax.experimental import pallas as pl
from jax.experimental.pallas import tpu as pltpu
from jax.sharding import PartitionSpec as P

BF = jnp.bfloat16
F32 = jnp.float32
AXES = ("particle", "shard")
LANES = 128
BLOCK = 256
MIB = 1024 * 1024
NT = (((1,), (1,)), ((), ()))

COL, CORE, SHARD, PROC, PIECE = range(5)


def any_spec():
    return pl.BlockSpec(memory_space=pl.ANY)


def smem_spec():
    return pl.BlockSpec(memory_space=pltpu.SMEM)


def params(mib):
    return pltpu.CompilerParams(vmem_limit_bytes=mib * MIB)


def run_copies(copies):
    for copy in copies:
        copy.start()
    for copy in copies:
        copy.wait()


def slice_index(ids, column, core, shard, columns):
    return 2 * lax.rem(column - shard + columns * 16, columns) + core


def prep_kernel(shards, ids, w, *out):
    pieces, slices = out[:shards], out[shards]
    _, rows, piece = pieces[0].shape
    particles, _, _, cols = slices.shape
    columns = particles // 2
    tiles, per_slice = piece // LANES, cols // LANES
    for r in range(shards):
        q = lax.rem(ids[SHARD] - r + shards, shards)
        for j in range(tiles):
            e = q * (tiles // per_slice) + j // per_slice
            column = lax.rem(lax.div(e, 2) + ids[SHARD], columns)
            p = 2 * column + lax.rem(e, 2)
            at, within = j * LANES, j % per_slice * LANES
            for kind in range(2):
                line = 2 * (q * tiles + j) + kind
                part = w[pl.ds(line, rows, stride=2 * shards * tiles), :].astype(BF)
                pieces[r][kind, :, at : at + LANES] = part
                slices[p, kind, :, within : within + LANES] = part


def up_kernel(shards, scale, ids, tokens, *refs):
    pieces = refs[:shards]
    act_t, slope_t, down_t, up_w, down_w, up_t = refs[shards:]
    width, part = up_w.shape
    rows = width // shards

    @pl.when(pl.program_id(0) == 0)
    def _():
        for r in range(shards):
            at = pl.multiple_of(lax.rem(ids[PIECE] + r, shards) * rows, rows)
            up_w[pl.ds(at, rows), :] = pieces[r][0]
            down_w[pl.ds(at, rows), :] = pieces[r][1]
        for i in range(width // LANES):
            span = slice(i * LANES, (i + 1) * LANES)
            up_t[:, span] = up_w[span, :].astype(F32).T.astype(BF)
            down_t[:, span] = down_w[span, :].astype(F32).T.astype(BF)

    u = lax.dot_general(up_t[...], tokens[...], NT, preferred_element_type=F32) * scale
    cdf = 0.5 * (1.0 + lax.erf(u * 0.7071067811865476))
    density = jnp.exp(-0.5 * u * u) * 0.3989422804014327
    act_t[...] = (u * cdf).astype(BF)
    slope_t[...] = (cdf + u * density).astype(BF)


def grad_kernel(shards, particles, up_scale, down_scale, back_scale, pick, ids, normed, act_t, slope_t, down_t, *refs):
    n_in = len(refs) - particles - 8
    sources, out = refs[:n_in], refs[n_in : n_in + particles]
    c, n, act, slope, grad, down, score, sems = refs[n_in + particles :]
    part, tokens = act.shape
    width = c.shape[1]
    chunk = tokens // shards
    first = [
        pltpu.make_async_copy(down_t, down, sems.at[1]),
        pltpu.make_async_copy(slope_t, slope, sems.at[2]),
    ]
    later = [
        pltpu.make_async_copy(act_t, act, sems.at[3]),
        pltpu.make_async_copy(normed, n, sems.at[4]),
    ]
    for copy in first:
        copy.start()
    pick(ids, sources, c, sems.at[0])
    for copy in later:
        copy.start()
    for copy in first:
        copy.wait()
    pltpu.make_async_copy(c, c, sems.at[0]).wait()

    def back(i, carry):
        at = pl.multiple_of(i * chunk, chunk)
        b = lax.dot_general(down[...], c[pl.ds(at, chunk), :], NT, preferred_element_type=F32)
        grad[:, pl.ds(at, chunk)] = (b * (slope[:, pl.ds(at, chunk)].astype(F32) * back_scale)).astype(BF)
        return carry

    lax.fori_loop(0, shards, back, 0)
    for copy in later:
        copy.wait()

    def gradient(j, carry):
        at = pl.multiple_of(j * BLOCK, BLOCK)
        g = jnp.dot(grad[...], n[:, pl.ds(at, BLOCK)], preferred_element_type=F32)
        score[0, pl.ds(at, BLOCK), :] = (g * up_scale).T.astype(BF)
        g = jnp.dot(act[...], c[:, pl.ds(at, BLOCK)], preferred_element_type=F32)
        score[1, pl.ds(at, BLOCK), :] = (g * down_scale).T.astype(BF)
        return carry

    lax.fori_loop(0, width // BLOCK, gradient, 0)
    rows = width // shards
    ratio = particles // shards
    cols = part // ratio
    mine = 2 * ids[COL] + ids[PROC]
    copies = []
    for t in range(particles):
        u = lax.rem(mine + ratio * ids[PIECE] - t + particles, particles)
        row = pl.multiple_of(lax.div(u, ratio) * rows, rows)
        col = pl.multiple_of(lax.rem(u, ratio) * cols, cols)
        copies.append(pltpu.make_async_copy(score.at[:, pl.ds(row, rows), pl.ds(col, cols)], out[t], sems.at[t]))
    run_copies(copies)


def distance_kernel(whole, out):
    particles, _, rows, cols = whole.shape
    pairs = [(i, j) for i in range(particles) for j in range(i)]
    tiles = cols // LANES

    def body(g, acc):
        kind = lax.div(g, rows // 16)
        row = pl.multiple_of(lax.rem(g, rows // 16) * 16, 16)
        for tile in range(tiles):
            w = [whole[p, kind, pl.ds(row, 16), tile * LANES : (tile + 1) * LANES].astype(F32) for p in range(particles)]
            new = []
            for a, (i, j) in zip(acc, pairs):
                d = w[i] - w[j]
                d = d * d
                new.append(a + (d[:8] + d[8:]))
            acc = tuple(new)
        return acc

    acc = lax.fori_loop(0, 2 * rows // 16, body, tuple(jnp.zeros((8, LANES), F32) for _ in pairs))
    lane = lax.broadcasted_iota(jnp.int32, (8, LANES), 1)
    row = jnp.zeros((8, LANES), F32)
    for i, a in enumerate(acc):
        total = jnp.sum(jnp.sum(a, axis=0, keepdims=True), axis=1, keepdims=True)
        row = row + jnp.where(lane == i, total, 0.0)
    out[...] = row


def stein_kernel(shards, particles, ids, coef, whole, *refs):
    sources, out = refs[:particles], refs[particles : 2 * particles]
    scores, field, pushed, sems = refs[2 * particles :]
    columns = particles // 2
    ratio = particles // shards
    _, _, rows, cols = whole.shape
    e = slice_index(ids, ids[COL], ids[CORE], ids[SHARD], columns)
    u = ids[SHARD] * ratio + lax.rem(e, ratio) + particles * shards - ratio * lax.div(e, ratio)
    run_copies(
        [pltpu.make_async_copy(sources[t], scores.at[lax.rem(u + t, particles)], sems.at[t]) for t in range(particles)]
    )
    repulse = coef[particles * particles + particles]
    chunk = min(rows, 64)
    groups = rows // chunk
    tiles = cols // LANES

    def body(g, carry):
        kind = lax.div(g, groups)
        row = pl.multiple_of(lax.rem(g, groups) * chunk, chunk)
        for tile in range(tiles):
            at = (kind, pl.ds(row, chunk), slice(tile * LANES, (tile + 1) * LANES))
            for p in range(particles):
                pushed[p] = scores[(p,) + at].astype(F32) - repulse * whole[(p,) + at].astype(F32)
            for i in range(particles):
                total = coef[particles * particles + i] * whole[(i,) + at].astype(F32)
                for j in range(particles):
                    total = total + coef[i * particles + j] * pushed[j]
                field[(i,) + at] = total.astype(BF)
        return carry

    lax.fori_loop(0, 2 * groups, body, 0)
    copies = []
    for k in range(columns):
        for x in range(2):
            column = lax.rem(ids[COL] + k, columns)
            core = ids[CORE] if x == 0 else 1 - ids[CORE]
            i = 2 * k + x
            copies.append(pltpu.make_async_copy(field.at[2 * column + core], out[i], sems.at[i]))
    run_copies(copies)


def adam_kernel(particles, ids, w, first, second, *refs):
    sources = refs[:particles]
    new_w, new_first, new_second, transport, field, sems = refs[particles:]
    columns = particles // 2
    _, _, hidden = field.shape
    width = hidden // particles
    step = pl.program_id(0)

    @pl.when(step == 0)
    def _():
        copies = []
        for k in range(columns):
            for x in range(2):
                column = lax.rem(ids[COL] - k + columns, columns)
                core = ids[CORE] if x == 0 else 1 - ids[CORE]
                at = pl.multiple_of(slice_index(ids, column, core, ids[SHARD], columns) * width, width)
                i = 2 * k + x
                copies.append(pltpu.make_async_copy(sources[i], field.at[:, :, pl.ds(at, width)], sems.at[i]))
        run_copies(copies)

    lane_tiles = hidden // LANES
    rows = w.shape[0] // (2 * lane_tiles)
    base = pl.multiple_of(step * rows, rows)
    for kind in range(2):
        for tile in range(lane_tiles):
            part = field[kind, pl.ds(base, rows), tile * LANES : (tile + 1) * LANES]
            transport[pl.ds(2 * tile + kind, rows, stride=2 * lane_tiles), :] = part.astype(F32)
    t = transport[...]
    m = 0.9 * first[...] - 0.1 * t
    v = 0.999 * second[...] + 0.001 * t * t
    new_first[...] = m
    new_second[...] = v
    new_w[...] = w[...] - 0.01 * m / (jnp.sqrt(v) + 1e-08)


def local(pool, batch_index, kernel_scale, cotangent, weights, first_moment, second_moment):
    shards = lax.axis_size("shard")
    particles = lax.axis_size("particle")
    columns, half = particles // 2, shards // 2
    tok_rows = batch_index.shape[0]
    width = pool.shape[1]
    _, rows, _, hidden = weights.shape
    part, cols = hidden // shards, hidden // particles
    tokens = tok_rows * shards
    blocks = tokens // BLOCK
    lane_tiles = hidden // LANES

    own = lax.axis_index("particle")
    shard = lax.axis_index("shard")
    core, column = own % 2, own // 2
    proc = shard // half
    piece = 2 * (shard % half) + core
    ids = jnp.stack([column, core, shard, proc, piece]).astype(jnp.int32)
    devices = [(m, c, s) for m in range(columns) for c in range(2) for s in range(shards)]

    def dev(m, c, s):
        return (2 * (m % columns) + c) * shards + s

    def move(x, pairs):
        if all(a == b for a, b in pairs) and len(pairs) == len(devices):
            return x
        return lax.ppermute(x, AXES, pairs)

    def swap_of(among):
        return [(dev(m, c, s), dev(m, 1 - c, s)) for m, c, s in devices if s in among]

    def flat(x):
        return x[0].reshape(rows, 2, lane_tiles, LANES).transpose(0, 2, 1, 3).reshape(-1, LANES)

    def unflat(x):
        return x.reshape(rows, lane_tiles, 2, LANES).transpose(0, 2, 1, 3).reshape(1, rows, 2, hidden)

    everyone = range(shards)
    half_rows = tok_rows // 2
    share = tok_rows // particles
    index = lax.dynamic_slice(batch_index, (own * share,), (share,))
    picked = jnp.take(pool, index, axis=0).astype(F32)
    normed = (picked * lax.rsqrt(jnp.mean(picked * picked, axis=1, keepdims=True) + 1e-06)).astype(BF)

    def shift_tokens(x):
        shifted = [[(dev(m, c, s), dev(m, c, (s + k) % shards)) for m, c, s in devices] for k in range(shards)]
        return jnp.stack([move(x, pairs) for pairs in shifted])

    w_flat = flat(weights)
    steps = max(rows // 64, 1)
    lines = w_flat.shape[0] // steps
    *prepared, slices = pl.pallas_call(
        functools.partial(prep_kernel, shards),
        grid=(steps,),
        out_shape=[jax.ShapeDtypeStruct((2, rows, part), BF)] * shards
        + [jax.ShapeDtypeStruct((particles, 2, rows, cols), BF)],
        in_specs=[smem_spec(), pl.BlockSpec((lines, LANES), lambda i: (i, 0))],
        out_specs=[pl.BlockSpec((2, rows // steps, part), lambda i: (0, i, 0))] * shards
        + [pl.BlockSpec((particles, 2, rows // steps, cols), lambda i: (0, 0, i, 0))],
        compiler_params=params(56),
        name="prep",
    )(ids, w_flat)

    w_routes = []
    for r in range(shards):
        pairs = []
        for m, c, s in devices:
            q = (s - r) % shards
            pairs.append((dev(m, c, s), dev(m, q % 2, c * half + q // 2)))
        w_routes.append(pairs)

    whole = lax.all_to_all(slices, "particle", 0, 0, tiled=True)

    pair_list = [(i, j) for i in range(particles) for j in range(i)]
    hops = []
    for count, stride in ((particles, shards), (shards, 1)):
        hop = 1
        while hop < count:
            hops.append([(d, d + ((d // stride % count ^ hop) - d // stride % count) * stride) for d in range(len(devices))])
            hop *= 2

    def pair_sums(whole):
        return pl.pallas_call(
            distance_kernel,
            out_shape=jax.ShapeDtypeStruct((8, LANES), F32),
            in_specs=[pl.BlockSpec(memory_space=pltpu.VMEM)],
            out_specs=pl.BlockSpec(memory_space=pltpu.VMEM),
            compiler_params=params(8),
                name="distances",
        )(whole)

    def add_over(sums, steps):
        for step in steps:
            sums = sums + move(sums, hops[step])
        return sums

    def gather_row(ids, which, turn):
        k = lax.rem(ids[SHARD] - which + shards, shards)
        return (turn * (particles // 2) * shards + k) * share

    def place(ids, ref, held, sem, which, turn, start=0):
        row = gather_row(ids, which, turn)
        for i in range(particles // 2):
            to = pl.multiple_of(row + i * shards * share, share)
            pltpu.make_async_copy(
                ref.at[pl.ds(start + i * share, share), :], held.at[pl.ds(to, share), :], sem
            ).start()

    if shards == 4:
        cot = cotangent[0]
        inner = jnp.logical_or(shard == 1, shard == 2)
        flip = jnp.where(jnp.logical_or(inner, core == proc), 0, 1)
        first_routes, second_routes = [], []
        for e in range(2):
            one, two = [], []
            for m, c, s in devices:
                at_home, is_inner = c == s // half, s in (1, 2)
                if not at_home:
                    to, turn = (3 - s, e) if is_inner else (1 if s == 3 else 2, 1 - e)
                    one.append((dev(m, c, s), dev(m, c ^ turn, to)))
                elif is_inner:
                    one.append((dev(m, c, s), dev(m, c ^ e, s ^ 1)))
                else:
                    two.append((dev(m, c, s), dev(m, c ^ e, s ^ 1)))
                if is_inner:
                    two.append((dev(m, c, s), dev(m, c, s ^ 1)))
            first_routes.append(one)
            second_routes.append(two)
        halves = [
            lax.dynamic_slice(cot, (((core + e + flip) % 2) * half_rows, 0), (half_rows, width)) for e in range(2)
        ]
        alpha = [move(x, route) for x, route in zip(halves, first_routes)]
        own_c = move(cot, [(dev(m, c, s), dev(m, 1 - c, s)) for m, c, s in devices if c == s // half])
        normed = shift_tokens(normed)
        alpha, own_c, prepared, normed = lax.optimization_barrier((alpha, own_c, prepared, normed))
        normed = lax.all_gather(normed[None], "particle", axis=0, tiled=True)
        w_pieces = [move(x, route) for x, route in zip(prepared, w_routes)]
        hand_on = [jnp.where(inner, a, x) for a, x in zip(alpha, halves)]
        alpha_x = [move(x, swap_of(everyone)) for x in alpha]
        beta = [move(hand_on[0], second_routes[0])]
        hand_on[1], whole, *w_pieces[:2] = lax.optimization_barrier((hand_on[1], whole, *w_pieces[:2]))
        beta.append(move(hand_on[1], second_routes[1]))
        sums = add_over(pair_sums(whole), range(len(hops) - 3))
        w_pieces, normed, sums = lax.optimization_barrier((w_pieces, normed, sums))
        beta_x = [move(x, swap_of(everyone)) for x in beta]
        sources = [cot, own_c, *alpha, *alpha_x, *beta, *beta_x]

        def pick(ids, refs, held, sem):
            s, core, proc = ids[SHARD], ids[CORE], ids[PROC]
            low = s < 2
            near, far, pair = jnp.where(low, 2, 1), jnp.where(low, 3, 0), s + 1 - 2 * lax.rem(s, 2)
            side = lax.rem(core + proc, 2)
            is_inner = jnp.logical_or(s == 1, s == 2)

            def own(ref):
                for turn in range(2):
                    place(ids, ref, held, sem, s, turn, turn * half_rows)

            def others(main, main_x, rest, rest_x):
                for e in range(2):
                    same = side == e
                    place(ids, main[e], held, sem, jnp.where(same, near, far), core)
                    place(ids, main_x[e], held, sem, jnp.where(same, far, near), 1 - core)

                    @pl.when(same)
                    def _():
                        place(ids, rest[e], held, sem, pair, core)
                        place(ids, rest_x[1 - e], held, sem, pair, 1 - core)

            @pl.when(side == 0)
            def _():
                own(refs[0])

            @pl.when(side == 1)
            def _():
                own(refs[1])

            @pl.when(is_inner)
            def _():
                others(refs[2:4], refs[4:6], refs[6:8], refs[8:10])

            @pl.when(jnp.logical_not(is_inner))
            def _():
                others(refs[6:8], refs[8:10], refs[2:4], refs[4:6])
    else:
        full = lax.all_gather(cotangent[0], "shard", axis=0, tiled=True)
        sources = [jnp.where(core == proc, full, move(full, swap_of(everyone)))]
        w_pieces = [move(x, route) for x, route in zip(prepared, w_routes)]
        normed = lax.all_gather(shift_tokens(normed)[None], "particle", axis=0, tiled=True)
        sums = add_over(pair_sums(whole), range(len(hops) - 3))

        def pick(ids, refs, held, sem):
            def one(which, carry):
                for turn in range(2):
                    start = pl.multiple_of(which * tok_rows + turn * half_rows, half_rows)
                    place(ids, refs[0], held, sem, which, turn, start)
                return carry

            lax.fori_loop(0, shards, one, 0)

    normed = normed.reshape(tokens, width)
    act_t, slope_t, down_t = pl.pallas_call(
        functools.partial(up_kernel, shards, width ** (-0.5)),
        grid=(blocks,),
        out_shape=[
            jax.ShapeDtypeStruct((part, tokens), BF),
            jax.ShapeDtypeStruct((part, tokens), BF),
            jax.ShapeDtypeStruct((part, width), BF),
        ],
        in_specs=[smem_spec(), pl.BlockSpec((BLOCK, width), lambda i: (i, 0))]
        + [pl.BlockSpec((2, rows, part), lambda i: (0, 0, 0))] * shards,
        out_specs=[
            pl.BlockSpec((part, BLOCK), lambda i: (0, i)),
            pl.BlockSpec((part, BLOCK), lambda i: (0, i)),
            pl.BlockSpec((part, width), lambda i: (0, 0)),
        ],
        scratch_shapes=[pltpu.VMEM((width, part), BF), pltpu.VMEM((width, part), BF), pltpu.VMEM((part, width), BF)],
        compiler_params=params(56),
        name="up",
    )(ids, normed, *w_pieces)

    sums = add_over(sums, [-3])
    sums, act_t, slope_t = lax.optimization_barrier((sums, act_t, slope_t))
    grad_scale = 1.0 / (tokens * width)
    scores = pl.pallas_call(
        functools.partial(
            grad_kernel,
            shards,
            particles,
            -(width ** (-0.5)) * grad_scale,
            -(hidden ** (-0.5)) * grad_scale,
            hidden ** (-0.5),
            pick,
        ),
        out_shape=[jax.ShapeDtypeStruct((2, rows, cols), BF)] * particles,
        in_specs=[smem_spec()] + [any_spec()] * (4 + len(sources)),
        out_specs=[any_spec()] * particles,
        scratch_shapes=[
            pltpu.VMEM((tokens, width), BF),
            pltpu.VMEM((tokens, width), BF),
            pltpu.VMEM((part, tokens), BF),
            pltpu.VMEM((part, tokens), BF),
            pltpu.VMEM((part, tokens), BF),
            pltpu.VMEM((part, width), BF),
            pltpu.VMEM((2, width, part), BF),
            pltpu.SemaphoreType.DMA((particles + 5,)),
        ],
        compiler_params=params(56),
        name="grads",
    )(ids, normed, act_t, slope_t, down_t, *sources)

    sums = add_over(sums, [-2])
    sums, *scores = lax.optimization_barrier((sums, *scores))

    ratio = particles // shards
    arrived = []
    for t in range(particles):
        pairs = []
        for m, c, s in devices:
            mine, q = 2 * m + s // half, 2 * (s % half) + c
            u = (mine + ratio * q - t) % particles
            z, e = u // ratio, q * ratio + u % ratio
            pairs.append((dev(m, c, s), dev(e // 2 + z, e % 2, z)))
        arrived.append(move(scores[t], pairs))

    rest = move(sums, hops[-1])
    sums, rest, *arrived[:4] = lax.optimization_barrier((sums, rest, *arrived[:4]))
    sums = sums + rest
    sums = sums[0]
    lookup = [
        [pair_list.index((max(i, j), min(i, j))) if i != j else len(pair_list) for j in range(particles)]
        for i in range(particles)
    ]
    table = jnp.concatenate([sums[: len(pair_list)], jnp.zeros((1,), F32)])
    distances = table[jnp.array(lookup, jnp.int32)]
    inverse_band = 1.0 / kernel_scale[0].astype(F32)
    repulse = 2.0 * inverse_band
    kernel = jnp.exp(-distances * inverse_band)
    scale = 2 * width * hidden / particles
    coef = jnp.concatenate(
        [(scale * kernel).reshape(-1), scale * repulse * jnp.sum(kernel, axis=1), repulse[None]]
    )

    fields = pl.pallas_call(
        functools.partial(stein_kernel, shards, particles),
        out_shape=[jax.ShapeDtypeStruct((2, rows, cols), BF)] * particles,
        in_specs=[smem_spec(), smem_spec(), pl.BlockSpec(memory_space=pltpu.VMEM)] + [any_spec()] * particles,
        out_specs=[any_spec()] * particles,
        scratch_shapes=[
            pltpu.VMEM((particles, 2, rows, cols), BF),
            pltpu.VMEM((particles, 2, rows, cols), BF),
            pltpu.VMEM((particles, min(rows, 64), LANES), F32),
            pltpu.SemaphoreType.DMA((particles,)),
        ],
        compiler_params=params(12),
        name="stein",
    )(ids, coef, whole, *arrived)

    back = []
    for k in range(columns):
        for x in range(2):
            pairs = [(dev(m, c, s), dev(m + k, c ^ x, s)) for m, c, s in devices]
            back.append(move(fields[2 * k + x], pairs))

    steps = max(rows // 32, 1)
    flat_rows = rows * 2 * lane_tiles
    state_spec = pl.BlockSpec((flat_rows // steps, LANES), lambda i: (i, 0))
    outs = pl.pallas_call(
        functools.partial(adam_kernel, particles),
        grid=(steps,),
        out_shape=[jax.ShapeDtypeStruct((flat_rows, LANES), F32)] * 4,
        in_specs=[smem_spec()] + [state_spec] * 3 + [any_spec()] * particles,
        out_specs=[state_spec] * 4,
        scratch_shapes=[pltpu.VMEM((2, rows, hidden), BF), pltpu.SemaphoreType.DMA((particles,))],
        compiler_params=params(56),
        name="adam",
    )(ids, w_flat, flat(first_moment), flat(second_moment), *back)
    return tuple(unflat(x) for x in outs)


def solution(mesh):
    state = P("particle", "shard", None, None)
    return jax.shard_map(
        local,
        mesh=mesh,
        in_specs=(P("shard", None), P("shard"), P(), P("particle", "shard", None), state, state, state),
        out_specs=(state, state, state, state),
        check_vma=False,
    )
```

```python
import functools

import jax
import jax.numpy as jnp
from jax import lax
from jax.experimental import pallas as pl
from jax.experimental.pallas import tpu as pltpu
from jax.sharding import PartitionSpec as P

BF = jnp.bfloat16
F32 = jnp.float32
AXES = ("particle", "shard")
LANES = 128
BLOCK = 256
MIB = 1024 * 1024
NT = (((1,), (1,)), ((), ()))

COL, CORE, SHARD, PROC, PIECE = range(5)


def any_spec():
    return pl.BlockSpec(memory_space=pl.ANY)


def smem_spec():
    return pl.BlockSpec(memory_space=pltpu.SMEM)


def params(mib):
    return pltpu.CompilerParams(vmem_limit_bytes=mib * MIB)


def run_copies(copies):
    for copy in copies:
        copy.start()
    for copy in copies:
        copy.wait()


def slice_index(ids, column, core, shard, columns):
    return 2 * lax.rem(column - shard + columns * 16, columns) + core


def prep_kernel(shards, ids, w, *out):
    pieces, slices = out[:-1], out[-1]
    rows, piece = pieces[0].shape
    particles, _, _, cols = slices.shape
    columns = particles // 2
    tiles, per_slice = piece // LANES, cols // LANES
    for r in range(shards):
        q = lax.rem(ids[SHARD] - r + shards, shards)
        for j in range(tiles):
            e = q * (tiles // per_slice) + j // per_slice
            column = lax.rem(lax.div(e, 2) + ids[SHARD], columns)
            p = 2 * column + lax.rem(e, 2)
            at, within = j * LANES, j % per_slice * LANES
            for kind in range(2):
                line = 2 * (q * tiles + j) + kind
                part = w[pl.ds(line, rows, stride=2 * shards * tiles), :].astype(BF)
                pieces[kind * shards + r][:, at : at + LANES] = part
                slices[p, kind, :, within : within + LANES] = part


def transpose_pieces(shards, ids, pieces, straight, turned):
    width = straight.shape[0]
    rows = width // shards
    for r in range(shards):
        at = pl.multiple_of(lax.rem(ids[PIECE] + r, shards) * rows, rows)
        straight[pl.ds(at, rows), :] = pieces[r][...]
    for i in range(width // LANES):
        span = slice(i * LANES, (i + 1) * LANES)
        turned[:, span] = straight[span, :].astype(F32).T.astype(BF)


def up_kernel(shards, scale, ids, tokens, *refs):
    pieces = refs[:shards]
    act_t, slope_t, up_w, up_t = refs[shards:]

    @pl.when(pl.program_id(0) == 0)
    def _():
        transpose_pieces(shards, ids, pieces, up_w, up_t)

    u = lax.dot_general(up_t[...], tokens[...], NT, preferred_element_type=F32) * scale
    cdf = 0.5 * (1.0 + lax.erf(u * 0.7071067811865476))
    density = jnp.exp(-0.5 * u * u) * 0.3989422804014327
    act_t[...] = (u * cdf).astype(BF)
    slope_t[...] = (cdf + u * density).astype(BF)


def grad_kernel(shards, particles, up_scale, down_scale, back_scale, pick, ids, normed, act_t, slope_t, *refs):
    n_in = len(refs) - particles - 9
    pieces, sources, out = refs[:shards], refs[shards:n_in], refs[n_in : n_in + particles]
    c, n, act, slope, grad, down_w, down, score, sems = refs[n_in + particles :]
    part, tokens = act.shape
    width = c.shape[1]
    chunk = tokens // shards
    first = [pltpu.make_async_copy(slope_t, slope, sems.at[1])]
    later = [
        pltpu.make_async_copy(act_t, act, sems.at[3]),
        pltpu.make_async_copy(normed, n, sems.at[4]),
    ]
    for copy in first:
        copy.start()
    pick(ids, sources, c, sems.at[0])
    for copy in later:
        copy.start()
    transpose_pieces(shards, ids, pieces, down_w, down)
    for copy in first:
        copy.wait()
    pltpu.make_async_copy(c, c, sems.at[0]).wait()

    def back(i, carry):
        at = pl.multiple_of(i * chunk, chunk)
        b = lax.dot_general(down[...], c[pl.ds(at, chunk), :], NT, preferred_element_type=F32)
        grad[:, pl.ds(at, chunk)] = (b * (slope[:, pl.ds(at, chunk)].astype(F32) * back_scale)).astype(BF)
        return carry

    lax.fori_loop(0, shards, back, 0)
    for copy in later:
        copy.wait()

    def gradient(j, carry):
        at = pl.multiple_of(j * BLOCK, BLOCK)
        g = jnp.dot(grad[...], n[:, pl.ds(at, BLOCK)], preferred_element_type=F32)
        score[0, pl.ds(at, BLOCK), :] = (g * up_scale).T.astype(BF)
        g = jnp.dot(act[...], c[:, pl.ds(at, BLOCK)], preferred_element_type=F32)
        score[1, pl.ds(at, BLOCK), :] = (g * down_scale).T.astype(BF)
        return carry

    lax.fori_loop(0, width // BLOCK, gradient, 0)
    rows = width // shards
    ratio = particles // shards
    cols = part // ratio
    mine = 2 * ids[COL] + ids[PROC]
    copies = []
    for t in range(particles):
        u = lax.rem(mine + ratio * ids[PIECE] - t + particles, particles)
        row = pl.multiple_of(lax.div(u, ratio) * rows, rows)
        col = pl.multiple_of(lax.rem(u, ratio) * cols, cols)
        copies.append(pltpu.make_async_copy(score.at[:, pl.ds(row, rows), pl.ds(col, cols)], out[t], sems.at[t]))
    run_copies(copies)


def distance_kernel(whole, out):
    particles, _, rows, cols = whole.shape
    pairs = [(i, j) for i in range(particles) for j in range(i)]
    tiles = cols // LANES

    def body(g, acc):
        kind = lax.div(g, rows // 16)
        row = pl.multiple_of(lax.rem(g, rows // 16) * 16, 16)
        for tile in range(tiles):
            w = [whole[p, kind, pl.ds(row, 16), tile * LANES : (tile + 1) * LANES].astype(F32) for p in range(particles)]
            new = []
            for a, (i, j) in zip(acc, pairs):
                d = w[i] - w[j]
                d = d * d
                new.append(a + (d[:8] + d[8:]))
            acc = tuple(new)
        return acc

    acc = lax.fori_loop(0, 2 * rows // 16, body, tuple(jnp.zeros((8, LANES), F32) for _ in pairs))
    lane = lax.broadcasted_iota(jnp.int32, (8, LANES), 1)
    row = jnp.zeros((8, LANES), F32)
    for i, a in enumerate(acc):
        total = jnp.sum(jnp.sum(a, axis=0, keepdims=True), axis=1, keepdims=True)
        row = row + jnp.where(lane == i, total, 0.0)
    out[...] = row


def stein_kernel(shards, particles, ids, coef, whole, *refs):
    sources, out = refs[:particles], refs[particles : 2 * particles]
    scores, field, pushed, sems = refs[2 * particles :]
    columns = particles // 2
    ratio = particles // shards
    _, _, rows, cols = whole.shape
    e = slice_index(ids, ids[COL], ids[CORE], ids[SHARD], columns)
    u = ids[SHARD] * ratio + lax.rem(e, ratio) + particles * shards - ratio * lax.div(e, ratio)
    run_copies(
        [pltpu.make_async_copy(sources[t], scores.at[lax.rem(u + t, particles)], sems.at[t]) for t in range(particles)]
    )
    repulse = coef[particles * particles + particles]
    chunk = min(rows, 64)
    groups = rows // chunk
    tiles = cols // LANES

    def body(g, carry):
        kind = lax.div(g, groups)
        row = pl.multiple_of(lax.rem(g, groups) * chunk, chunk)
        for tile in range(tiles):
            at = (kind, pl.ds(row, chunk), slice(tile * LANES, (tile + 1) * LANES))
            for p in range(particles):
                pushed[p] = scores[(p,) + at].astype(F32) - repulse * whole[(p,) + at].astype(F32)
            for i in range(particles):
                total = coef[particles * particles + i] * whole[(i,) + at].astype(F32)
                for j in range(particles):
                    total = total + coef[i * particles + j] * pushed[j]
                field[(i,) + at] = total.astype(BF)
        return carry

    lax.fori_loop(0, 2 * groups, body, 0)
    copies = []
    for k in range(columns):
        for x in range(2):
            column = lax.rem(ids[COL] + k, columns)
            core = ids[CORE] if x == 0 else 1 - ids[CORE]
            i = 2 * k + x
            copies.append(pltpu.make_async_copy(field.at[2 * column + core], out[i], sems.at[i]))
    run_copies(copies)


def adam_kernel(particles, ids, w, first, second, *refs):
    sources = refs[:particles]
    new_w, new_first, new_second, transport, field, sems = refs[particles:]
    columns = particles // 2
    _, _, hidden = field.shape
    width = hidden // particles
    step = pl.program_id(0)

    @pl.when(step == 0)
    def _():
        copies = []
        for k in range(columns):
            for x in range(2):
                column = lax.rem(ids[COL] - k + columns, columns)
                core = ids[CORE] if x == 0 else 1 - ids[CORE]
                at = pl.multiple_of(slice_index(ids, column, core, ids[SHARD], columns) * width, width)
                i = 2 * k + x
                copies.append(pltpu.make_async_copy(sources[i], field.at[:, :, pl.ds(at, width)], sems.at[i]))
        run_copies(copies)

    lane_tiles = hidden // LANES
    rows = w.shape[0] // (2 * lane_tiles)
    base = pl.multiple_of(step * rows, rows)
    for kind in range(2):
        for tile in range(lane_tiles):
            part = field[kind, pl.ds(base, rows), tile * LANES : (tile + 1) * LANES]
            transport[pl.ds(2 * tile + kind, rows, stride=2 * lane_tiles), :] = part.astype(F32)
    t = transport[...]
    m = 0.9 * first[...] - 0.1 * t
    v = 0.999 * second[...] + 0.001 * t * t
    new_first[...] = m
    new_second[...] = v
    new_w[...] = w[...] - 0.01 * m / (jnp.sqrt(v) + 1e-08)


def local(pool, batch_index, kernel_scale, cotangent, weights, first_moment, second_moment):
    shards = lax.axis_size("shard")
    particles = lax.axis_size("particle")
    columns, half = particles // 2, shards // 2
    tok_rows = batch_index.shape[0]
    width = pool.shape[1]
    _, rows, _, hidden = weights.shape
    part, cols = hidden // shards, hidden // particles
    tokens = tok_rows * shards
    blocks = tokens // BLOCK
    lane_tiles = hidden // LANES

    own = lax.axis_index("particle")
    shard = lax.axis_index("shard")
    core, column = own % 2, own // 2
    proc = shard // half
    piece = 2 * (shard % half) + core
    ids = jnp.stack([column, core, shard, proc, piece]).astype(jnp.int32)
    devices = [(m, c, s) for m in range(columns) for c in range(2) for s in range(shards)]

    def dev(m, c, s):
        return (2 * (m % columns) + c) * shards + s

    def move(x, pairs):
        if all(a == b for a, b in pairs) and len(pairs) == len(devices):
            return x
        return lax.ppermute(x, AXES, pairs)

    def swap_of(among):
        return [(dev(m, c, s), dev(m, 1 - c, s)) for m, c, s in devices if s in among]

    def flat(x):
        return x[0].reshape(rows, 2, lane_tiles, LANES).transpose(0, 2, 1, 3).reshape(-1, LANES)

    def unflat(x):
        return x.reshape(rows, lane_tiles, 2, LANES).transpose(0, 2, 1, 3).reshape(1, rows, 2, hidden)

    everyone = range(shards)
    half_rows = tok_rows // 2
    share = tok_rows // particles
    index = lax.dynamic_slice(batch_index, (own * share,), (share,))
    picked = jnp.take(pool, index, axis=0).astype(F32)
    normed = (picked * lax.rsqrt(jnp.mean(picked * picked, axis=1, keepdims=True) + 1e-06)).astype(BF)

    def shift_tokens(x):
        shifted = [[(dev(m, c, s), dev(m, c, (s + k) % shards)) for m, c, s in devices] for k in range(shards)]
        return jnp.stack([move(x, pairs) for pairs in shifted])

    w_flat = flat(weights)
    steps = max(rows // 64, 1)
    lines = w_flat.shape[0] // steps
    *prepared, slices = pl.pallas_call(
        functools.partial(prep_kernel, shards),
        grid=(steps,),
        out_shape=[jax.ShapeDtypeStruct((rows, part), BF)] * (2 * shards)
        + [jax.ShapeDtypeStruct((particles, 2, rows, cols), BF)],
        in_specs=[smem_spec(), pl.BlockSpec((lines, LANES), lambda i: (i, 0))],
        out_specs=[pl.BlockSpec((rows // steps, part), lambda i: (i, 0))] * (2 * shards)
        + [pl.BlockSpec((particles, 2, rows // steps, cols), lambda i: (0, 0, i, 0))],
        compiler_params=params(56),
        name="prep",
    )(ids, w_flat)

    w_routes = []
    for r in range(shards):
        pairs = []
        for m, c, s in devices:
            q = (s - r) % shards
            pairs.append((dev(m, c, s), dev(m, q % 2, c * half + q // 2)))
        w_routes.append(pairs)

    whole = lax.all_to_all(slices, "particle", 0, 0, tiled=True)

    pair_list = [(i, j) for i in range(particles) for j in range(i)]
    hops = []
    for count, stride in ((particles, shards), (shards, 1)):
        hop = 1
        while hop < count:
            hops.append([(d, d + ((d // stride % count ^ hop) - d // stride % count) * stride) for d in range(len(devices))])
            hop *= 2

    def pair_sums(whole):
        return pl.pallas_call(
            distance_kernel,
            out_shape=jax.ShapeDtypeStruct((8, LANES), F32),
            in_specs=[pl.BlockSpec(memory_space=pltpu.VMEM)],
            out_specs=pl.BlockSpec(memory_space=pltpu.VMEM),
            compiler_params=params(8),
                name="distances",
        )(whole)

    def add_over(sums, steps):
        for step in steps:
            sums = sums + move(sums, hops[step])
        return sums

    def gather_row(ids, which, turn):
        k = lax.rem(ids[SHARD] - which + shards, shards)
        return (turn * (particles // 2) * shards + k) * share

    def place(ids, ref, held, sem, which, turn, start=0):
        row = gather_row(ids, which, turn)
        for i in range(particles // 2):
            to = pl.multiple_of(row + i * shards * share, share)
            pltpu.make_async_copy(
                ref.at[pl.ds(start + i * share, share), :], held.at[pl.ds(to, share), :], sem
            ).start()

    if shards == 4:
        cot = cotangent[0]
        inner = jnp.logical_or(shard == 1, shard == 2)
        flip = jnp.where(jnp.logical_or(inner, core == proc), 0, 1)
        first_routes, second_routes = [], []
        for e in range(2):
            one, two = [], []
            for m, c, s in devices:
                at_home, is_inner = c == s // half, s in (1, 2)
                if not at_home:
                    to, turn = (3 - s, e) if is_inner else (1 if s == 3 else 2, 1 - e)
                    one.append((dev(m, c, s), dev(m, c ^ turn, to)))
                elif is_inner:
                    one.append((dev(m, c, s), dev(m, c ^ e, s ^ 1)))
                else:
                    two.append((dev(m, c, s), dev(m, c ^ e, s ^ 1)))
                if is_inner:
                    two.append((dev(m, c, s), dev(m, c, s ^ 1)))
            first_routes.append(one)
            second_routes.append(two)
        halves = [
            lax.dynamic_slice(cot, (((core + e + flip) % 2) * half_rows, 0), (half_rows, width)) for e in range(2)
        ]
        alpha = [move(x, route) for x, route in zip(halves, first_routes)]
        own_c = move(cot, [(dev(m, c, s), dev(m, 1 - c, s)) for m, c, s in devices if c == s // half])
        normed = shift_tokens(normed)
        alpha, own_c, prepared, normed = lax.optimization_barrier((alpha, own_c, prepared, normed))
        normed = lax.all_gather(normed[None], "particle", axis=0, tiled=True)
        w_pieces = [move(x, w_routes[i % shards]) for i, x in enumerate(prepared)]
        hand_on = [jnp.where(inner, a, x) for a, x in zip(alpha, halves)]
        alpha_x = [move(x, swap_of(everyone)) for x in alpha]
        beta = [move(hand_on[0], second_routes[0])]
        hand_on[1], *w_pieces[:2] = lax.optimization_barrier((hand_on[1], *w_pieces[:2]))
        beta.append(move(hand_on[1], second_routes[1]))
        w_pieces[:shards], normed = lax.optimization_barrier((w_pieces[:shards], normed))
        beta_x = [move(x, swap_of(everyone)) for x in beta]
        sources = [cot, own_c, *alpha, *alpha_x, *beta, *beta_x]

        def pick(ids, refs, held, sem):
            s, core, proc = ids[SHARD], ids[CORE], ids[PROC]
            low = s < 2
            near, far, pair = jnp.where(low, 2, 1), jnp.where(low, 3, 0), s + 1 - 2 * lax.rem(s, 2)
            side = lax.rem(core + proc, 2)
            is_inner = jnp.logical_or(s == 1, s == 2)

            def own(ref):
                for turn in range(2):
                    place(ids, ref, held, sem, s, turn, turn * half_rows)

            def others(main, main_x, rest, rest_x):
                for e in range(2):
                    same = side == e
                    place(ids, main[e], held, sem, jnp.where(same, near, far), core)
                    place(ids, main_x[e], held, sem, jnp.where(same, far, near), 1 - core)

                    @pl.when(same)
                    def _():
                        place(ids, rest[e], held, sem, pair, core)
                        place(ids, rest_x[1 - e], held, sem, pair, 1 - core)

            @pl.when(side == 0)
            def _():
                own(refs[0])

            @pl.when(side == 1)
            def _():
                own(refs[1])

            @pl.when(is_inner)
            def _():
                others(refs[2:4], refs[4:6], refs[6:8], refs[8:10])

            @pl.when(jnp.logical_not(is_inner))
            def _():
                others(refs[6:8], refs[8:10], refs[2:4], refs[4:6])
    else:
        full = lax.all_gather(cotangent[0], "shard", axis=0, tiled=True)
        sources = [jnp.where(core == proc, full, move(full, swap_of(everyone)))]
        w_pieces = [move(x, w_routes[i % shards]) for i, x in enumerate(prepared)]
        normed = lax.all_gather(shift_tokens(normed)[None], "particle", axis=0, tiled=True)

        def pick(ids, refs, held, sem):
            def one(which, carry):
                for turn in range(2):
                    start = pl.multiple_of(which * tok_rows + turn * half_rows, half_rows)
                    place(ids, refs[0], held, sem, which, turn, start)
                return carry

            lax.fori_loop(0, shards, one, 0)

    normed = normed.reshape(tokens, width)
    act_t, slope_t = pl.pallas_call(
        functools.partial(up_kernel, shards, width ** (-0.5)),
        grid=(blocks,),
        out_shape=[
            jax.ShapeDtypeStruct((part, tokens), BF),
            jax.ShapeDtypeStruct((part, tokens), BF),
        ],
        in_specs=[smem_spec(), pl.BlockSpec((BLOCK, width), lambda i: (i, 0))]
        + [pl.BlockSpec((rows, part), lambda i: (0, 0))] * shards,
        out_specs=[
            pl.BlockSpec((part, BLOCK), lambda i: (0, i)),
            pl.BlockSpec((part, BLOCK), lambda i: (0, i)),
        ],
        scratch_shapes=[pltpu.VMEM((width, part), BF), pltpu.VMEM((part, width), BF)],
        compiler_params=params(56),
        name="up",
    )(ids, normed, *w_pieces[:shards])

    whole, act_t = lax.optimization_barrier((whole, act_t))
    sums = add_over(pair_sums(whole), range(len(hops) - 3))
    sums, w_pieces[shards:] = lax.optimization_barrier((sums, w_pieces[shards:]))
    sums = add_over(sums, [-3])
    sums, slope_t = lax.optimization_barrier((sums, slope_t))
    grad_scale = 1.0 / (tokens * width)
    scores = pl.pallas_call(
        functools.partial(
            grad_kernel,
            shards,
            particles,
            -(width ** (-0.5)) * grad_scale,
            -(hidden ** (-0.5)) * grad_scale,
            hidden ** (-0.5),
            pick,
        ),
        out_shape=[jax.ShapeDtypeStruct((2, rows, cols), BF)] * particles,
        in_specs=[smem_spec()]
        + [any_spec()] * 3
        + [pl.BlockSpec(memory_space=pltpu.VMEM)] * shards
        + [any_spec()] * len(sources),
        out_specs=[any_spec()] * particles,
        scratch_shapes=[
            pltpu.VMEM((tokens, width), BF),
            pltpu.VMEM((tokens, width), BF),
            pltpu.VMEM((part, tokens), BF),
            pltpu.VMEM((part, tokens), BF),
            pltpu.VMEM((part, tokens), BF),
            pltpu.VMEM((width, part), BF),
            pltpu.VMEM((part, width), BF),
            pltpu.VMEM((2, width, part), BF),
            pltpu.SemaphoreType.DMA((particles + 5,)),
        ],
        compiler_params=params(56),
        name="grads",
    )(ids, normed, act_t, slope_t, *w_pieces[shards:], *sources)

    sums = add_over(sums, [-2])
    sums, *scores = lax.optimization_barrier((sums, *scores))

    ratio = particles // shards
    arrived = []
    for t in range(particles):
        pairs = []
        for m, c, s in devices:
            mine, q = 2 * m + s // half, 2 * (s % half) + c
            u = (mine + ratio * q - t) % particles
            z, e = u // ratio, q * ratio + u % ratio
            pairs.append((dev(m, c, s), dev(e // 2 + z, e % 2, z)))
        arrived.append(move(scores[t], pairs))

    rest = move(sums, hops[-1])
    sums, rest, *arrived[:4] = lax.optimization_barrier((sums, rest, *arrived[:4]))
    sums = sums + rest
    sums = sums[0]
    lookup = [
        [pair_list.index((max(i, j), min(i, j))) if i != j else len(pair_list) for j in range(particles)]
        for i in range(particles)
    ]
    table = jnp.concatenate([sums[: len(pair_list)], jnp.zeros((1,), F32)])
    distances = table[jnp.array(lookup, jnp.int32)]
    inverse_band = 1.0 / kernel_scale[0].astype(F32)
    repulse = 2.0 * inverse_band
    kernel = jnp.exp(-distances * inverse_band)
    scale = 2 * width * hidden / particles
    coef = jnp.concatenate(
        [(scale * kernel).reshape(-1), scale * repulse * jnp.sum(kernel, axis=1), repulse[None]]
    )

    fields = pl.pallas_call(
        functools.partial(stein_kernel, shards, particles),
        out_shape=[jax.ShapeDtypeStruct((2, rows, cols), BF)] * particles,
        in_specs=[smem_spec(), smem_spec(), pl.BlockSpec(memory_space=pltpu.VMEM)] + [any_spec()] * particles,
        out_specs=[any_spec()] * particles,
        scratch_shapes=[
            pltpu.VMEM((particles, 2, rows, cols), BF),
            pltpu.VMEM((particles, 2, rows, cols), BF),
            pltpu.VMEM((particles, min(rows, 64), LANES), F32),
            pltpu.SemaphoreType.DMA((particles,)),
        ],
        compiler_params=params(12),
        name="stein",
    )(ids, coef, whole, *arrived)

    back = []
    for k in range(columns):
        for x in range(2):
            pairs = [(dev(m, c, s), dev(m + k, c ^ x, s)) for m, c, s in devices]
            back.append(move(fields[2 * k + x], pairs))

    steps = max(rows // 32, 1)
    flat_rows = rows * 2 * lane_tiles
    state_spec = pl.BlockSpec((flat_rows // steps, LANES), lambda i: (i, 0))
    outs = pl.pallas_call(
        functools.partial(adam_kernel, particles),
        grid=(steps,),
        out_shape=[jax.ShapeDtypeStruct((flat_rows, LANES), F32)] * 4,
        in_specs=[smem_spec()] + [state_spec] * 3 + [any_spec()] * particles,
        out_specs=[state_spec] * 4,
        scratch_shapes=[pltpu.VMEM((2, rows, hidden), BF), pltpu.SemaphoreType.DMA((particles,))],
        compiler_params=params(56),
        name="adam",
    )(ids, w_flat, flat(first_moment), flat(second_moment), *back)
    return tuple(unflat(x) for x in outs)


def solution(mesh):
    state = P("particle", "shard", None, None)
    return jax.shard_map(
        local,
        mesh=mesh,
        in_specs=(P("shard", None), P("shard"), P(), P("particle", "shard", None), state, state, state),
        out_specs=(state, state, state, state),
        check_vma=False,
    )
```

```python
import functools

import jax
import jax.numpy as jnp
from jax import lax
from jax.experimental import pallas as pl
from jax.experimental.pallas import tpu as pltpu
from jax.sharding import PartitionSpec as P

BF = jnp.bfloat16
F32 = jnp.float32
AXES = ("particle", "shard")
LANES = 128
BLOCK = 256
MIB = 1024 * 1024
NT = (((1,), (1,)), ((), ()))

COL, CORE, SHARD, PROC, PIECE = range(5)


def any_spec():
    return pl.BlockSpec(memory_space=pl.ANY)


def smem_spec():
    return pl.BlockSpec(memory_space=pltpu.SMEM)


def params(mib):
    return pltpu.CompilerParams(vmem_limit_bytes=mib * MIB)


def run_copies(copies):
    for copy in copies:
        copy.start()
    for copy in copies:
        copy.wait()


def slice_index(ids, column, core, shard, columns):
    return 2 * lax.rem(column - shard + columns * 16, columns) + core


def prep_kernel(shards, ids, w, *out):
    pieces, slices = out[:shards], out[shards]
    _, rows, piece = pieces[0].shape
    particles, _, _, cols = slices.shape
    columns = particles // 2
    tiles, per_slice = piece // LANES, cols // LANES
    for r in range(shards):
        q = lax.rem(ids[SHARD] - r + shards, shards)
        for j in range(tiles):
            e = q * (tiles // per_slice) + j // per_slice
            column = lax.rem(lax.div(e, 2) + ids[SHARD], columns)
            p = 2 * column + lax.rem(e, 2)
            at, within = j * LANES, j % per_slice * LANES
            for kind in range(2):
                line = 2 * (q * tiles + j) + kind
                part = w[pl.ds(line, rows, stride=2 * shards * tiles), :].astype(BF)
                pieces[r][kind, :, at : at + LANES] = part
                slices[p, kind, :, within : within + LANES] = part


def up_kernel(shards, scale, ids, tokens, *refs):
    pieces = refs[:shards]
    act_t, slope_t, down_t, up_w, down_w, up_t = refs[shards:]
    width, part = up_w.shape
    rows = width // shards

    @pl.when(pl.program_id(0) == 0)
    def _():
        for r in range(shards):
            at = pl.multiple_of(lax.rem(ids[PIECE] + r, shards) * rows, rows)
            up_w[pl.ds(at, rows), :] = pieces[r][0]
            down_w[pl.ds(at, rows), :] = pieces[r][1]
        for i in range(width // LANES):
            span = slice(i * LANES, (i + 1) * LANES)
            up_t[:, span] = up_w[span, :].astype(F32).T.astype(BF)
            down_t[:, span] = down_w[span, :].astype(F32).T.astype(BF)

    u = lax.dot_general(up_t[...], tokens[...], NT, preferred_element_type=F32) * scale
    cdf = 0.5 * (1.0 + lax.erf(u * 0.7071067811865476))
    density = jnp.exp(-0.5 * u * u) * 0.3989422804014327
    act_t[...] = (u * cdf).astype(BF)
    slope_t[...] = (cdf + u * density).astype(BF)


def grad_kernel(shards, particles, up_scale, down_scale, back_scale, pick, ids, normed, act_t, slope_t, down_t, *refs):
    n_in = len(refs) - particles - 8
    sources, out = refs[:n_in], refs[n_in : n_in + particles]
    c, n, act, slope, grad, down, score, sems = refs[n_in + particles :]
    part, tokens = act.shape
    width = c.shape[1]
    chunk = tokens // shards
    first = [
        pltpu.make_async_copy(down_t, down, sems.at[1]),
        pltpu.make_async_copy(slope_t, slope, sems.at[2]),
    ]
    later = [
        pltpu.make_async_copy(act_t, act, sems.at[3]),
        pltpu.make_async_copy(normed, n, sems.at[4]),
    ]
    for copy in first:
        copy.start()
    pick(ids, sources, c, sems.at[0])
    for copy in later:
        copy.start()
    for copy in first:
        copy.wait()
    pltpu.make_async_copy(c, c, sems.at[0]).wait()

    def back(i, carry):
        at = pl.multiple_of(i * chunk, chunk)
        b = lax.dot_general(down[...], c[pl.ds(at, chunk), :], NT, preferred_element_type=F32)
        grad[:, pl.ds(at, chunk)] = (b * (slope[:, pl.ds(at, chunk)].astype(F32) * back_scale)).astype(BF)
        return carry

    lax.fori_loop(0, shards, back, 0)
    for copy in later:
        copy.wait()

    def gradient(j, carry):
        at = pl.multiple_of(j * BLOCK, BLOCK)
        g = jnp.dot(grad[...], n[:, pl.ds(at, BLOCK)], preferred_element_type=F32)
        score[0, pl.ds(at, BLOCK), :] = (g * up_scale).T.astype(BF)
        g = jnp.dot(act[...], c[:, pl.ds(at, BLOCK)], preferred_element_type=F32)
        score[1, pl.ds(at, BLOCK), :] = (g * down_scale).T.astype(BF)
        return carry

    lax.fori_loop(0, width // BLOCK, gradient, 0)
    rows = width // shards
    ratio = particles // shards
    cols = part // ratio
    mine = 2 * ids[COL] + ids[PROC]
    copies = []
    for t in range(particles):
        u = lax.rem(mine + ratio * ids[PIECE] - t + particles, particles)
        row = pl.multiple_of(lax.div(u, ratio) * rows, rows)
        col = pl.multiple_of(lax.rem(u, ratio) * cols, cols)
        copies.append(pltpu.make_async_copy(score.at[:, pl.ds(row, rows), pl.ds(col, cols)], out[t], sems.at[t]))
    run_copies(copies)


def distance_kernel(whole, out):
    particles, _, rows, cols = whole.shape
    pairs = [(i, j) for i in range(particles) for j in range(i)]
    tiles = cols // LANES

    def body(g, acc):
        kind = lax.div(g, rows // 16)
        row = pl.multiple_of(lax.rem(g, rows // 16) * 16, 16)
        for tile in range(tiles):
            w = [whole[p, kind, pl.ds(row, 16), tile * LANES : (tile + 1) * LANES].astype(F32) for p in range(particles)]
            new = []
            for a, (i, j) in zip(acc, pairs):
                d = w[i] - w[j]
                d = d * d
                new.append(a + (d[:8] + d[8:]))
            acc = tuple(new)
        return acc

    acc = lax.fori_loop(0, 2 * rows // 16, body, tuple(jnp.zeros((8, LANES), F32) for _ in pairs))
    lane = lax.broadcasted_iota(jnp.int32, (8, LANES), 1)
    row = jnp.zeros((8, LANES), F32)
    for i, a in enumerate(acc):
        total = jnp.sum(jnp.sum(a, axis=0, keepdims=True), axis=1, keepdims=True)
        row = row + jnp.where(lane == i, total, 0.0)
    out[...] = row


def stein_kernel(shards, particles, ids, coef, whole, *refs):
    sources, out = refs[:particles], refs[particles : 2 * particles]
    scores, field, pushed, sems = refs[2 * particles :]
    columns = particles // 2
    ratio = particles // shards
    _, _, rows, cols = whole.shape
    e = slice_index(ids, ids[COL], ids[CORE], ids[SHARD], columns)
    u = ids[SHARD] * ratio + lax.rem(e, ratio) + particles * shards - ratio * lax.div(e, ratio)
    run_copies(
        [pltpu.make_async_copy(sources[t], scores.at[lax.rem(u + t, particles)], sems.at[t]) for t in range(particles)]
    )
    repulse = coef[particles * particles + particles]
    chunk = min(rows, 64)
    groups = rows // chunk
    tiles = cols // LANES

    def body(g, carry):
        kind = lax.div(g, groups)
        row = pl.multiple_of(lax.rem(g, groups) * chunk, chunk)
        for tile in range(tiles):
            at = (kind, pl.ds(row, chunk), slice(tile * LANES, (tile + 1) * LANES))
            for p in range(particles):
                pushed[p] = scores[(p,) + at].astype(F32) - repulse * whole[(p,) + at].astype(F32)
            for i in range(particles):
                total = coef[particles * particles + i] * whole[(i,) + at].astype(F32)
                for j in range(particles):
                    total = total + coef[i * particles + j] * pushed[j]
                field[(i,) + at] = total.astype(BF)
        return carry

    lax.fori_loop(0, 2 * groups, body, 0)
    copies = []
    for k in range(columns):
        for x in range(2):
            column = lax.rem(ids[COL] + k, columns)
            core = ids[CORE] if x == 0 else 1 - ids[CORE]
            i = 2 * k + x
            copies.append(pltpu.make_async_copy(field.at[2 * column + core], out[i], sems.at[i]))
    run_copies(copies)


def adam_kernel(particles, ids, w, first, second, *refs):
    sources = refs[:particles]
    new_w, new_first, new_second, transport, field, sems = refs[particles:]
    columns = particles // 2
    _, _, hidden = field.shape
    width = hidden // particles
    step = pl.program_id(0)

    @pl.when(step == 0)
    def _():
        copies = []
        for k in range(columns):
            for x in range(2):
                column = lax.rem(ids[COL] - k + columns, columns)
                core = ids[CORE] if x == 0 else 1 - ids[CORE]
                at = pl.multiple_of(slice_index(ids, column, core, ids[SHARD], columns) * width, width)
                i = 2 * k + x
                copies.append(pltpu.make_async_copy(sources[i], field.at[:, :, pl.ds(at, width)], sems.at[i]))
        run_copies(copies)

    lane_tiles = hidden // LANES
    rows = w.shape[0] // (2 * lane_tiles)
    base = pl.multiple_of(step * rows, rows)
    for kind in range(2):
        for tile in range(lane_tiles):
            part = field[kind, pl.ds(base, rows), tile * LANES : (tile + 1) * LANES]
            transport[pl.ds(2 * tile + kind, rows, stride=2 * lane_tiles), :] = part.astype(F32)
    t = transport[...]
    m = first[...] - 0.1 * t
    v = second[...] + 0.001 * t * t
    new_first[...] = m
    new_second[...] = v
    new_w[...] = w[...] - 0.01 * m / (jnp.sqrt(v) + 1e-08)


def local(pool, batch_index, kernel_scale, cotangent, weights, first_moment, second_moment):
    shards = lax.axis_size("shard")
    particles = lax.axis_size("particle")
    columns, half = particles // 2, shards // 2
    tok_rows = batch_index.shape[0]
    width = pool.shape[1]
    _, rows, _, hidden = weights.shape
    part, cols = hidden // shards, hidden // particles
    tokens = tok_rows * shards
    blocks = tokens // BLOCK
    lane_tiles = hidden // LANES

    own = lax.axis_index("particle")
    shard = lax.axis_index("shard")
    core, column = own % 2, own // 2
    proc = shard // half
    piece = 2 * (shard % half) + core
    ids = jnp.stack([column, core, shard, proc, piece]).astype(jnp.int32)
    devices = [(m, c, s) for m in range(columns) for c in range(2) for s in range(shards)]

    def dev(m, c, s):
        return (2 * (m % columns) + c) * shards + s

    def move(x, pairs):
        if all(a == b for a, b in pairs) and len(pairs) == len(devices):
            return x
        return lax.ppermute(x, AXES, pairs)

    def swap_of(among):
        return [(dev(m, c, s), dev(m, 1 - c, s)) for m, c, s in devices if s in among]

    def flat(x):
        return x[0].reshape(rows, 2, lane_tiles, LANES).transpose(0, 2, 1, 3).reshape(-1, LANES)

    def unflat(x):
        return x.reshape(rows, lane_tiles, 2, LANES).transpose(0, 2, 1, 3).reshape(1, rows, 2, hidden)

    everyone = range(shards)
    half_rows = tok_rows // 2
    share = tok_rows // particles
    index = lax.dynamic_slice(batch_index, (own * share,), (share,))
    picked = jnp.take(pool, index, axis=0).astype(F32)
    normed = (picked * lax.rsqrt(jnp.mean(picked * picked, axis=1, keepdims=True) + 1e-06)).astype(BF)

    def shift_tokens(x):
        shifted = [[(dev(m, c, s), dev(m, c, (s + k) % shards)) for m, c, s in devices] for k in range(shards)]
        return jnp.stack([move(x, pairs) for pairs in shifted])

    w_flat = flat(weights)
    steps = max(rows // 64, 1)
    lines = w_flat.shape[0] // steps
    *prepared, slices = pl.pallas_call(
        functools.partial(prep_kernel, shards),
        grid=(steps,),
        out_shape=[jax.ShapeDtypeStruct((2, rows, part), BF)] * shards
        + [jax.ShapeDtypeStruct((particles, 2, rows, cols), BF)],
        in_specs=[smem_spec(), pl.BlockSpec((lines, LANES), lambda i: (i, 0))],
        out_specs=[pl.BlockSpec((2, rows // steps, part), lambda i: (0, i, 0))] * shards
        + [pl.BlockSpec((particles, 2, rows // steps, cols), lambda i: (0, 0, i, 0))],
        compiler_params=params(56),
        name="prep",
    )(ids, w_flat)

    w_routes = []
    for r in range(shards):
        pairs = []
        for m, c, s in devices:
            q = (s - r) % shards
            pairs.append((dev(m, c, s), dev(m, q % 2, c * half + q // 2)))
        w_routes.append(pairs)

    whole = lax.all_to_all(slices, "particle", 0, 0, tiled=True)

    pair_list = [(i, j) for i in range(particles) for j in range(i)]
    hops = []
    for count, stride in ((particles, shards), (shards, 1)):
        hop = 1
        while hop < count:
            hops.append([(d, d + ((d // stride % count ^ hop) - d // stride % count) * stride) for d in range(len(devices))])
            hop *= 2

    def pair_sums(whole):
        return pl.pallas_call(
            distance_kernel,
            out_shape=jax.ShapeDtypeStruct((8, LANES), F32),
            in_specs=[pl.BlockSpec(memory_space=pltpu.VMEM)],
            out_specs=pl.BlockSpec(memory_space=pltpu.VMEM),
            compiler_params=params(8),
                name="distances",
        )(whole)

    def add_over(sums, steps):
        for step in steps:
            sums = sums + move(sums, hops[step])
        return sums

    def gather_row(ids, which, turn):
        k = lax.rem(ids[SHARD] - which + shards, shards)
        return (turn * (particles // 2) * shards + k) * share

    def place(ids, ref, held, sem, which, turn, start=0):
        row = gather_row(ids, which, turn)
        for i in range(particles // 2):
            to = pl.multiple_of(row + i * shards * share, share)
            pltpu.make_async_copy(
                ref.at[pl.ds(start + i * share, share), :], held.at[pl.ds(to, share), :], sem
            ).start()

    if shards == 4:
        cot = cotangent[0]
        inner = jnp.logical_or(shard == 1, shard == 2)
        flip = jnp.where(jnp.logical_or(inner, core == proc), 0, 1)
        first_routes, second_routes = [], []
        for e in range(2):
            one, two = [], []
            for m, c, s in devices:
                at_home, is_inner = c == s // half, s in (1, 2)
                if not at_home:
                    to, turn = (3 - s, e) if is_inner else (1 if s == 3 else 2, 1 - e)
                    one.append((dev(m, c, s), dev(m, c ^ turn, to)))
                elif is_inner:
                    one.append((dev(m, c, s), dev(m, c ^ e, s ^ 1)))
                else:
                    two.append((dev(m, c, s), dev(m, c ^ e, s ^ 1)))
                if is_inner:
                    two.append((dev(m, c, s), dev(m, c, s ^ 1)))
            first_routes.append(one)
            second_routes.append(two)
        halves = [
            lax.dynamic_slice(cot, (((core + e + flip) % 2) * half_rows, 0), (half_rows, width)) for e in range(2)
        ]
        alpha = [move(x, route) for x, route in zip(halves, first_routes)]
        own_c = move(cot, [(dev(m, c, s), dev(m, 1 - c, s)) for m, c, s in devices if c == s // half])
        normed = shift_tokens(normed)
        alpha, own_c, prepared, normed = lax.optimization_barrier((alpha, own_c, prepared, normed))
        normed = lax.all_gather(normed[None], "particle", axis=0, tiled=True)
        w_pieces = [move(x, route) for x, route in zip(prepared, w_routes)]
        beta = [move(jnp.where(inner, a, x), route) for a, x, route in zip(alpha, halves, second_routes)]
        alpha_x = [move(x, swap_of(everyone)) for x in alpha]
        whole, *w_pieces[:3] = lax.optimization_barrier((whole, *w_pieces[:3]))
        sums = add_over(pair_sums(whole), range(len(hops) - 2))
        w_pieces, normed, sums = lax.optimization_barrier((w_pieces, normed, sums))
        beta_x = [move(x, swap_of(everyone)) for x in beta]
        sources = [cot, own_c, *alpha, *alpha_x, *beta, *beta_x]

        def pick(ids, refs, held, sem):
            s, core, proc = ids[SHARD], ids[CORE], ids[PROC]
            low = s < 2
            near, far, pair = jnp.where(low, 2, 1), jnp.where(low, 3, 0), s + 1 - 2 * lax.rem(s, 2)
            side = lax.rem(core + proc, 2)
            is_inner = jnp.logical_or(s == 1, s == 2)

            def own(ref):
                for turn in range(2):
                    place(ids, ref, held, sem, s, turn, turn * half_rows)

            def others(main, main_x, rest, rest_x):
                for e in range(2):
                    same = side == e
                    place(ids, main[e], held, sem, jnp.where(same, near, far), core)
                    place(ids, main_x[e], held, sem, jnp.where(same, far, near), 1 - core)

                    @pl.when(same)
                    def _():
                        place(ids, rest[e], held, sem, pair, core)
                        place(ids, rest_x[1 - e], held, sem, pair, 1 - core)

            @pl.when(side == 0)
            def _():
                own(refs[0])

            @pl.when(side == 1)
            def _():
                own(refs[1])

            @pl.when(is_inner)
            def _():
                others(refs[2:4], refs[4:6], refs[6:8], refs[8:10])

            @pl.when(jnp.logical_not(is_inner))
            def _():
                others(refs[6:8], refs[8:10], refs[2:4], refs[4:6])
    else:
        full = lax.all_gather(cotangent[0], "shard", axis=0, tiled=True)
        sources = [jnp.where(core == proc, full, move(full, swap_of(everyone)))]
        w_pieces = [move(x, route) for x, route in zip(prepared, w_routes)]
        normed = lax.all_gather(shift_tokens(normed)[None], "particle", axis=0, tiled=True)
        sums = add_over(pair_sums(whole), range(len(hops) - 2))

        def pick(ids, refs, held, sem):
            def one(which, carry):
                for turn in range(2):
                    start = pl.multiple_of(which * tok_rows + turn * half_rows, half_rows)
                    place(ids, refs[0], held, sem, which, turn, start)
                return carry

            lax.fori_loop(0, shards, one, 0)

    normed = normed.reshape(tokens, width)
    act_t, slope_t, down_t = pl.pallas_call(
        functools.partial(up_kernel, shards, width ** (-0.5)),
        grid=(blocks,),
        out_shape=[
            jax.ShapeDtypeStruct((part, tokens), BF),
            jax.ShapeDtypeStruct((part, tokens), BF),
            jax.ShapeDtypeStruct((part, width), BF),
        ],
        in_specs=[smem_spec(), pl.BlockSpec((BLOCK, width), lambda i: (i, 0))]
        + [pl.BlockSpec((2, rows, part), lambda i: (0, 0, 0))] * shards,
        out_specs=[
            pl.BlockSpec((part, BLOCK), lambda i: (0, i)),
            pl.BlockSpec((part, BLOCK), lambda i: (0, i)),
            pl.BlockSpec((part, width), lambda i: (0, 0)),
        ],
        scratch_shapes=[pltpu.VMEM((width, part), BF), pltpu.VMEM((width, part), BF), pltpu.VMEM((part, width), BF)],
        compiler_params=params(56),
        name="up",
    )(ids, normed, *w_pieces)

    sums = add_over(sums, [-2])
    sums, act_t, slope_t = lax.optimization_barrier((sums, act_t, slope_t))
    grad_scale = 1.0 / (tokens * width)
    scores = pl.pallas_call(
        functools.partial(
            grad_kernel,
            shards,
            particles,
            -(width ** (-0.5)) * grad_scale,
            -(hidden ** (-0.5)) * grad_scale,
            hidden ** (-0.5),
            pick,
        ),
        out_shape=[jax.ShapeDtypeStruct((2, rows, cols), BF)] * particles,
        in_specs=[smem_spec()] + [any_spec()] * (4 + len(sources)),
        out_specs=[any_spec()] * particles,
        scratch_shapes=[
            pltpu.VMEM((tokens, width), BF),
            pltpu.VMEM((tokens, width), BF),
            pltpu.VMEM((part, tokens), BF),
            pltpu.VMEM((part, tokens), BF),
            pltpu.VMEM((part, tokens), BF),
            pltpu.VMEM((part, width), BF),
            pltpu.VMEM((2, width, part), BF),
            pltpu.SemaphoreType.DMA((particles + 5,)),
        ],
        compiler_params=params(56),
        name="grads",
    )(ids, normed, act_t, slope_t, down_t, *sources)

    sums = add_over(sums, [-1])
    sums, *scores = lax.optimization_barrier((sums, *scores))

    ratio = particles // shards
    arrived = []
    for t in range(particles):
        pairs = []
        for m, c, s in devices:
            mine, q = 2 * m + s // half, 2 * (s % half) + c
            u = (mine + ratio * q - t) % particles
            z, e = u // ratio, q * ratio + u % ratio
            pairs.append((dev(m, c, s), dev(e // 2 + z, e % 2, z)))
        arrived.append(move(scores[t], pairs))

    first_moment, second_moment, sums, *arrived[:5] = lax.optimization_barrier(
        (flat(first_moment), flat(second_moment), sums, *arrived[:5])
    )
    first_moment, second_moment = 0.9 * first_moment, 0.999 * second_moment
    sums = sums[0]
    lookup = [
        [pair_list.index((max(i, j), min(i, j))) if i != j else len(pair_list) for j in range(particles)]
        for i in range(particles)
    ]
    table = jnp.concatenate([sums[: len(pair_list)], jnp.zeros((1,), F32)])
    distances = table[jnp.array(lookup, jnp.int32)]
    inverse_band = 1.0 / kernel_scale[0].astype(F32)
    repulse = 2.0 * inverse_band
    kernel = jnp.exp(-distances * inverse_band)
    scale = 2 * width * hidden / particles
    coef = jnp.concatenate(
        [(scale * kernel).reshape(-1), scale * repulse * jnp.sum(kernel, axis=1), repulse[None]]
    )

    fields = pl.pallas_call(
        functools.partial(stein_kernel, shards, particles),
        out_shape=[jax.ShapeDtypeStruct((2, rows, cols), BF)] * particles,
        in_specs=[smem_spec(), smem_spec(), pl.BlockSpec(memory_space=pltpu.VMEM)] + [any_spec()] * particles,
        out_specs=[any_spec()] * particles,
        scratch_shapes=[
            pltpu.VMEM((particles, 2, rows, cols), BF),
            pltpu.VMEM((particles, 2, rows, cols), BF),
            pltpu.VMEM((particles, min(rows, 64), LANES), F32),
            pltpu.SemaphoreType.DMA((particles,)),
        ],
        compiler_params=params(12),
        name="stein",
    )(ids, coef, whole, *arrived)

    back = []
    for k in range(columns):
        for x in range(2):
            pairs = [(dev(m, c, s), dev(m + k, c ^ x, s)) for m, c, s in devices]
            back.append(move(fields[2 * k + x], pairs))

    steps = max(rows // 32, 1)
    flat_rows = rows * 2 * lane_tiles
    state_spec = pl.BlockSpec((flat_rows // steps, LANES), lambda i: (i, 0))
    outs = pl.pallas_call(
        functools.partial(adam_kernel, particles),
        grid=(steps,),
        out_shape=[jax.ShapeDtypeStruct((flat_rows, LANES), F32)] * 4,
        in_specs=[smem_spec()] + [state_spec] * 3 + [any_spec()] * particles,
        out_specs=[state_spec] * 4,
        scratch_shapes=[pltpu.VMEM((2, rows, hidden), BF), pltpu.SemaphoreType.DMA((particles,))],
        compiler_params=params(20),
        name="adam",
    )(ids, w_flat, first_moment, second_moment, *back)
    return tuple(unflat(x) for x in outs)


def solution(mesh):
    state = P("particle", "shard", None, None)
    return jax.shard_map(
        local,
        mesh=mesh,
        in_specs=(P("shard", None), P("shard"), P(), P("particle", "shard", None), state, state, state),
        out_specs=(state, state, state, state),
        check_vma=False,
    )
```

```python
import functools

import jax
import jax.numpy as jnp
from jax import lax
from jax.experimental import pallas as pl
from jax.experimental.pallas import tpu as pltpu
from jax.sharding import PartitionSpec as P

BF = jnp.bfloat16
F32 = jnp.float32
AXES = ("particle", "shard")
LANES = 128
BLOCK = 256
MIB = 1024 * 1024
NT = (((1,), (1,)), ((), ()))

COL, CORE, SHARD, PROC, PIECE = range(5)


def any_spec():
    return pl.BlockSpec(memory_space=pl.ANY)


def smem_spec():
    return pl.BlockSpec(memory_space=pltpu.SMEM)


def params(mib):
    return pltpu.CompilerParams(vmem_limit_bytes=mib * MIB)


def run_copies(copies):
    for copy in copies:
        copy.start()
    for copy in copies:
        copy.wait()


def slice_index(ids, column, core, shard, columns):
    return 2 * lax.rem(column - shard + columns * 16, columns) + core


def prep_kernel(shards, ids, w, *out):
    pieces, slices = out[:shards], out[shards]
    _, rows, piece = pieces[0].shape
    particles, _, _, cols = slices.shape
    columns = particles // 2
    tiles, per_slice = piece // LANES, cols // LANES
    for r in range(shards):
        q = lax.rem(ids[SHARD] - r + shards, shards)
        for j in range(tiles):
            e = q * (tiles // per_slice) + j // per_slice
            column = lax.rem(lax.div(e, 2) + ids[SHARD], columns)
            p = 2 * column + lax.rem(e, 2)
            at, within = j * LANES, j % per_slice * LANES
            for kind in range(2):
                line = 2 * (q * tiles + j) + kind
                part = w[pl.ds(line, rows, stride=2 * shards * tiles), :].astype(BF)
                pieces[r][kind, :, at : at + LANES] = part
                slices[p, kind, :, within : within + LANES] = part


def up_kernel(shards, scale, ids, tokens, *refs):
    pieces = refs[:shards]
    act_t, slope_t, down_t, up_w, down_w, up_t = refs[shards:]
    width, part = up_w.shape
    rows = width // shards

    @pl.when(pl.program_id(0) == 0)
    def _():
        for r in range(shards):
            at = pl.multiple_of(lax.rem(ids[PIECE] + r, shards) * rows, rows)
            up_w[pl.ds(at, rows), :] = pieces[r][0]
            down_w[pl.ds(at, rows), :] = pieces[r][1]
        for i in range(width // LANES):
            span = slice(i * LANES, (i + 1) * LANES)
            up_t[:, span] = up_w[span, :].astype(F32).T.astype(BF)
            down_t[:, span] = down_w[span, :].astype(F32).T.astype(BF)

    u = lax.dot_general(up_t[...], tokens[...], NT, preferred_element_type=F32) * scale
    cdf = 0.5 * (1.0 + lax.erf(u * 0.7071067811865476))
    density = jnp.exp(-0.5 * u * u) * 0.3989422804014327
    act_t[...] = (u * cdf).astype(BF)
    slope_t[...] = (cdf + u * density).astype(BF)


def grad_kernel(shards, particles, up_scale, down_scale, back_scale, pick, ids, normed, act_t, slope_t, down_t, *refs):
    n_in = len(refs) - particles - 8
    sources, out = refs[:n_in], refs[n_in : n_in + particles]
    c, n, act, slope, grad, down, score, sems = refs[n_in + particles :]
    part, tokens = act.shape
    width = c.shape[1]
    chunk = tokens // shards
    per_turn, per_part = shards // 2, max(shards // 4, 1)

    def chunk_of(i):
        rest = lax.rem(i, 2 * per_part)
        return lax.div(rest, per_part) * per_turn + lax.div(i, 2 * per_part) * per_part + lax.rem(rest, per_part)

    def slope_copy(i):
        at = pl.multiple_of(chunk_of(i) * chunk, chunk)
        span = (slice(None), pl.ds(at, chunk))
        return pltpu.make_async_copy(slope_t.at[span], slope.at[span], sems.at[shards + chunk_of(i)])

    down_copy = pltpu.make_async_copy(down_t, down, sems.at[2 * shards])
    act_copy = pltpu.make_async_copy(act_t, act, sems.at[2 * shards + 1])
    n_copy = pltpu.make_async_copy(normed, n, sems.at[2 * shards + 2])
    down_copy.start()
    for i in range(2):
        pick(ids, sources, c, sems, i)
        for j in range(i * shards // 2, (i + 1) * shards // 2):
            slope_copy(jnp.int32(j)).start()
    act_copy.start()
    n_copy.start()
    down_copy.wait()

    def back(i, carry):
        at = pl.multiple_of(chunk_of(i) * chunk, chunk)
        rows = c.at[pl.ds(at, chunk), :]
        pltpu.make_async_copy(rows, rows, sems.at[chunk_of(i)]).wait()
        slope_copy(i).wait()
        b = lax.dot_general(down[...], c[pl.ds(at, chunk), :], NT, preferred_element_type=F32)
        grad[:, pl.ds(at, chunk)] = (b * (slope[:, pl.ds(at, chunk)].astype(F32) * back_scale)).astype(BF)
        return carry

    lax.fori_loop(0, shards, back, 0)
    rows = width // shards
    ratio = particles // shards
    cols = part // ratio
    mine = 2 * ids[COL] + ids[PROC]
    copies = []

    def send(kind):
        for t in range(particles):
            u = lax.rem(mine + ratio * ids[PIECE] - t + particles, particles)
            row = pl.multiple_of(lax.div(u, ratio) * rows, rows)
            col = pl.multiple_of(lax.rem(u, ratio) * cols, cols)
            source = score.at[kind, pl.ds(row, rows), pl.ds(col, cols)]
            copies.append(pltpu.make_async_copy(source, out[t].at[kind], sems.at[2 * shards + 3 + kind * particles + t]))
            copies[-1].start()

    def gradient(left, right, scale, kind):
        def tile(j, carry):
            at = pl.multiple_of(j * BLOCK, BLOCK)
            g = jnp.dot(left[...], right[:, pl.ds(at, BLOCK)], preferred_element_type=F32)
            score[kind, pl.ds(at, BLOCK), :] = (g * scale).T.astype(BF)
            return carry

        lax.fori_loop(0, width // BLOCK, tile, 0)
        send(kind)

    act_copy.wait()
    gradient(act, c, down_scale, 1)
    n_copy.wait()
    gradient(grad, n, up_scale, 0)
    for copy in copies:
        copy.wait()


def distance_kernel(whole, out):
    particles, _, rows, cols = whole.shape
    pairs = [(i, j) for i in range(particles) for j in range(i)]
    tiles = cols // LANES

    def body(g, acc):
        kind = lax.div(g, rows // 16)
        row = pl.multiple_of(lax.rem(g, rows // 16) * 16, 16)
        for tile in range(tiles):
            w = [whole[p, kind, pl.ds(row, 16), tile * LANES : (tile + 1) * LANES].astype(F32) for p in range(particles)]
            new = []
            for a, (i, j) in zip(acc, pairs):
                d = w[i] - w[j]
                d = d * d
                new.append(a + (d[:8] + d[8:]))
            acc = tuple(new)
        return acc

    acc = lax.fori_loop(0, 2 * rows // 16, body, tuple(jnp.zeros((8, LANES), F32) for _ in pairs))
    lane = lax.broadcasted_iota(jnp.int32, (8, LANES), 1)
    row = jnp.zeros((8, LANES), F32)
    for i, a in enumerate(acc):
        total = jnp.sum(jnp.sum(a, axis=0, keepdims=True), axis=1, keepdims=True)
        row = row + jnp.where(lane == i, total, 0.0)
    out[...] = row


def stein_kernel(shards, particles, ids, coef, whole, *refs):
    sources, out = refs[:particles], refs[particles : 2 * particles]
    scores, field, pushed, sems = refs[2 * particles :]
    columns = particles // 2
    ratio = particles // shards
    _, _, rows, cols = whole.shape
    e = slice_index(ids, ids[COL], ids[CORE], ids[SHARD], columns)
    u = ids[SHARD] * ratio + lax.rem(e, ratio) + particles * shards - ratio * lax.div(e, ratio)
    run_copies(
        [pltpu.make_async_copy(sources[t], scores.at[lax.rem(u + t, particles)], sems.at[t]) for t in range(particles)]
    )
    repulse = coef[particles * particles + particles]
    chunk = min(rows, 64)
    groups = rows // chunk
    tiles = cols // LANES

    def body(g, carry):
        kind = lax.div(g, groups)
        row = pl.multiple_of(lax.rem(g, groups) * chunk, chunk)
        for tile in range(tiles):
            at = (kind, pl.ds(row, chunk), slice(tile * LANES, (tile + 1) * LANES))
            for p in range(particles):
                pushed[p] = scores[(p,) + at].astype(F32) - repulse * whole[(p,) + at].astype(F32)
            for i in range(particles):
                total = coef[particles * particles + i] * whole[(i,) + at].astype(F32)
                for j in range(particles):
                    total = total + coef[i * particles + j] * pushed[j]
                field[(i,) + at] = total.astype(BF)
        return carry

    lax.fori_loop(0, 2 * groups, body, 0)
    copies = []
    for k in range(columns):
        for x in range(2):
            column = lax.rem(ids[COL] + k, columns)
            core = ids[CORE] if x == 0 else 1 - ids[CORE]
            i = 2 * k + x
            copies.append(pltpu.make_async_copy(field.at[2 * column + core], out[i], sems.at[i]))
    run_copies(copies)


def adam_kernel(particles, ids, w, first, second, *refs):
    sources = refs[:particles]
    new_w, new_first, new_second, transport, field, sems = refs[particles:]
    columns = particles // 2
    _, _, hidden = field.shape
    width = hidden // particles
    step = pl.program_id(0)

    @pl.when(step == 0)
    def _():
        copies = []
        for k in range(columns):
            for x in range(2):
                column = lax.rem(ids[COL] - k + columns, columns)
                core = ids[CORE] if x == 0 else 1 - ids[CORE]
                at = pl.multiple_of(slice_index(ids, column, core, ids[SHARD], columns) * width, width)
                i = 2 * k + x
                copies.append(pltpu.make_async_copy(sources[i], field.at[:, :, pl.ds(at, width)], sems.at[i]))
        run_copies(copies)

    lane_tiles = hidden // LANES
    rows = w.shape[0] // (2 * lane_tiles)
    base = pl.multiple_of(step * rows, rows)
    for kind in range(2):
        for tile in range(lane_tiles):
            part = field[kind, pl.ds(base, rows), tile * LANES : (tile + 1) * LANES]
            transport[pl.ds(2 * tile + kind, rows, stride=2 * lane_tiles), :] = part.astype(F32)
    t = transport[...]
    m = first[...] - 0.1 * t
    v = second[...] + 0.001 * t * t
    new_first[...] = m
    new_second[...] = v
    new_w[...] = w[...] - 0.01 * m / (jnp.sqrt(v) + 1e-08)


def local(pool, batch_index, kernel_scale, cotangent, weights, first_moment, second_moment):
    shards = lax.axis_size("shard")
    particles = lax.axis_size("particle")
    columns, half = particles // 2, shards // 2
    tok_rows = batch_index.shape[0]
    width = pool.shape[1]
    _, rows, _, hidden = weights.shape
    part, cols = hidden // shards, hidden // particles
    tokens = tok_rows * shards
    blocks = tokens // BLOCK
    lane_tiles = hidden // LANES

    own = lax.axis_index("particle")
    shard = lax.axis_index("shard")
    core, column = own % 2, own // 2
    proc = shard // half
    piece = 2 * (shard % half) + core
    ids = jnp.stack([column, core, shard, proc, piece]).astype(jnp.int32)
    devices = [(m, c, s) for m in range(columns) for c in range(2) for s in range(shards)]

    def dev(m, c, s):
        return (2 * (m % columns) + c) * shards + s

    def move(x, pairs):
        if all(a == b for a, b in pairs) and len(pairs) == len(devices):
            return x
        return lax.ppermute(x, AXES, pairs)

    def swap_of(among):
        return [(dev(m, c, s), dev(m, 1 - c, s)) for m, c, s in devices if s in among]

    def flat(x):
        return x[0].reshape(rows, 2, lane_tiles, LANES).transpose(0, 2, 1, 3).reshape(-1, LANES)

    def unflat(x):
        return x.reshape(rows, lane_tiles, 2, LANES).transpose(0, 2, 1, 3).reshape(1, rows, 2, hidden)

    everyone = range(shards)
    half_rows = tok_rows // 2
    share = tok_rows // particles
    index = lax.dynamic_slice(batch_index, (own * share,), (share,))
    picked = jnp.take(pool, index, axis=0).astype(F32)
    normed = (picked * lax.rsqrt(jnp.mean(picked * picked, axis=1, keepdims=True) + 1e-06)).astype(BF)

    def shift_tokens(x):
        shifted = [[(dev(m, c, s), dev(m, c, (s + k) % shards)) for m, c, s in devices] for k in range(shards)]
        return jnp.stack([move(x, pairs) for pairs in shifted])

    w_flat = flat(weights)
    steps = max(rows // 64, 1)
    lines = w_flat.shape[0] // steps
    *prepared, slices = pl.pallas_call(
        functools.partial(prep_kernel, shards),
        grid=(steps,),
        out_shape=[jax.ShapeDtypeStruct((2, rows, part), BF)] * shards
        + [jax.ShapeDtypeStruct((particles, 2, rows, cols), BF)],
        in_specs=[smem_spec(), pl.BlockSpec((lines, LANES), lambda i: (i, 0))],
        out_specs=[pl.BlockSpec((2, rows // steps, part), lambda i: (0, i, 0))] * shards
        + [pl.BlockSpec((particles, 2, rows // steps, cols), lambda i: (0, 0, i, 0))],
        compiler_params=params(56),
        name="prep",
    )(ids, w_flat)

    w_routes = []
    for r in range(shards):
        pairs = []
        for m, c, s in devices:
            q = (s - r) % shards
            pairs.append((dev(m, c, s), dev(m, q % 2, c * half + q // 2)))
        w_routes.append(pairs)

    whole = lax.all_to_all(slices, "particle", 0, 0, tiled=True)

    pair_list = [(i, j) for i in range(particles) for j in range(i)]
    hops = []
    for count, stride in ((particles, shards), (shards, 1)):
        hop = 1
        while hop < count:
            hops.append([(d, d + ((d // stride % count ^ hop) - d // stride % count) * stride) for d in range(len(devices))])
            hop *= 2

    def pair_sums(whole):
        return pl.pallas_call(
            distance_kernel,
            out_shape=jax.ShapeDtypeStruct((8, LANES), F32),
            in_specs=[pl.BlockSpec(memory_space=pltpu.VMEM)],
            out_specs=pl.BlockSpec(memory_space=pltpu.VMEM),
            compiler_params=params(8),
                name="distances",
        )(whole)

    def add_over(sums, steps):
        for step in steps:
            sums = sums + move(sums, hops[step])
        return sums

    def gather_row(ids, which, turn):
        k = lax.rem(ids[SHARD] - which + shards, shards)
        return (turn * (particles // 2) * shards + k) * share

    def place(ids, ref, held, sems, part, which, turn, start=0):
        quarter = max(particles // 4, 1)
        row = gather_row(ids, which, turn)
        for i in range(part * quarter, (part + 1) * quarter):
            to = pl.multiple_of(row + i * shards * share, share)
            sem = sems.at[lax.div(to, tokens // shards)]
            pltpu.make_async_copy(
                ref.at[pl.ds(start + i * share, share), :], held.at[pl.ds(to, share), :], sem
            ).start()

    if shards == 4:
        cot = cotangent[0]
        inner = jnp.logical_or(shard == 1, shard == 2)
        flip = jnp.where(jnp.logical_or(inner, core == proc), 0, 1)
        first_routes, second_routes = [], []
        for e in range(2):
            one, two = [], []
            for m, c, s in devices:
                at_home, is_inner = c == s // half, s in (1, 2)
                if not at_home:
                    to, turn = (3 - s, e) if is_inner else (1 if s == 3 else 2, 1 - e)
                    one.append((dev(m, c, s), dev(m, c ^ turn, to)))
                elif is_inner:
                    one.append((dev(m, c, s), dev(m, c ^ e, s ^ 1)))
                else:
                    two.append((dev(m, c, s), dev(m, c ^ e, s ^ 1)))
                if is_inner:
                    two.append((dev(m, c, s), dev(m, c, s ^ 1)))
            first_routes.append(one)
            second_routes.append(two)
        halves = [
            lax.dynamic_slice(cot, (((core + e + flip) % 2) * half_rows, 0), (half_rows, width)) for e in range(2)
        ]
        alpha = [move(x, route) for x, route in zip(halves, first_routes)]
        own_c = move(cot, [(dev(m, c, s), dev(m, 1 - c, s)) for m, c, s in devices if c == s // half])
        normed = shift_tokens(normed)
        alpha, own_c, prepared, normed = lax.optimization_barrier((alpha, own_c, prepared, normed))
        normed = lax.all_gather(normed[None], "particle", axis=0, tiled=True)
        w_pieces = [move(x, route) for x, route in zip(prepared, w_routes)]
        hand_on = [jnp.where(inner, a, x) for a, x in zip(alpha, halves)]
        alpha_x = [move(x, swap_of(everyone)) for x in alpha]
        beta = [move(hand_on[0], second_routes[0])]
        w_pieces, normed, whole, hand_on[1], alpha_x = lax.optimization_barrier(
            (w_pieces, normed, whole, hand_on[1], alpha_x)
        )
        beta.append(move(hand_on[1], second_routes[1]))
        def pick(ids, refs, held, sems, part):
            s, core, proc = ids[SHARD], ids[CORE], ids[PROC]
            low = s < 2
            near, far, pair = jnp.where(low, 2, 1), jnp.where(low, 3, 0), s + 1 - 2 * lax.rem(s, 2)
            side = lax.rem(core + proc, 2)
            is_inner = jnp.logical_or(s == 1, s == 2)

            def own(ref):
                for turn in range(2):
                    place(ids, ref, held, sems, part, s, turn, turn * half_rows)

            def others(main, main_x, rest, rest_x):
                for e in range(2):
                    same = side == e
                    place(ids, main[e], held, sems, part, jnp.where(same, near, far), core)
                    place(ids, main_x[e], held, sems, part, jnp.where(same, far, near), 1 - core)

                    @pl.when(same)
                    def _():
                        place(ids, rest[e], held, sems, part, pair, core)
                        place(ids, rest_x[1 - e], held, sems, part, pair, 1 - core)

            @pl.when(side == 0)
            def _():
                own(refs[0])

            @pl.when(side == 1)
            def _():
                own(refs[1])

            @pl.when(is_inner)
            def _():
                others(refs[2:4], refs[4:6], refs[6:8], refs[8:10])

            @pl.when(jnp.logical_not(is_inner))
            def _():
                others(refs[6:8], refs[8:10], refs[2:4], refs[4:6])
    else:
        full = lax.all_gather(cotangent[0], "shard", axis=0, tiled=True)
        sources = [jnp.where(core == proc, full, move(full, swap_of(everyone)))]
        w_pieces = [move(x, route) for x, route in zip(prepared, w_routes)]
        normed = lax.all_gather(shift_tokens(normed)[None], "particle", axis=0, tiled=True)

        def pick(ids, refs, held, sems, part):
            def one(which, carry):
                for turn in range(2):
                    start = pl.multiple_of(which * tok_rows + turn * half_rows, half_rows)
                    place(ids, refs[0], held, sems, part, which, turn, start)
                return carry

            lax.fori_loop(0, shards, one, 0)

    normed = normed.reshape(tokens, width)
    act_t, slope_t, down_t = pl.pallas_call(
        functools.partial(up_kernel, shards, width ** (-0.5)),
        grid=(blocks,),
        out_shape=[
            jax.ShapeDtypeStruct((part, tokens), BF),
            jax.ShapeDtypeStruct((part, tokens), BF),
            jax.ShapeDtypeStruct((part, width), BF),
        ],
        in_specs=[smem_spec(), pl.BlockSpec((BLOCK, width), lambda i: (i, 0))]
        + [pl.BlockSpec((2, rows, part), lambda i: (0, 0, 0))] * shards,
        out_specs=[
            pl.BlockSpec((part, BLOCK), lambda i: (0, i)),
            pl.BlockSpec((part, BLOCK), lambda i: (0, i)),
            pl.BlockSpec((part, width), lambda i: (0, 0)),
        ],
        scratch_shapes=[pltpu.VMEM((width, part), BF), pltpu.VMEM((width, part), BF), pltpu.VMEM((part, width), BF)],
        compiler_params=params(56),
        name="up",
    )(ids, normed, *w_pieces)

    sums = add_over(pair_sums(whole), [0])
    sums, act_t = lax.optimization_barrier((sums, act_t))
    if shards == 4:
        beta[1], act_t = lax.optimization_barrier((beta[1], act_t))
        beta_x = [move(x, swap_of(everyone)) for x in beta]
        sources = [cot, own_c, *alpha, *alpha_x, *beta, *beta_x]
    sums = add_over(sums, range(1, len(hops) - 2))
    sums, slope_t = lax.optimization_barrier((sums, slope_t))
    grad_scale = 1.0 / (tokens * width)
    scores = pl.pallas_call(
        functools.partial(
            grad_kernel,
            shards,
            particles,
            -(width ** (-0.5)) * grad_scale,
            -(hidden ** (-0.5)) * grad_scale,
            hidden ** (-0.5),
            pick,
        ),
        out_shape=[jax.ShapeDtypeStruct((2, rows, cols), BF)] * particles,
        in_specs=[smem_spec()] + [any_spec()] * (4 + len(sources)),
        out_specs=[any_spec()] * particles,
        scratch_shapes=[
            pltpu.VMEM((tokens, width), BF),
            pltpu.VMEM((tokens, width), BF),
            pltpu.VMEM((part, tokens), BF),
            pltpu.VMEM((part, tokens), BF),
            pltpu.VMEM((part, tokens), BF),
            pltpu.VMEM((part, width), BF),
            pltpu.VMEM((2, width, part), BF),
            pltpu.SemaphoreType.DMA((2 * shards + 3 + 2 * particles,)),
        ],
        compiler_params=params(56),
        name="grads",
    )(ids, normed, act_t, slope_t, down_t, *sources)

    sums = add_over(sums, [-2])
    sums, *scores = lax.optimization_barrier((sums, *scores))

    ratio = particles // shards
    arrived = []
    for t in range(particles):
        pairs = []
        for m, c, s in devices:
            mine, q = 2 * m + s // half, 2 * (s % half) + c
            u = (mine + ratio * q - t) % particles
            z, e = u // ratio, q * ratio + u % ratio
            pairs.append((dev(m, c, s), dev(e // 2 + z, e % 2, z)))
        arrived.append(move(scores[t], pairs))

    rest = move(sums, hops[-1])
    first_moment, second_moment, sums, rest, *arrived[:4] = lax.optimization_barrier(
        (flat(first_moment), flat(second_moment), sums, rest, *arrived[:4])
    )
    sums = sums + rest
    first_moment, second_moment = 0.9 * first_moment, 0.999 * second_moment
    sums = sums[0]
    lookup = [
        [pair_list.index((max(i, j), min(i, j))) if i != j else len(pair_list) for j in range(particles)]
        for i in range(particles)
    ]
    table = jnp.concatenate([sums[: len(pair_list)], jnp.zeros((1,), F32)])
    distances = table[jnp.array(lookup, jnp.int32)]
    inverse_band = 1.0 / kernel_scale[0].astype(F32)
    repulse = 2.0 * inverse_band
    kernel = jnp.exp(-distances * inverse_band)
    scale = 2 * width * hidden / particles
    coef = jnp.concatenate(
        [(scale * kernel).reshape(-1), scale * repulse * jnp.sum(kernel, axis=1), repulse[None]]
    )

    fields = pl.pallas_call(
        functools.partial(stein_kernel, shards, particles),
        out_shape=[jax.ShapeDtypeStruct((2, rows, cols), BF)] * particles,
        in_specs=[smem_spec(), smem_spec(), pl.BlockSpec(memory_space=pltpu.VMEM)] + [any_spec()] * particles,
        out_specs=[any_spec()] * particles,
        scratch_shapes=[
            pltpu.VMEM((particles, 2, rows, cols), BF),
            pltpu.VMEM((particles, 2, rows, cols), BF),
            pltpu.VMEM((particles, min(rows, 64), LANES), F32),
            pltpu.SemaphoreType.DMA((particles,)),
        ],
        compiler_params=params(12),
        name="stein",
    )(ids, coef, whole, *arrived)

    back = []
    for k in range(columns):
        for x in range(2):
            pairs = [(dev(m, c, s), dev(m + k, c ^ x, s)) for m, c, s in devices]
            back.append(move(fields[2 * k + x], pairs))

    steps = max(rows // 32, 1)
    flat_rows = rows * 2 * lane_tiles
    state_spec = pl.BlockSpec((flat_rows // steps, LANES), lambda i: (i, 0))
    outs = pl.pallas_call(
        functools.partial(adam_kernel, particles),
        grid=(steps,),
        out_shape=[jax.ShapeDtypeStruct((flat_rows, LANES), F32)] * 4,
        in_specs=[smem_spec()] + [state_spec] * 3 + [any_spec()] * particles,
        out_specs=[state_spec] * 4,
        scratch_shapes=[pltpu.VMEM((2, rows, hidden), BF), pltpu.SemaphoreType.DMA((particles,))],
        compiler_params=params(20),
        name="adam",
    )(ids, w_flat, first_moment, second_moment, *back)
    return tuple(unflat(x) for x in outs)


def solution(mesh):
    state = P("particle", "shard", None, None)
    return jax.shard_map(
        local,
        mesh=mesh,
        in_specs=(P("shard", None), P("shard"), P(), P("particle", "shard", None), state, state, state),
        out_specs=(state, state, state, state),
        check_vma=False,
    )
```

```python
import functools

import jax
import jax.numpy as jnp
from jax import lax
from jax.experimental import pallas as pl
from jax.experimental.pallas import tpu as pltpu
from jax.sharding import PartitionSpec as P

BF = jnp.bfloat16
F32 = jnp.float32
AXES = ("particle", "shard")
LANES = 128
BLOCK = 256
MIB = 1024 * 1024
NT = (((1,), (1,)), ((), ()))

COL, CORE, SHARD, PROC, PIECE = range(5)


def any_spec():
    return pl.BlockSpec(memory_space=pl.ANY)


def smem_spec():
    return pl.BlockSpec(memory_space=pltpu.SMEM)


def params(mib):
    return pltpu.CompilerParams(vmem_limit_bytes=mib * MIB)


def run_copies(copies):
    for copy in copies:
        copy.start()
    for copy in copies:
        copy.wait()


def slice_index(ids, column, core, shard, columns):
    return 2 * lax.rem(column - shard + columns * 16, columns) + core


def prep_kernel(shards, ids, w, *out):
    pieces, slices = out[:shards], out[shards]
    _, rows, piece = pieces[0].shape
    particles, _, _, cols = slices.shape
    columns = particles // 2
    tiles, per_slice = piece // LANES, cols // LANES
    for r in range(shards):
        q = lax.rem(ids[SHARD] - r + shards, shards)
        for j in range(tiles):
            e = q * (tiles // per_slice) + j // per_slice
            column = lax.rem(lax.div(e, 2) + ids[SHARD], columns)
            p = 2 * column + lax.rem(e, 2)
            at, within = j * LANES, j % per_slice * LANES
            for kind in range(2):
                line = 2 * (q * tiles + j) + kind
                part = w[pl.ds(line, rows, stride=2 * shards * tiles), :].astype(BF)
                pieces[r][kind, :, at : at + LANES] = part
                slices[p, kind, :, within : within + LANES] = part


def up_kernel(shards, scale, ids, tokens, *refs):
    pieces = refs[:shards]
    act_t, slope_t, down_t, up_w, down_w, up_t = refs[shards:]
    width, part = up_w.shape
    rows = width // shards

    @pl.when(pl.program_id(0) == 0)
    def _():
        for r in range(shards):
            at = pl.multiple_of(lax.rem(ids[PIECE] + r, shards) * rows, rows)
            up_w[pl.ds(at, rows), :] = pieces[r][0]
            down_w[pl.ds(at, rows), :] = pieces[r][1]
        for i in range(width // LANES):
            span = slice(i * LANES, (i + 1) * LANES)
            up_t[:, span] = up_w[span, :].astype(F32).T.astype(BF)
            down_t[:, span] = down_w[span, :].astype(F32).T.astype(BF)

    u = lax.dot_general(up_t[...], tokens[...], NT, preferred_element_type=F32) * scale
    cdf = 0.5 * (1.0 + lax.erf(u * 0.7071067811865476))
    density = jnp.exp(-0.5 * u * u) * 0.3989422804014327
    act_t[...] = (u * cdf).astype(BF)
    slope_t[...] = (cdf + u * density).astype(BF)


def grad_kernel(shards, particles, up_scale, down_scale, back_scale, pick, ids, normed, act_t, slope_t, down_t, *refs):
    n_in = len(refs) - particles - 8
    sources, out = refs[:n_in], refs[n_in : n_in + particles]
    c, n, act, slope, grad, down, score, sems = refs[n_in + particles :]
    part, tokens = act.shape
    width = c.shape[1]
    chunk = tokens // shards
    first = [
        pltpu.make_async_copy(down_t, down, sems.at[1]),
        pltpu.make_async_copy(slope_t, slope, sems.at[2]),
    ]
    later = [
        pltpu.make_async_copy(act_t, act, sems.at[3]),
        pltpu.make_async_copy(normed, n, sems.at[4]),
    ]
    for copy in first:
        copy.start()
    pick(ids, sources, c, sems.at[0])
    for copy in later:
        copy.start()
    for copy in first:
        copy.wait()
    pltpu.make_async_copy(c, c, sems.at[0]).wait()

    def back(i, carry):
        at = pl.multiple_of(i * chunk, chunk)
        b = lax.dot_general(down[...], c[pl.ds(at, chunk), :], NT, preferred_element_type=F32)
        grad[:, pl.ds(at, chunk)] = (b * (slope[:, pl.ds(at, chunk)].astype(F32) * back_scale)).astype(BF)
        return carry

    lax.fori_loop(0, shards, back, 0)
    for copy in later:
        copy.wait()

    def gradient(j, carry):
        at = pl.multiple_of(j * BLOCK, BLOCK)
        g = jnp.dot(grad[...], n[:, pl.ds(at, BLOCK)], preferred_element_type=F32)
        score[0, pl.ds(at, BLOCK), :] = (g * up_scale).T.astype(BF)
        g = jnp.dot(act[...], c[:, pl.ds(at, BLOCK)], preferred_element_type=F32)
        score[1, pl.ds(at, BLOCK), :] = (g * down_scale).T.astype(BF)
        return carry

    lax.fori_loop(0, width // BLOCK, gradient, 0)
    rows = width // shards
    ratio = particles // shards
    cols = part // ratio
    mine = 2 * ids[COL] + ids[PROC]
    copies = []
    for t in range(particles):
        u = lax.rem(mine + ratio * ids[PIECE] - t + particles, particles)
        row = pl.multiple_of(lax.div(u, ratio) * rows, rows)
        col = pl.multiple_of(lax.rem(u, ratio) * cols, cols)
        copies.append(pltpu.make_async_copy(score.at[:, pl.ds(row, rows), pl.ds(col, cols)], out[t], sems.at[t]))
    run_copies(copies)


def distance_kernel(whole, out):
    particles, _, rows, cols = whole.shape
    pairs = [(i, j) for i in range(particles) for j in range(i)]
    tiles = cols // LANES

    def body(g, acc):
        kind = lax.div(g, rows // 16)
        row = pl.multiple_of(lax.rem(g, rows // 16) * 16, 16)
        for tile in range(tiles):
            w = [whole[p, kind, pl.ds(row, 16), tile * LANES : (tile + 1) * LANES].astype(F32) for p in range(particles)]
            new = []
            for a, (i, j) in zip(acc, pairs):
                d = w[i] - w[j]
                d = d * d
                new.append(a + (d[:8] + d[8:]))
            acc = tuple(new)
        return acc

    acc = lax.fori_loop(0, 2 * rows // 16, body, tuple(jnp.zeros((8, LANES), F32) for _ in pairs))
    lane = lax.broadcasted_iota(jnp.int32, (8, LANES), 1)
    row = jnp.zeros((8, LANES), F32)
    for i, a in enumerate(acc):
        total = jnp.sum(jnp.sum(a, axis=0, keepdims=True), axis=1, keepdims=True)
        row = row + jnp.where(lane == i, total, 0.0)
    out[...] = row


def stein_kernel(shards, particles, ids, coef, whole, *refs):
    sources, out = refs[:particles], refs[particles : 2 * particles]
    scores, field, pushed, sems = refs[2 * particles :]
    columns = particles // 2
    ratio = particles // shards
    _, _, rows, cols = whole.shape
    e = slice_index(ids, ids[COL], ids[CORE], ids[SHARD], columns)
    u = ids[SHARD] * ratio + lax.rem(e, ratio) + particles * shards - ratio * lax.div(e, ratio)
    run_copies(
        [pltpu.make_async_copy(sources[t], scores.at[lax.rem(u + t, particles)], sems.at[t]) for t in range(particles)]
    )
    repulse = coef[particles * particles + particles]
    chunk = min(rows, 64)
    groups = rows // chunk
    tiles = cols // LANES

    def body(g, carry):
        kind = lax.div(g, groups)
        row = pl.multiple_of(lax.rem(g, groups) * chunk, chunk)
        for tile in range(tiles):
            at = (kind, pl.ds(row, chunk), slice(tile * LANES, (tile + 1) * LANES))
            for p in range(particles):
                pushed[p] = scores[(p,) + at].astype(F32) - repulse * whole[(p,) + at].astype(F32)
            for i in range(particles):
                total = coef[particles * particles + i] * whole[(i,) + at].astype(F32)
                for j in range(particles):
                    total = total + coef[i * particles + j] * pushed[j]
                field[(i,) + at] = total.astype(BF)
        return carry

    lax.fori_loop(0, 2 * groups, body, 0)
    copies = []
    for k in range(columns):
        for x in range(2):
            column = lax.rem(ids[COL] + k, columns)
            core = ids[CORE] if x == 0 else 1 - ids[CORE]
            i = 2 * k + x
            copies.append(pltpu.make_async_copy(field.at[2 * column + core], out[i], sems.at[i]))
    run_copies(copies)


def adam_kernel(particles, ids, w, first, second, *refs):
    sources = refs[:particles]
    new_w, new_first, new_second, transport, field, sems = refs[particles:]
    columns = particles // 2
    _, _, hidden = field.shape
    width = hidden // particles
    step = pl.program_id(0)

    @pl.when(step == 0)
    def _():
        copies = []
        for k in range(columns):
            for x in range(2):
                column = lax.rem(ids[COL] - k + columns, columns)
                core = ids[CORE] if x == 0 else 1 - ids[CORE]
                at = pl.multiple_of(slice_index(ids, column, core, ids[SHARD], columns) * width, width)
                i = 2 * k + x
                copies.append(pltpu.make_async_copy(sources[i], field.at[:, :, pl.ds(at, width)], sems.at[i]))
        run_copies(copies)

    lane_tiles = hidden // LANES
    rows = w.shape[0] // (2 * lane_tiles)
    base = pl.multiple_of(step * rows, rows)
    for kind in range(2):
        for tile in range(lane_tiles):
            part = field[kind, pl.ds(base, rows), tile * LANES : (tile + 1) * LANES]
            transport[pl.ds(2 * tile + kind, rows, stride=2 * lane_tiles), :] = part.astype(F32)
    t = transport[...]
    m = first[...] - 0.1 * t
    v = second[...] + 0.001 * t * t
    new_first[...] = m
    new_second[...] = v
    new_w[...] = w[...] - 0.01 * m / (jnp.sqrt(v) + 1e-08)


def local(pool, batch_index, kernel_scale, cotangent, weights, first_moment, second_moment):
    shards = lax.axis_size("shard")
    particles = lax.axis_size("particle")
    columns, half = particles // 2, shards // 2
    tok_rows = batch_index.shape[0]
    width = pool.shape[1]
    _, rows, _, hidden = weights.shape
    part, cols = hidden // shards, hidden // particles
    tokens = tok_rows * shards
    blocks = tokens // BLOCK
    lane_tiles = hidden // LANES

    own = lax.axis_index("particle")
    shard = lax.axis_index("shard")
    core, column = own % 2, own // 2
    proc = shard // half
    piece = 2 * (shard % half) + core
    ids = jnp.stack([column, core, shard, proc, piece]).astype(jnp.int32)
    devices = [(m, c, s) for m in range(columns) for c in range(2) for s in range(shards)]

    def dev(m, c, s):
        return (2 * (m % columns) + c) * shards + s

    def move(x, pairs):
        if all(a == b for a, b in pairs) and len(pairs) == len(devices):
            return x
        return lax.ppermute(x, AXES, pairs)

    def swap_of(among):
        return [(dev(m, c, s), dev(m, 1 - c, s)) for m, c, s in devices if s in among]

    def flat(x):
        return x[0].reshape(rows, 2, lane_tiles, LANES).transpose(0, 2, 1, 3).reshape(-1, LANES)

    def unflat(x):
        return x.reshape(rows, lane_tiles, 2, LANES).transpose(0, 2, 1, 3).reshape(1, rows, 2, hidden)

    everyone = range(shards)
    half_rows = tok_rows // 2
    share = tok_rows // particles
    index = lax.dynamic_slice(batch_index, (own * share,), (share,))
    picked = jnp.take(pool, index, axis=0).astype(F32)
    normed = (picked * lax.rsqrt(jnp.mean(picked * picked, axis=1, keepdims=True) + 1e-06)).astype(BF)

    def shift_tokens(x):
        shifted = [[(dev(m, c, s), dev(m, c, (s + k) % shards)) for m, c, s in devices] for k in range(shards)]
        return jnp.stack([move(x, pairs) for pairs in shifted])

    w_flat = flat(weights)
    steps = max(rows // 64, 1)
    lines = w_flat.shape[0] // steps
    *prepared, slices = pl.pallas_call(
        functools.partial(prep_kernel, shards),
        grid=(steps,),
        out_shape=[jax.ShapeDtypeStruct((2, rows, part), BF)] * shards
        + [jax.ShapeDtypeStruct((particles, 2, rows, cols), BF)],
        in_specs=[smem_spec(), pl.BlockSpec((lines, LANES), lambda i: (i, 0))],
        out_specs=[pl.BlockSpec((2, rows // steps, part), lambda i: (0, i, 0))] * shards
        + [pl.BlockSpec((particles, 2, rows // steps, cols), lambda i: (0, 0, i, 0))],
        compiler_params=params(56),
        name="prep",
    )(ids, w_flat)

    w_routes = []
    for r in range(shards):
        pairs = []
        for m, c, s in devices:
            q = (s - r) % shards
            pairs.append((dev(m, c, s), dev(m, q % 2, c * half + q // 2)))
        w_routes.append(pairs)

    whole = lax.all_to_all(slices, "particle", 0, 0, tiled=True)

    pair_list = [(i, j) for i in range(particles) for j in range(i)]
    hops = []
    for count, stride in ((particles, shards), (shards, 1)):
        hop = 1
        while hop < count:
            hops.append([(d, d + ((d // stride % count ^ hop) - d // stride % count) * stride) for d in range(len(devices))])
            hop *= 2

    def pair_sums(whole):
        return pl.pallas_call(
            distance_kernel,
            out_shape=jax.ShapeDtypeStruct((8, LANES), F32),
            in_specs=[pl.BlockSpec(memory_space=pltpu.VMEM)],
            out_specs=pl.BlockSpec(memory_space=pltpu.VMEM),
            compiler_params=params(8),
                name="distances",
        )(whole)

    def add_over(sums, steps):
        for step in steps:
            sums = sums + move(sums, hops[step])
        return sums

    def gather_row(ids, which, turn):
        k = lax.rem(ids[SHARD] - which + shards, shards)
        return (turn * (particles // 2) * shards + k) * share

    def place(ids, ref, held, sem, which, turn, start=0):
        row = gather_row(ids, which, turn)
        for i in range(particles // 2):
            to = pl.multiple_of(row + i * shards * share, share)
            pltpu.make_async_copy(
                ref.at[pl.ds(start + i * share, share), :], held.at[pl.ds(to, share), :], sem
            ).start()

    if shards == 4:
        cot = cotangent[0]
        inner = jnp.logical_or(shard == 1, shard == 2)
        flip = jnp.where(jnp.logical_or(inner, core == proc), 0, 1)
        first_routes, second_routes = [], []
        for e in range(2):
            one, two = [], []
            for m, c, s in devices:
                at_home, is_inner = c == s // half, s in (1, 2)
                if not at_home:
                    to, turn = (3 - s, e) if is_inner else (1 if s == 3 else 2, 1 - e)
                    one.append((dev(m, c, s), dev(m, c ^ turn, to)))
                elif is_inner:
                    one.append((dev(m, c, s), dev(m, c ^ e, s ^ 1)))
                else:
                    two.append((dev(m, c, s), dev(m, c ^ e, s ^ 1)))
                if is_inner:
                    two.append((dev(m, c, s), dev(m, c, s ^ 1)))
            first_routes.append(one)
            second_routes.append(two)
        halves = [
            lax.dynamic_slice(cot, (((core + e + flip) % 2) * half_rows, 0), (half_rows, width)) for e in range(2)
        ]
        alpha = [move(x, route) for x, route in zip(halves, first_routes)]
        normed = shift_tokens(normed)
        alpha, prepared, normed = lax.optimization_barrier((alpha, prepared, normed))
        normed = lax.all_gather(normed[None], "particle", axis=0, tiled=True)
        w_pieces = [move(x, route) for x, route in zip(prepared, w_routes)]
        beta = [move(jnp.where(inner, a, x), route) for a, x, route in zip(alpha, halves, second_routes)]
        alpha_x = [move(x, swap_of(everyone)) for x in alpha]
        whole, w_pieces[:3], beta = lax.optimization_barrier((whole, w_pieces[:3], beta))
        sums = add_over(pair_sums(whole), range(len(hops) - 2))
        beta_x = [move(beta[0], swap_of(everyone))]
        w_pieces, normed, sums, cot, alpha_x, beta_x = lax.optimization_barrier(
            (w_pieces, normed, sums, cot, alpha_x, beta_x)
        )
        own_c = move(cot, [(dev(m, c, s), dev(m, 1 - c, s)) for m, c, s in devices if c == s // half])
        beta_x.append(move(beta[1], swap_of(everyone)))
        sources = [cot, own_c, *alpha, *alpha_x, *beta, *beta_x]

        def pick(ids, refs, held, sem):
            s, core, proc = ids[SHARD], ids[CORE], ids[PROC]
            low = s < 2
            near, far, pair = jnp.where(low, 2, 1), jnp.where(low, 3, 0), s + 1 - 2 * lax.rem(s, 2)
            side = lax.rem(core + proc, 2)
            is_inner = jnp.logical_or(s == 1, s == 2)

            def own(ref):
                for turn in range(2):
                    place(ids, ref, held, sem, s, turn, turn * half_rows)

            def others(main, main_x, rest, rest_x):
                for e in range(2):
                    same = side == e
                    place(ids, main[e], held, sem, jnp.where(same, near, far), core)
                    place(ids, main_x[e], held, sem, jnp.where(same, far, near), 1 - core)

                    @pl.when(same)
                    def _():
                        place(ids, rest[e], held, sem, pair, core)
                        place(ids, rest_x[1 - e], held, sem, pair, 1 - core)

            @pl.when(side == 0)
            def _():
                own(refs[0])

            @pl.when(side == 1)
            def _():
                own(refs[1])

            @pl.when(is_inner)
            def _():
                others(refs[2:4], refs[4:6], refs[6:8], refs[8:10])

            @pl.when(jnp.logical_not(is_inner))
            def _():
                others(refs[6:8], refs[8:10], refs[2:4], refs[4:6])
    else:
        full = lax.all_gather(cotangent[0], "shard", axis=0, tiled=True)
        sources = [jnp.where(core == proc, full, move(full, swap_of(everyone)))]
        w_pieces = [move(x, route) for x, route in zip(prepared, w_routes)]
        normed = lax.all_gather(shift_tokens(normed)[None], "particle", axis=0, tiled=True)
        sums = add_over(pair_sums(whole), range(len(hops) - 2))

        def pick(ids, refs, held, sem):
            def one(which, carry):
                for turn in range(2):
                    start = pl.multiple_of(which * tok_rows + turn * half_rows, half_rows)
                    place(ids, refs[0], held, sem, which, turn, start)
                return carry

            lax.fori_loop(0, shards, one, 0)

    normed = normed.reshape(tokens, width)
    act_t, slope_t, down_t = pl.pallas_call(
        functools.partial(up_kernel, shards, width ** (-0.5)),
        grid=(blocks,),
        out_shape=[
            jax.ShapeDtypeStruct((part, tokens), BF),
            jax.ShapeDtypeStruct((part, tokens), BF),
            jax.ShapeDtypeStruct((part, width), BF),
        ],
        in_specs=[smem_spec(), pl.BlockSpec((BLOCK, width), lambda i: (i, 0))]
        + [pl.BlockSpec((2, rows, part), lambda i: (0, 0, 0))] * shards,
        out_specs=[
            pl.BlockSpec((part, BLOCK), lambda i: (0, i)),
            pl.BlockSpec((part, BLOCK), lambda i: (0, i)),
            pl.BlockSpec((part, width), lambda i: (0, 0)),
        ],
        scratch_shapes=[pltpu.VMEM((width, part), BF), pltpu.VMEM((width, part), BF), pltpu.VMEM((part, width), BF)],
        compiler_params=params(56),
        name="up",
    )(ids, normed, *w_pieces)

    sums = add_over(sums, [-2])
    sums, act_t, slope_t = lax.optimization_barrier((sums, act_t, slope_t))
    grad_scale = 1.0 / (tokens * width)
    scores = pl.pallas_call(
        functools.partial(
            grad_kernel,
            shards,
            particles,
            -(width ** (-0.5)) * grad_scale,
            -(hidden ** (-0.5)) * grad_scale,
            hidden ** (-0.5),
            pick,
        ),
        out_shape=[jax.ShapeDtypeStruct((2, rows, cols), BF)] * particles,
        in_specs=[smem_spec()] + [any_spec()] * (4 + len(sources)),
        out_specs=[any_spec()] * particles,
        scratch_shapes=[
            pltpu.VMEM((tokens, width), BF),
            pltpu.VMEM((tokens, width), BF),
            pltpu.VMEM((part, tokens), BF),
            pltpu.VMEM((part, tokens), BF),
            pltpu.VMEM((part, tokens), BF),
            pltpu.VMEM((part, width), BF),
            pltpu.VMEM((2, width, part), BF),
            pltpu.SemaphoreType.DMA((particles + 5,)),
        ],
        compiler_params=params(56),
        name="grads",
    )(ids, normed, act_t, slope_t, down_t, *sources)

    sums = add_over(sums, [-1])
    sums, *scores = lax.optimization_barrier((sums, *scores))

    ratio = particles // shards
    arrived = []
    for t in range(particles):
        pairs = []
        for m, c, s in devices:
            mine, q = 2 * m + s // half, 2 * (s % half) + c
            u = (mine + ratio * q - t) % particles
            z, e = u // ratio, q * ratio + u % ratio
            pairs.append((dev(m, c, s), dev(e // 2 + z, e % 2, z)))
        arrived.append(move(scores[t], pairs))

    first_moment, second_moment, sums, *arrived[:5] = lax.optimization_barrier(
        (flat(first_moment), flat(second_moment), sums, *arrived[:5])
    )
    first_moment, second_moment = 0.9 * first_moment, 0.999 * second_moment
    sums = sums[0]
    lookup = [
        [pair_list.index((max(i, j), min(i, j))) if i != j else len(pair_list) for j in range(particles)]
        for i in range(particles)
    ]
    table = jnp.concatenate([sums[: len(pair_list)], jnp.zeros((1,), F32)])
    distances = table[jnp.array(lookup, jnp.int32)]
    inverse_band = 1.0 / kernel_scale[0].astype(F32)
    repulse = 2.0 * inverse_band
    kernel = jnp.exp(-distances * inverse_band)
    scale = 2 * width * hidden / particles
    coef = jnp.concatenate(
        [(scale * kernel).reshape(-1), scale * repulse * jnp.sum(kernel, axis=1), repulse[None]]
    )

    fields = pl.pallas_call(
        functools.partial(stein_kernel, shards, particles),
        out_shape=[jax.ShapeDtypeStruct((2, rows, cols), BF)] * particles,
        in_specs=[smem_spec(), smem_spec(), pl.BlockSpec(memory_space=pltpu.VMEM)] + [any_spec()] * particles,
        out_specs=[any_spec()] * particles,
        scratch_shapes=[
            pltpu.VMEM((particles, 2, rows, cols), BF),
            pltpu.VMEM((particles, 2, rows, cols), BF),
            pltpu.VMEM((particles, min(rows, 64), LANES), F32),
            pltpu.SemaphoreType.DMA((particles,)),
        ],
        compiler_params=params(12),
        name="stein",
    )(ids, coef, whole, *arrived)

    back = []
    for k in range(columns):
        for x in range(2):
            pairs = [(dev(m, c, s), dev(m + k, c ^ x, s)) for m, c, s in devices]
            back.append(move(fields[2 * k + x], pairs))

    steps = max(rows // 32, 1)
    flat_rows = rows * 2 * lane_tiles
    state_spec = pl.BlockSpec((flat_rows // steps, LANES), lambda i: (i, 0))
    outs = pl.pallas_call(
        functools.partial(adam_kernel, particles),
        grid=(steps,),
        out_shape=[jax.ShapeDtypeStruct((flat_rows, LANES), F32)] * 4,
        in_specs=[smem_spec()] + [state_spec] * 3 + [any_spec()] * particles,
        out_specs=[state_spec] * 4,
        scratch_shapes=[pltpu.VMEM((2, rows, hidden), BF), pltpu.SemaphoreType.DMA((particles,))],
        compiler_params=params(20),
        name="adam",
    )(ids, w_flat, first_moment, second_moment, *back)
    return tuple(unflat(x) for x in outs)


def solution(mesh):
    state = P("particle", "shard", None, None)
    return jax.shard_map(
        local,
        mesh=mesh,
        in_specs=(P("shard", None), P("shard"), P(), P("particle", "shard", None), state, state, state),
        out_specs=(state, state, state, state),
        check_vma=False,
    )
```

```python
import functools

import jax
import jax.numpy as jnp
from jax import lax
from jax.experimental import pallas as pl
from jax.experimental.pallas import tpu as pltpu
from jax.sharding import PartitionSpec as P

BF = jnp.bfloat16
F32 = jnp.float32
AXES = ("particle", "shard")
LANES = 128
BLOCK = 256
MIB = 1024 * 1024
NT = (((1,), (1,)), ((), ()))

COL, CORE, SHARD, PROC, PIECE = range(5)


def any_spec():
    return pl.BlockSpec(memory_space=pl.ANY)


def smem_spec():
    return pl.BlockSpec(memory_space=pltpu.SMEM)


def params(mib):
    return pltpu.CompilerParams(vmem_limit_bytes=mib * MIB)


def run_copies(copies):
    for copy in copies:
        copy.start()
    for copy in copies:
        copy.wait()


def slice_index(ids, column, core, shard, columns):
    return 2 * lax.rem(column - shard + columns * 16, columns) + core


def sent_piece(shards, ids, r):
    if shards != 4:
        return lax.rem(ids[SHARD] - r + shards, shards)
    side = lax.rem(ids[SHARD], 2)
    if r < 2:
        return 2 * (1 - side) + r
    away = lax.rem(ids[PROC] + ids[CORE], 2)
    return 2 * side + lax.rem(r + 1 - away, 2)


def place_pieces(shards, ids, pieces, store):
    if shards != 4:
        for r in range(shards):
            store(pieces[r], lax.rem(ids[PIECE] + r, shards))
        return
    s = ids[SHARD]
    beside = s + 1 - 2 * lax.rem(s, 2)
    across = lax.rem(s + 2, 4)
    for e in range(2):

        @pl.when(ids[CORE] == e)
        def _():
            store(pieces[e], beside)
            store(pieces[2 + e], 3 - s)
            store(pieces[4 + e], across)
            store(pieces[5 - e], s)


def prep_kernel(shards, ids, w, *out):
    pieces, slices = out[:shards], out[shards]
    _, rows, piece = pieces[0].shape
    particles, _, _, cols = slices.shape
    columns = particles // 2
    tiles, per_slice = piece // LANES, cols // LANES
    for r in range(shards):
        q = sent_piece(shards, ids, r)
        for j in range(tiles):
            e = q * (tiles // per_slice) + j // per_slice
            column = lax.rem(lax.div(e, 2) + ids[SHARD], columns)
            p = 2 * column + lax.rem(e, 2)
            at, within = j * LANES, j % per_slice * LANES
            for kind in range(2):
                line = 2 * (q * tiles + j) + kind
                part = w[pl.ds(line, rows, stride=2 * shards * tiles), :].astype(BF)
                pieces[r][kind, :, at : at + LANES] = part
                slices[p, kind, :, within : within + LANES] = part


def up_kernel(shards, scale, ids, tokens, *refs):
    pieces = refs[:-6]
    act_t, slope_t, down_t, up_w, down_w, up_t = refs[-6:]
    width, part = up_w.shape
    rows = width // shards

    @pl.when(pl.program_id(0) == 0)
    def _():
        def store(piece, shard):
            at = pl.multiple_of(shard * rows, rows)
            up_w[pl.ds(at, rows), :] = piece[0]
            down_w[pl.ds(at, rows), :] = piece[1]

        place_pieces(shards, ids, pieces, store)
        for i in range(width // LANES):
            span = slice(i * LANES, (i + 1) * LANES)
            up_t[:, span] = up_w[span, :].astype(F32).T.astype(BF)
            down_t[:, span] = down_w[span, :].astype(F32).T.astype(BF)

    u = lax.dot_general(up_t[...], tokens[...], NT, preferred_element_type=F32) * scale
    cdf = 0.5 * (1.0 + lax.erf(u * 0.7071067811865476))
    density = jnp.exp(-0.5 * u * u) * 0.3989422804014327
    act_t[...] = (u * cdf).astype(BF)
    slope_t[...] = (cdf + u * density).astype(BF)


def grad_kernel(shards, particles, up_scale, down_scale, back_scale, pick, ids, normed, act_t, slope_t, down_t, *refs):
    n_in = len(refs) - particles - 8
    sources, out = refs[:n_in], refs[n_in : n_in + particles]
    c, n, act, slope, grad, down, score, sems = refs[n_in + particles :]
    part, tokens = act.shape
    width = c.shape[1]
    chunk = tokens // shards
    first = [
        pltpu.make_async_copy(down_t, down, sems.at[1]),
        pltpu.make_async_copy(slope_t, slope, sems.at[2]),
    ]
    later = [
        pltpu.make_async_copy(act_t, act, sems.at[3]),
        pltpu.make_async_copy(normed, n, sems.at[4]),
    ]
    for copy in first:
        copy.start()
    pick(ids, sources, c, sems.at[0])
    for copy in later:
        copy.start()
    for copy in first:
        copy.wait()
    pltpu.make_async_copy(c, c, sems.at[0]).wait()

    def back(i, carry):
        at = pl.multiple_of(i * chunk, chunk)
        b = lax.dot_general(down[...], c[pl.ds(at, chunk), :], NT, preferred_element_type=F32)
        grad[:, pl.ds(at, chunk)] = (b * (slope[:, pl.ds(at, chunk)].astype(F32) * back_scale)).astype(BF)
        return carry

    lax.fori_loop(0, shards, back, 0)
    for copy in later:
        copy.wait()

    def gradient(j, carry):
        at = pl.multiple_of(j * BLOCK, BLOCK)
        g = jnp.dot(grad[...], n[:, pl.ds(at, BLOCK)], preferred_element_type=F32)
        score[0, pl.ds(at, BLOCK), :] = (g * up_scale).T.astype(BF)
        g = jnp.dot(act[...], c[:, pl.ds(at, BLOCK)], preferred_element_type=F32)
        score[1, pl.ds(at, BLOCK), :] = (g * down_scale).T.astype(BF)
        return carry

    lax.fori_loop(0, width // BLOCK, gradient, 0)
    rows = width // shards
    ratio = particles // shards
    cols = part // ratio
    mine = 2 * ids[COL] + ids[PROC]
    copies = []
    for t in range(particles):
        u = lax.rem(mine + ratio * ids[PIECE] - t + particles, particles)
        row = pl.multiple_of(lax.div(u, ratio) * rows, rows)
        col = pl.multiple_of(lax.rem(u, ratio) * cols, cols)
        copies.append(pltpu.make_async_copy(score.at[:, pl.ds(row, rows), pl.ds(col, cols)], out[t], sems.at[t]))
    run_copies(copies)


def distance_kernel(whole, out):
    particles, _, rows, cols = whole.shape
    pairs = [(i, j) for i in range(particles) for j in range(i)]
    tiles = cols // LANES

    def body(g, acc):
        kind = lax.div(g, rows // 16)
        row = pl.multiple_of(lax.rem(g, rows // 16) * 16, 16)
        for tile in range(tiles):
            w = [whole[p, kind, pl.ds(row, 16), tile * LANES : (tile + 1) * LANES].astype(F32) for p in range(particles)]
            new = []
            for a, (i, j) in zip(acc, pairs):
                d = w[i] - w[j]
                d = d * d
                new.append(a + (d[:8] + d[8:]))
            acc = tuple(new)
        return acc

    acc = lax.fori_loop(0, 2 * rows // 16, body, tuple(jnp.zeros((8, LANES), F32) for _ in pairs))
    lane = lax.broadcasted_iota(jnp.int32, (8, LANES), 1)
    row = jnp.zeros((8, LANES), F32)
    for i, a in enumerate(acc):
        total = jnp.sum(jnp.sum(a, axis=0, keepdims=True), axis=1, keepdims=True)
        row = row + jnp.where(lane == i, total, 0.0)
    out[...] = row


def stein_kernel(shards, particles, ids, coef, whole, *refs):
    sources, out = refs[:particles], refs[particles : 2 * particles]
    scores, field, pushed, sems = refs[2 * particles :]
    columns = particles // 2
    ratio = particles // shards
    _, _, rows, cols = whole.shape
    e = slice_index(ids, ids[COL], ids[CORE], ids[SHARD], columns)
    u = ids[SHARD] * ratio + lax.rem(e, ratio) + particles * shards - ratio * lax.div(e, ratio)
    run_copies(
        [pltpu.make_async_copy(sources[t], scores.at[lax.rem(u + t, particles)], sems.at[t]) for t in range(particles)]
    )
    repulse = coef[particles * particles + particles]
    chunk = min(rows, 64)
    groups = rows // chunk
    tiles = cols // LANES

    def body(g, carry):
        kind = lax.div(g, groups)
        row = pl.multiple_of(lax.rem(g, groups) * chunk, chunk)
        for tile in range(tiles):
            at = (kind, pl.ds(row, chunk), slice(tile * LANES, (tile + 1) * LANES))
            for p in range(particles):
                pushed[p] = scores[(p,) + at].astype(F32) - repulse * whole[(p,) + at].astype(F32)
            for i in range(particles):
                total = coef[particles * particles + i] * whole[(i,) + at].astype(F32)
                for j in range(particles):
                    total = total + coef[i * particles + j] * pushed[j]
                field[(i,) + at] = total.astype(BF)
        return carry

    lax.fori_loop(0, 2 * groups, body, 0)
    copies = []
    for k in range(columns):
        for x in range(2):
            column = lax.rem(ids[COL] + k, columns)
            core = ids[CORE] if x == 0 else 1 - ids[CORE]
            i = 2 * k + x
            copies.append(pltpu.make_async_copy(field.at[2 * column + core], out[i], sems.at[i]))
    run_copies(copies)


def adam_kernel(particles, ids, w, first, second, *refs):
    sources = refs[:particles]
    new_w, new_first, new_second, transport, field, sems = refs[particles:]
    columns = particles // 2
    _, _, hidden = field.shape
    width = hidden // particles
    step = pl.program_id(0)

    @pl.when(step == 0)
    def _():
        copies = []
        for k in range(columns):
            for x in range(2):
                column = lax.rem(ids[COL] - k + columns, columns)
                core = ids[CORE] if x == 0 else 1 - ids[CORE]
                at = pl.multiple_of(slice_index(ids, column, core, ids[SHARD], columns) * width, width)
                i = 2 * k + x
                copies.append(pltpu.make_async_copy(sources[i], field.at[:, :, pl.ds(at, width)], sems.at[i]))
        run_copies(copies)

    lane_tiles = hidden // LANES
    rows = w.shape[0] // (2 * lane_tiles)
    base = pl.multiple_of(step * rows, rows)
    for kind in range(2):
        for tile in range(lane_tiles):
            part = field[kind, pl.ds(base, rows), tile * LANES : (tile + 1) * LANES]
            transport[pl.ds(2 * tile + kind, rows, stride=2 * lane_tiles), :] = part.astype(F32)
    t = transport[...]
    m = first[...] - 0.1 * t
    v = second[...] + 0.001 * t * t
    new_first[...] = m
    new_second[...] = v
    new_w[...] = w[...] - 0.01 * m / (jnp.sqrt(v) + 1e-08)


def local(pool, batch_index, kernel_scale, cotangent, weights, first_moment, second_moment):
    shards = lax.axis_size("shard")
    particles = lax.axis_size("particle")
    columns, half = particles // 2, shards // 2
    tok_rows = batch_index.shape[0]
    width = pool.shape[1]
    _, rows, _, hidden = weights.shape
    part, cols = hidden // shards, hidden // particles
    tokens = tok_rows * shards
    blocks = tokens // BLOCK
    lane_tiles = hidden // LANES

    own = lax.axis_index("particle")
    shard = lax.axis_index("shard")
    core, column = own % 2, own // 2
    proc = shard // half
    piece = 2 * (shard % half) + core
    ids = jnp.stack([column, core, shard, proc, piece]).astype(jnp.int32)
    devices = [(m, c, s) for m in range(columns) for c in range(2) for s in range(shards)]

    def dev(m, c, s):
        return (2 * (m % columns) + c) * shards + s

    def move(x, pairs):
        if all(a == b for a, b in pairs) and len(pairs) == len(devices):
            return x
        return lax.ppermute(x, AXES, pairs)

    def swap_of(among):
        return [(dev(m, c, s), dev(m, 1 - c, s)) for m, c, s in devices if s in among]

    def flat(x):
        return x[0].reshape(rows, 2, lane_tiles, LANES).transpose(0, 2, 1, 3).reshape(-1, LANES)

    def unflat(x):
        return x.reshape(rows, lane_tiles, 2, LANES).transpose(0, 2, 1, 3).reshape(1, rows, 2, hidden)

    everyone = range(shards)
    half_rows = tok_rows // 2
    share = tok_rows // particles
    index = lax.dynamic_slice(batch_index, (own * share,), (share,))
    picked = jnp.take(pool, index, axis=0).astype(F32)
    normed = (picked * lax.rsqrt(jnp.mean(picked * picked, axis=1, keepdims=True) + 1e-06)).astype(BF)

    def shift_tokens(x):
        shifted = [[(dev(m, c, s), dev(m, c, (s + k) % shards)) for m, c, s in devices] for k in range(shards)]
        return jnp.stack([move(x, pairs) for pairs in shifted])

    w_flat = flat(weights)
    steps = max(rows // 64, 1)
    lines = w_flat.shape[0] // steps
    *prepared, slices = pl.pallas_call(
        functools.partial(prep_kernel, shards),
        grid=(steps,),
        out_shape=[jax.ShapeDtypeStruct((2, rows, part), BF)] * shards
        + [jax.ShapeDtypeStruct((particles, 2, rows, cols), BF)],
        in_specs=[smem_spec(), pl.BlockSpec((lines, LANES), lambda i: (i, 0))],
        out_specs=[pl.BlockSpec((2, rows // steps, part), lambda i: (0, i, 0))] * shards
        + [pl.BlockSpec((particles, 2, rows // steps, cols), lambda i: (0, 0, i, 0))],
        compiler_params=params(56),
        name="prep",
    )(ids, w_flat)

    w_routes = []
    if shards == 4:
        for own, far_by in ((True, 1), (False, 3), (None, 2)):
            for e in range(2):
                pairs = []
                for m, c, s in devices:
                    at_home = c == s // half
                    if own is None and at_home:
                        pairs.append((dev(m, c, s), dev(m, 1 - e, s)))
                    elif own is None or own == at_home:
                        pairs.append((dev(m, c, s), dev(m, e, s ^ far_by)))
                w_routes.append(pairs)
    else:
        for r in range(shards):
            pairs = []
            for m, c, s in devices:
                q = (s - r) % shards
                pairs.append((dev(m, c, s), dev(m, q % 2, c * half + q // 2)))
            w_routes.append(pairs)

    whole = lax.all_to_all(slices, "particle", 0, 0, tiled=True)

    pair_list = [(i, j) for i in range(particles) for j in range(i)]
    hops = []
    for count, stride in ((particles, shards), (shards, 1)):
        hop = 1
        while hop < count:
            hops.append([(d, d + ((d // stride % count ^ hop) - d // stride % count) * stride) for d in range(len(devices))])
            hop *= 2

    def pair_sums(whole):
        return pl.pallas_call(
            distance_kernel,
            out_shape=jax.ShapeDtypeStruct((8, LANES), F32),
            in_specs=[pl.BlockSpec(memory_space=pltpu.VMEM)],
            out_specs=pl.BlockSpec(memory_space=pltpu.VMEM),
            compiler_params=params(8),
                name="distances",
        )(whole)

    def add_over(sums, steps):
        for step in steps:
            sums = sums + move(sums, hops[step])
        return sums

    def gather_row(ids, which, turn):
        k = lax.rem(ids[SHARD] - which + shards, shards)
        return (turn * (particles // 2) * shards + k) * share

    def place(ids, ref, held, sem, which, turn, start=0):
        row = gather_row(ids, which, turn)
        for i in range(particles // 2):
            to = pl.multiple_of(row + i * shards * share, share)
            pltpu.make_async_copy(
                ref.at[pl.ds(start + i * share, share), :], held.at[pl.ds(to, share), :], sem
            ).start()

    if shards == 4:
        cot = cotangent[0]
        inner = jnp.logical_or(shard == 1, shard == 2)
        flip = jnp.where(jnp.logical_or(inner, core == proc), 0, 1)
        first_routes, second_routes = [], []
        for e in range(2):
            one, two = [], []
            for m, c, s in devices:
                at_home, is_inner = c == s // half, s in (1, 2)
                if not at_home:
                    to, turn = (3 - s, e) if is_inner else (1 if s == 3 else 2, 1 - e)
                    one.append((dev(m, c, s), dev(m, c ^ turn, to)))
                elif is_inner:
                    one.append((dev(m, c, s), dev(m, c ^ e, s ^ 1)))
                else:
                    two.append((dev(m, c, s), dev(m, c ^ e, s ^ 1)))
                if is_inner:
                    two.append((dev(m, c, s), dev(m, c, s ^ 1)))
            first_routes.append(one)
            second_routes.append(two)
        halves = [
            lax.dynamic_slice(cot, (((core + e + flip) % 2) * half_rows, 0), (half_rows, width)) for e in range(2)
        ]
        alpha = [move(x, route) for x, route in zip(halves, first_routes)]
        own_c = move(cot, [(dev(m, c, s), dev(m, 1 - c, s)) for m, c, s in devices if c == s // half])
        normed = shift_tokens(normed)
        w_pieces = [move(x, route) for x, route in zip(prepared[:2], w_routes[:2])]
        alpha, own_c, prepared, normed, w_pieces = lax.optimization_barrier((alpha, own_c, prepared, normed, w_pieces))
        normed = lax.all_gather(normed[None], "particle", axis=0, tiled=True)
        w_pieces = w_pieces + [move(x, route) for x, route in zip(prepared, w_routes[2:])]
        beta = [move(jnp.where(inner, a, x), route) for a, x, route in zip(alpha, halves, second_routes)]
        alpha_x = [move(x, swap_of(everyone)) for x in alpha]
        whole, w_pieces[2:5] = lax.optimization_barrier((whole, w_pieces[2:5]))
        sums = add_over(pair_sums(whole), range(len(hops) - 2))
        w_pieces, normed, sums = lax.optimization_barrier((w_pieces, normed, sums))
        beta_x = [move(x, swap_of(everyone)) for x in beta]
        sources = [cot, own_c, *alpha, *alpha_x, *beta, *beta_x]

        def pick(ids, refs, held, sem):
            s, core, proc = ids[SHARD], ids[CORE], ids[PROC]
            low = s < 2
            near, far, pair = jnp.where(low, 2, 1), jnp.where(low, 3, 0), s + 1 - 2 * lax.rem(s, 2)
            side = lax.rem(core + proc, 2)
            is_inner = jnp.logical_or(s == 1, s == 2)

            def own(ref):
                for turn in range(2):
                    place(ids, ref, held, sem, s, turn, turn * half_rows)

            def others(main, main_x, rest, rest_x):
                for e in range(2):
                    same = side == e
                    place(ids, main[e], held, sem, jnp.where(same, near, far), core)
                    place(ids, main_x[e], held, sem, jnp.where(same, far, near), 1 - core)

                    @pl.when(same)
                    def _():
                        place(ids, rest[e], held, sem, pair, core)
                        place(ids, rest_x[1 - e], held, sem, pair, 1 - core)

            @pl.when(side == 0)
            def _():
                own(refs[0])

            @pl.when(side == 1)
            def _():
                own(refs[1])

            @pl.when(is_inner)
            def _():
                others(refs[2:4], refs[4:6], refs[6:8], refs[8:10])

            @pl.when(jnp.logical_not(is_inner))
            def _():
                others(refs[6:8], refs[8:10], refs[2:4], refs[4:6])
    else:
        full = lax.all_gather(cotangent[0], "shard", axis=0, tiled=True)
        sources = [jnp.where(core == proc, full, move(full, swap_of(everyone)))]
        w_pieces = [move(x, route) for x, route in zip(prepared, w_routes)]
        normed = lax.all_gather(shift_tokens(normed)[None], "particle", axis=0, tiled=True)
        sums = add_over(pair_sums(whole), range(len(hops) - 2))

        def pick(ids, refs, held, sem):
            def one(which, carry):
                for turn in range(2):
                    start = pl.multiple_of(which * tok_rows + turn * half_rows, half_rows)
                    place(ids, refs[0], held, sem, which, turn, start)
                return carry

            lax.fori_loop(0, shards, one, 0)

    normed = normed.reshape(tokens, width)
    act_t, slope_t, down_t = pl.pallas_call(
        functools.partial(up_kernel, shards, width ** (-0.5)),
        grid=(blocks,),
        out_shape=[
            jax.ShapeDtypeStruct((part, tokens), BF),
            jax.ShapeDtypeStruct((part, tokens), BF),
            jax.ShapeDtypeStruct((part, width), BF),
        ],
        in_specs=[smem_spec(), pl.BlockSpec((BLOCK, width), lambda i: (i, 0))]
        + [pl.BlockSpec((2, rows, part), lambda i: (0, 0, 0))] * len(w_pieces),
        out_specs=[
            pl.BlockSpec((part, BLOCK), lambda i: (0, i)),
            pl.BlockSpec((part, BLOCK), lambda i: (0, i)),
            pl.BlockSpec((part, width), lambda i: (0, 0)),
        ],
        scratch_shapes=[pltpu.VMEM((width, part), BF), pltpu.VMEM((width, part), BF), pltpu.VMEM((part, width), BF)],
        compiler_params=params(56),
        name="up",
    )(ids, normed, *w_pieces)

    sums = add_over(sums, [-2])
    sums, act_t, slope_t = lax.optimization_barrier((sums, act_t, slope_t))
    grad_scale = 1.0 / (tokens * width)
    scores = pl.pallas_call(
        functools.partial(
            grad_kernel,
            shards,
            particles,
            -(width ** (-0.5)) * grad_scale,
            -(hidden ** (-0.5)) * grad_scale,
            hidden ** (-0.5),
            pick,
        ),
        out_shape=[jax.ShapeDtypeStruct((2, rows, cols), BF)] * particles,
        in_specs=[smem_spec()] + [any_spec()] * (4 + len(sources)),
        out_specs=[any_spec()] * particles,
        scratch_shapes=[
            pltpu.VMEM((tokens, width), BF),
            pltpu.VMEM((tokens, width), BF),
            pltpu.VMEM((part, tokens), BF),
            pltpu.VMEM((part, tokens), BF),
            pltpu.VMEM((part, tokens), BF),
            pltpu.VMEM((part, width), BF),
            pltpu.VMEM((2, width, part), BF),
            pltpu.SemaphoreType.DMA((particles + 5,)),
        ],
        compiler_params=params(56),
        name="grads",
    )(ids, normed, act_t, slope_t, down_t, *sources)

    sums = add_over(sums, [-1])
    sums, *scores = lax.optimization_barrier((sums, *scores))

    ratio = particles // shards
    arrived = []
    for t in range(particles):
        pairs = []
        for m, c, s in devices:
            mine, q = 2 * m + s // half, 2 * (s % half) + c
            u = (mine + ratio * q - t) % particles
            z, e = u // ratio, q * ratio + u % ratio
            pairs.append((dev(m, c, s), dev(e // 2 + z, e % 2, z)))
        arrived.append(move(scores[t], pairs))

    first_moment, second_moment, sums, *arrived[:5] = lax.optimization_barrier(
        (flat(first_moment), flat(second_moment), sums, *arrived[:5])
    )
    first_moment, second_moment = 0.9 * first_moment, 0.999 * second_moment
    sums = sums[0]
    lookup = [
        [pair_list.index((max(i, j), min(i, j))) if i != j else len(pair_list) for j in range(particles)]
        for i in range(particles)
    ]
    table = jnp.concatenate([sums[: len(pair_list)], jnp.zeros((1,), F32)])
    distances = table[jnp.array(lookup, jnp.int32)]
    inverse_band = 1.0 / kernel_scale[0].astype(F32)
    repulse = 2.0 * inverse_band
    kernel = jnp.exp(-distances * inverse_band)
    scale = 2 * width * hidden / particles
    coef = jnp.concatenate(
        [(scale * kernel).reshape(-1), scale * repulse * jnp.sum(kernel, axis=1), repulse[None]]
    )

    fields = pl.pallas_call(
        functools.partial(stein_kernel, shards, particles),
        out_shape=[jax.ShapeDtypeStruct((2, rows, cols), BF)] * particles,
        in_specs=[smem_spec(), smem_spec(), pl.BlockSpec(memory_space=pltpu.VMEM)] + [any_spec()] * particles,
        out_specs=[any_spec()] * particles,
        scratch_shapes=[
            pltpu.VMEM((particles, 2, rows, cols), BF),
            pltpu.VMEM((particles, 2, rows, cols), BF),
            pltpu.VMEM((particles, min(rows, 64), LANES), F32),
            pltpu.SemaphoreType.DMA((particles,)),
        ],
        compiler_params=params(12),
        name="stein",
    )(ids, coef, whole, *arrived)

    back = []
    for k in range(columns):
        for x in range(2):
            pairs = [(dev(m, c, s), dev(m + k, c ^ x, s)) for m, c, s in devices]
            back.append(move(fields[2 * k + x], pairs))

    steps = max(rows // 32, 1)
    flat_rows = rows * 2 * lane_tiles
    state_spec = pl.BlockSpec((flat_rows // steps, LANES), lambda i: (i, 0))
    outs = pl.pallas_call(
        functools.partial(adam_kernel, particles),
        grid=(steps,),
        out_shape=[jax.ShapeDtypeStruct((flat_rows, LANES), F32)] * 4,
        in_specs=[smem_spec()] + [state_spec] * 3 + [any_spec()] * particles,
        out_specs=[state_spec] * 4,
        scratch_shapes=[pltpu.VMEM((2, rows, hidden), BF), pltpu.SemaphoreType.DMA((particles,))],
        compiler_params=params(20),
        name="adam",
    )(ids, w_flat, first_moment, second_moment, *back)
    return tuple(unflat(x) for x in outs)


def solution(mesh):
    state = P("particle", "shard", None, None)
    return jax.shard_map(
        local,
        mesh=mesh,
        in_specs=(P("shard", None), P("shard"), P(), P("particle", "shard", None), state, state, state),
        out_specs=(state, state, state, state),
        check_vma=False,
    )
```

```python
import functools

import jax
import jax.numpy as jnp
from jax import lax
from jax.experimental import pallas as pl
from jax.experimental.pallas import tpu as pltpu
from jax.sharding import PartitionSpec as P

BF = jnp.bfloat16
F32 = jnp.float32
AXES = ("particle", "shard")
LANES = 128
BLOCK = 256
MIB = 1024 * 1024

COL, CORE, SHARD, PROC, PIECE = range(5)


def any_spec():
    return pl.BlockSpec(memory_space=pl.ANY)


def smem_spec():
    return pl.BlockSpec(memory_space=pltpu.SMEM)


def params(mib):
    return pltpu.CompilerParams(vmem_limit_bytes=mib * MIB)


def run_copies(copies):
    for copy in copies:
        copy.start()
    for copy in copies:
        copy.wait()


def slice_index(ids, column, core, shard, columns):
    return 2 * lax.rem(column - shard + columns * 16, columns) + core


def sent_piece(shards, ids, r):
    if shards != 4:
        return lax.rem(ids[SHARD] - r + shards, shards)
    side = lax.rem(ids[SHARD], 2)
    if r < 2:
        return 2 * (1 - side) + r
    away = lax.rem(ids[PROC] + ids[CORE], 2)
    return 2 * side + lax.rem(r + 1 - away, 2)


def place_pieces(shards, ids, pieces, store):
    if shards != 4:
        for r in range(shards):
            store(pieces[r], lax.rem(ids[PIECE] + r, shards))
        return
    s = ids[SHARD]
    beside = s + 1 - 2 * lax.rem(s, 2)
    across = lax.rem(s + 2, 4)
    for e in range(2):

        @pl.when(ids[CORE] == e)
        def _():
            store(pieces[e], beside)
            store(pieces[2 + e], 3 - s)
            store(pieces[4 + e], across)
            store(pieces[5 - e], s)


def prep_kernel(shards, ids, w, *out):
    pieces, slices = out[:shards], out[shards]
    _, rows, piece = pieces[0].shape
    particles, _, _, cols = slices.shape
    columns = particles // 2
    tiles, per_slice = piece // LANES, cols // LANES
    for r in range(shards):
        q = sent_piece(shards, ids, r)
        for j in range(tiles):
            e = q * (tiles // per_slice) + j // per_slice
            column = lax.rem(lax.div(e, 2) + ids[SHARD], columns)
            p = 2 * column + lax.rem(e, 2)
            at, within = j * LANES, j % per_slice * LANES
            for kind in range(2):
                line = 2 * (q * tiles + j) + kind
                part = w[pl.ds(line, rows, stride=2 * shards * tiles), :].astype(BF)
                pieces[r][kind, :, at : at + LANES] = part
                slices[p, kind, :, within : within + LANES] = part


def up_kernel(shards, scale, ids, tokens, *refs):
    pieces = refs[:-4]
    act_t, slope, down_w, up_w = refs[-4:]
    width, part = up_w.shape
    rows = width // shards

    @pl.when(pl.program_id(0) == 0)
    def _():
        def store(piece, shard):
            at = pl.multiple_of(shard * rows, rows)
            up_w[pl.ds(at, rows), :] = piece[0]
            down_w[pl.ds(at, rows), :] = piece[1]

        place_pieces(shards, ids, pieces, store)

    u = jnp.dot(tokens[...], up_w[...], preferred_element_type=F32) * scale
    cdf = 0.5 * (1.0 + lax.erf(u * 0.7071067811865476))
    density = jnp.exp(-0.5 * u * u) * 0.3989422804014327
    act_t[...] = (u * cdf).astype(BF).T
    slope[...] = (cdf + u * density).astype(BF)


def grad_kernel(shards, particles, up_scale, down_scale, back_scale, pick, ids, normed, act_t, slope_rows, down_w, *refs):
    n_in = len(refs) - particles - 8
    sources, out = refs[:n_in], refs[n_in : n_in + particles]
    c, n, act, slope, grad, down, score, sems = refs[n_in + particles :]
    part, tokens = act.shape
    width = c.shape[1]
    chunk = tokens // shards
    first = [
        pltpu.make_async_copy(down_w, down, sems.at[1]),
        pltpu.make_async_copy(slope_rows, slope, sems.at[2]),
    ]
    later = [
        pltpu.make_async_copy(act_t, act, sems.at[3]),
        pltpu.make_async_copy(normed, n, sems.at[4]),
    ]
    for copy in first:
        copy.start()
    pick(ids, sources, c, sems.at[0])
    for copy in later:
        copy.start()
    for copy in first:
        copy.wait()
    pltpu.make_async_copy(c, c, sems.at[0]).wait()

    def back(i, carry):
        at = pl.multiple_of(i * chunk, chunk)
        b = jnp.dot(c[pl.ds(at, chunk), :], down[...], preferred_element_type=F32)
        b = (b * (slope[pl.ds(at, chunk), :].astype(F32) * back_scale)).astype(BF)
        grad[:, pl.ds(at, chunk)] = b.T
        return carry

    lax.fori_loop(0, shards, back, 0)
    for copy in later:
        copy.wait()

    def gradient(j, carry):
        at = pl.multiple_of(j * BLOCK, BLOCK)
        g = jnp.dot(grad[...], n[:, pl.ds(at, BLOCK)], preferred_element_type=F32)
        score[0, pl.ds(at, BLOCK), :] = (g * up_scale).T.astype(BF)
        g = jnp.dot(act[...], c[:, pl.ds(at, BLOCK)], preferred_element_type=F32)
        score[1, pl.ds(at, BLOCK), :] = (g * down_scale).T.astype(BF)
        return carry

    lax.fori_loop(0, width // BLOCK, gradient, 0)
    rows = width // shards
    ratio = particles // shards
    cols = part // ratio
    mine = 2 * ids[COL] + ids[PROC]
    copies = []
    for t in range(particles):
        u = lax.rem(mine + ratio * ids[PIECE] - t + particles, particles)
        row = pl.multiple_of(lax.div(u, ratio) * rows, rows)
        col = pl.multiple_of(lax.rem(u, ratio) * cols, cols)
        copies.append(pltpu.make_async_copy(score.at[:, pl.ds(row, rows), pl.ds(col, cols)], out[t], sems.at[t]))
    run_copies(copies)


def distance_kernel(whole, out):
    particles, _, rows, cols = whole.shape
    pairs = [(i, j) for i in range(particles) for j in range(i)]
    tiles = cols // LANES

    def body(g, acc):
        kind = lax.div(g, rows // 16)
        row = pl.multiple_of(lax.rem(g, rows // 16) * 16, 16)
        for tile in range(tiles):
            w = [whole[p, kind, pl.ds(row, 16), tile * LANES : (tile + 1) * LANES].astype(F32) for p in range(particles)]
            new = []
            for a, (i, j) in zip(acc, pairs):
                d = w[i] - w[j]
                d = d * d
                new.append(a + (d[:8] + d[8:]))
            acc = tuple(new)
        return acc

    acc = lax.fori_loop(0, 2 * rows // 16, body, tuple(jnp.zeros((8, LANES), F32) for _ in pairs))
    lane = lax.broadcasted_iota(jnp.int32, (8, LANES), 1)
    row = jnp.zeros((8, LANES), F32)
    for i, a in enumerate(acc):
        total = jnp.sum(jnp.sum(a, axis=0, keepdims=True), axis=1, keepdims=True)
        row = row + jnp.where(lane == i, total, 0.0)
    out[...] = row


def stein_kernel(shards, particles, ids, coef, whole, *refs):
    sources, out = refs[:particles], refs[particles : 2 * particles]
    scores, field, pushed, sems = refs[2 * particles :]
    columns = particles // 2
    ratio = particles // shards
    _, _, rows, cols = whole.shape
    e = slice_index(ids, ids[COL], ids[CORE], ids[SHARD], columns)
    u = ids[SHARD] * ratio + lax.rem(e, ratio) + particles * shards - ratio * lax.div(e, ratio)
    run_copies(
        [pltpu.make_async_copy(sources[t], scores.at[lax.rem(u + t, particles)], sems.at[t]) for t in range(particles)]
    )
    repulse = coef[particles * particles + particles]
    chunk = min(rows, 64)
    groups = rows // chunk
    tiles = cols // LANES

    def body(g, carry):
        kind = lax.div(g, groups)
        row = pl.multiple_of(lax.rem(g, groups) * chunk, chunk)
        for tile in range(tiles):
            at = (kind, pl.ds(row, chunk), slice(tile * LANES, (tile + 1) * LANES))
            for p in range(particles):
                pushed[p] = scores[(p,) + at].astype(F32) - repulse * whole[(p,) + at].astype(F32)
            for i in range(particles):
                total = coef[particles * particles + i] * whole[(i,) + at].astype(F32)
                for j in range(particles):
                    total = total + coef[i * particles + j] * pushed[j]
                field[(i,) + at] = total.astype(BF)
        return carry

    lax.fori_loop(0, 2 * groups, body, 0)
    copies = []
    for k in range(columns):
        for x in range(2):
            column = lax.rem(ids[COL] + k, columns)
            core = ids[CORE] if x == 0 else 1 - ids[CORE]
            i = 2 * k + x
            copies.append(pltpu.make_async_copy(field.at[2 * column + core], out[i], sems.at[i]))
    run_copies(copies)


def adam_kernel(particles, ids, w, first, second, *refs):
    sources = refs[:particles]
    new_w, new_first, new_second, transport, field, sems = refs[particles:]
    columns = particles // 2
    _, _, hidden = field.shape
    width = hidden // particles
    step = pl.program_id(0)

    @pl.when(step == 0)
    def _():
        copies = []
        for k in range(columns):
            for x in range(2):
                column = lax.rem(ids[COL] - k + columns, columns)
                core = ids[CORE] if x == 0 else 1 - ids[CORE]
                at = pl.multiple_of(slice_index(ids, column, core, ids[SHARD], columns) * width, width)
                i = 2 * k + x
                copies.append(pltpu.make_async_copy(sources[i], field.at[:, :, pl.ds(at, width)], sems.at[i]))
        run_copies(copies)

    lane_tiles = hidden // LANES
    rows = w.shape[0] // (2 * lane_tiles)
    base = pl.multiple_of(step * rows, rows)
    for kind in range(2):
        for tile in range(lane_tiles):
            part = field[kind, pl.ds(base, rows), tile * LANES : (tile + 1) * LANES]
            transport[pl.ds(2 * tile + kind, rows, stride=2 * lane_tiles), :] = part.astype(F32)
    t = transport[...]
    m = first[...] - 0.1 * t
    v = second[...] + 0.001 * t * t
    new_first[...] = m
    new_second[...] = v
    new_w[...] = w[...] - 0.01 * m / (jnp.sqrt(v) + 1e-08)


def local(pool, batch_index, kernel_scale, cotangent, weights, first_moment, second_moment):
    shards = lax.axis_size("shard")
    particles = lax.axis_size("particle")
    columns, half = particles // 2, shards // 2
    tok_rows = batch_index.shape[0]
    width = pool.shape[1]
    _, rows, _, hidden = weights.shape
    part, cols = hidden // shards, hidden // particles
    tokens = tok_rows * shards
    blocks = tokens // BLOCK
    lane_tiles = hidden // LANES

    own = lax.axis_index("particle")
    shard = lax.axis_index("shard")
    core, column = own % 2, own // 2
    proc = shard // half
    piece = 2 * (shard % half) + core
    ids = jnp.stack([column, core, shard, proc, piece]).astype(jnp.int32)
    devices = [(m, c, s) for m in range(columns) for c in range(2) for s in range(shards)]

    def dev(m, c, s):
        return (2 * (m % columns) + c) * shards + s

    def move(x, pairs):
        if all(a == b for a, b in pairs) and len(pairs) == len(devices):
            return x
        return lax.ppermute(x, AXES, pairs)

    def swap_of(among):
        return [(dev(m, c, s), dev(m, 1 - c, s)) for m, c, s in devices if s in among]

    def flat(x):
        return x[0].reshape(rows, 2, lane_tiles, LANES).transpose(0, 2, 1, 3).reshape(-1, LANES)

    def unflat(x):
        return x.reshape(rows, lane_tiles, 2, LANES).transpose(0, 2, 1, 3).reshape(1, rows, 2, hidden)

    everyone = range(shards)
    half_rows = tok_rows // 2
    share = tok_rows // particles
    index = lax.dynamic_slice(batch_index, (own * share,), (share,))
    picked = jnp.take(pool, index, axis=0).astype(F32)
    normed = (picked * lax.rsqrt(jnp.mean(picked * picked, axis=1, keepdims=True) + 1e-06)).astype(BF)

    def shift_tokens(x):
        shifted = [[(dev(m, c, s), dev(m, c, (s + k) % shards)) for m, c, s in devices] for k in range(shards)]
        return jnp.stack([move(x, pairs) for pairs in shifted])

    w_flat = flat(weights)
    steps = max(rows // 64, 1)
    lines = w_flat.shape[0] // steps
    *prepared, slices = pl.pallas_call(
        functools.partial(prep_kernel, shards),
        grid=(steps,),
        out_shape=[jax.ShapeDtypeStruct((2, rows, part), BF)] * shards
        + [jax.ShapeDtypeStruct((particles, 2, rows, cols), BF)],
        in_specs=[smem_spec(), pl.BlockSpec((lines, LANES), lambda i: (i, 0))],
        out_specs=[pl.BlockSpec((2, rows // steps, part), lambda i: (0, i, 0))] * shards
        + [pl.BlockSpec((particles, 2, rows // steps, cols), lambda i: (0, 0, i, 0))],
        compiler_params=params(56),
        name="prep",
    )(ids, w_flat)

    w_routes = []
    if shards == 4:
        for own, far_by in ((True, 1), (False, 3), (None, 2)):
            for e in range(2):
                pairs = []
                for m, c, s in devices:
                    at_home = c == s // half
                    if own is None and at_home:
                        pairs.append((dev(m, c, s), dev(m, 1 - e, s)))
                    elif own is None or own == at_home:
                        pairs.append((dev(m, c, s), dev(m, e, s ^ far_by)))
                w_routes.append(pairs)
    else:
        for r in range(shards):
            pairs = []
            for m, c, s in devices:
                q = (s - r) % shards
                pairs.append((dev(m, c, s), dev(m, q % 2, c * half + q // 2)))
            w_routes.append(pairs)

    whole = lax.all_to_all(slices, "particle", 0, 0, tiled=True)

    pair_list = [(i, j) for i in range(particles) for j in range(i)]
    hops = []
    for count, stride in ((particles, shards), (shards, 1)):
        hop = 1
        while hop < count:
            hops.append([(d, d + ((d // stride % count ^ hop) - d // stride % count) * stride) for d in range(len(devices))])
            hop *= 2

    def pair_sums(whole):
        return pl.pallas_call(
            distance_kernel,
            out_shape=jax.ShapeDtypeStruct((8, LANES), F32),
            in_specs=[pl.BlockSpec(memory_space=pltpu.VMEM)],
            out_specs=pl.BlockSpec(memory_space=pltpu.VMEM),
            compiler_params=params(8),
                name="distances",
        )(whole)

    def add_over(sums, steps):
        for step in steps:
            sums = sums + move(sums, hops[step])
        return sums

    def gather_row(ids, which, turn):
        k = lax.rem(ids[SHARD] - which + shards, shards)
        return (turn * (particles // 2) * shards + k) * share

    def place(ids, ref, held, sem, which, turn, start=0):
        row = gather_row(ids, which, turn)
        for i in range(particles // 2):
            to = pl.multiple_of(row + i * shards * share, share)
            pltpu.make_async_copy(
                ref.at[pl.ds(start + i * share, share), :], held.at[pl.ds(to, share), :], sem
            ).start()

    if shards == 4:
        cot = cotangent[0]
        inner = jnp.logical_or(shard == 1, shard == 2)
        flip = jnp.where(jnp.logical_or(inner, core == proc), 0, 1)
        first_routes, second_routes = [], []
        for e in range(2):
            one, two = [], []
            for m, c, s in devices:
                at_home, is_inner = c == s // half, s in (1, 2)
                if not at_home:
                    to, turn = (3 - s, e) if is_inner else (1 if s == 3 else 2, 1 - e)
                    one.append((dev(m, c, s), dev(m, c ^ turn, to)))
                elif is_inner:
                    one.append((dev(m, c, s), dev(m, c ^ e, s ^ 1)))
                else:
                    two.append((dev(m, c, s), dev(m, c ^ e, s ^ 1)))
                if is_inner:
                    two.append((dev(m, c, s), dev(m, c, s ^ 1)))
            first_routes.append(one)
            second_routes.append(two)
        halves = [
            lax.dynamic_slice(cot, (((core + e + flip) % 2) * half_rows, 0), (half_rows, width)) for e in range(2)
        ]
        alpha = [move(x, route) for x, route in zip(halves, first_routes)]
        own_c = move(cot, [(dev(m, c, s), dev(m, 1 - c, s)) for m, c, s in devices if c == s // half])
        normed = shift_tokens(normed)
        w_pieces = [move(x, route) for x, route in zip(prepared[:2], w_routes[:2])]
        alpha, own_c, prepared, normed, w_pieces = lax.optimization_barrier((alpha, own_c, prepared, normed, w_pieces))
        normed = lax.all_gather(normed[None], "particle", axis=0, tiled=True)
        w_pieces = w_pieces + [move(x, route) for x, route in zip(prepared, w_routes[2:])]
        beta = [move(jnp.where(inner, a, x), route) for a, x, route in zip(alpha, halves, second_routes)]
        alpha_x = [move(x, swap_of(everyone)) for x in alpha]
        whole, w_pieces[2:5] = lax.optimization_barrier((whole, w_pieces[2:5]))
        sums = add_over(pair_sums(whole), range(len(hops) - 3))
        w_pieces, normed, sums = lax.optimization_barrier((w_pieces, normed, sums))
        beta_x = [move(x, swap_of(everyone)) for x in beta]
        sources = [cot, own_c, *alpha, *alpha_x, *beta, *beta_x]

        def pick(ids, refs, held, sem):
            s, core, proc = ids[SHARD], ids[CORE], ids[PROC]
            low = s < 2
            near, far, pair = jnp.where(low, 2, 1), jnp.where(low, 3, 0), s + 1 - 2 * lax.rem(s, 2)
            side = lax.rem(core + proc, 2)
            is_inner = jnp.logical_or(s == 1, s == 2)

            def own(ref):
                for turn in range(2):
                    place(ids, ref, held, sem, s, turn, turn * half_rows)

            def others(main, main_x, rest, rest_x):
                for e in range(2):
                    same = side == e
                    place(ids, main[e], held, sem, jnp.where(same, near, far), core)
                    place(ids, main_x[e], held, sem, jnp.where(same, far, near), 1 - core)

                    @pl.when(same)
                    def _():
                        place(ids, rest[e], held, sem, pair, core)
                        place(ids, rest_x[1 - e], held, sem, pair, 1 - core)

            @pl.when(side == 0)
            def _():
                own(refs[0])

            @pl.when(side == 1)
            def _():
                own(refs[1])

            @pl.when(is_inner)
            def _():
                others(refs[2:4], refs[4:6], refs[6:8], refs[8:10])

            @pl.when(jnp.logical_not(is_inner))
            def _():
                others(refs[6:8], refs[8:10], refs[2:4], refs[4:6])
    else:
        full = lax.all_gather(cotangent[0], "shard", axis=0, tiled=True)
        sources = [jnp.where(core == proc, full, move(full, swap_of(everyone)))]
        w_pieces = [move(x, route) for x, route in zip(prepared, w_routes)]
        normed = lax.all_gather(shift_tokens(normed)[None], "particle", axis=0, tiled=True)
        sums = add_over(pair_sums(whole), range(len(hops) - 3))

        def pick(ids, refs, held, sem):
            def one(which, carry):
                for turn in range(2):
                    start = pl.multiple_of(which * tok_rows + turn * half_rows, half_rows)
                    place(ids, refs[0], held, sem, which, turn, start)
                return carry

            lax.fori_loop(0, shards, one, 0)

    normed = normed.reshape(tokens, width)
    act_t, slope, down_w = pl.pallas_call(
        functools.partial(up_kernel, shards, width ** (-0.5)),
        grid=(blocks,),
        out_shape=[
            jax.ShapeDtypeStruct((part, tokens), BF),
            jax.ShapeDtypeStruct((tokens, part), BF),
            jax.ShapeDtypeStruct((width, part), BF),
        ],
        in_specs=[smem_spec(), pl.BlockSpec((BLOCK, width), lambda i: (i, 0))]
        + [pl.BlockSpec((2, rows, part), lambda i: (0, 0, 0))] * len(w_pieces),
        out_specs=[
            pl.BlockSpec((part, BLOCK), lambda i: (0, i)),
            pl.BlockSpec((BLOCK, part), lambda i: (i, 0)),
            pl.BlockSpec((width, part), lambda i: (0, 0)),
        ],
        scratch_shapes=[pltpu.VMEM((width, part), BF)],
        compiler_params=params(56),
        name="up",
    )(ids, normed, *w_pieces)

    sums = add_over(sums, [-3])
    sums, act_t, slope = lax.optimization_barrier((sums, act_t, slope))
    grad_scale = 1.0 / (tokens * width)
    scores = pl.pallas_call(
        functools.partial(
            grad_kernel,
            shards,
            particles,
            -(width ** (-0.5)) * grad_scale,
            -(hidden ** (-0.5)) * grad_scale,
            hidden ** (-0.5),
            pick,
        ),
        out_shape=[jax.ShapeDtypeStruct((2, rows, cols), BF)] * particles,
        in_specs=[smem_spec()] + [any_spec()] * (4 + len(sources)),
        out_specs=[any_spec()] * particles,
        scratch_shapes=[
            pltpu.VMEM((tokens, width), BF),
            pltpu.VMEM((tokens, width), BF),
            pltpu.VMEM((part, tokens), BF),
            pltpu.VMEM((tokens, part), BF),
            pltpu.VMEM((part, tokens), BF),
            pltpu.VMEM((width, part), BF),
            pltpu.VMEM((2, width, part), BF),
            pltpu.SemaphoreType.DMA((particles + 5,)),
        ],
        compiler_params=params(56),
        name="grads",
    )(ids, normed, act_t, slope, down_w, *sources)

    sums = add_over(sums, [-2])
    sums, *scores = lax.optimization_barrier((sums, *scores))

    ratio = particles // shards
    arrived = []
    for t in range(particles):
        pairs = []
        for m, c, s in devices:
            mine, q = 2 * m + s // half, 2 * (s % half) + c
            u = (mine + ratio * q - t) % particles
            z, e = u // ratio, q * ratio + u % ratio
            pairs.append((dev(m, c, s), dev(e // 2 + z, e % 2, z)))
        arrived.append(move(scores[t], pairs))

    sums = add_over(sums, [-1])
    first_moment, second_moment, sums, *arrived[:5] = lax.optimization_barrier(
        (flat(first_moment), flat(second_moment), sums, *arrived[:5])
    )
    first_moment, second_moment = 0.9 * first_moment, 0.999 * second_moment
    sums = sums[0]
    lookup = [
        [pair_list.index((max(i, j), min(i, j))) if i != j else len(pair_list) for j in range(particles)]
        for i in range(particles)
    ]
    table = jnp.concatenate([sums[: len(pair_list)], jnp.zeros((1,), F32)])
    distances = table[jnp.array(lookup, jnp.int32)]
    inverse_band = 1.0 / kernel_scale[0].astype(F32)
    repulse = 2.0 * inverse_band
    kernel = jnp.exp(-distances * inverse_band)
    scale = 2 * width * hidden / particles
    coef = jnp.concatenate(
        [(scale * kernel).reshape(-1), scale * repulse * jnp.sum(kernel, axis=1), repulse[None]]
    )

    fields = pl.pallas_call(
        functools.partial(stein_kernel, shards, particles),
        out_shape=[jax.ShapeDtypeStruct((2, rows, cols), BF)] * particles,
        in_specs=[smem_spec(), smem_spec(), pl.BlockSpec(memory_space=pltpu.VMEM)] + [any_spec()] * particles,
        out_specs=[any_spec()] * particles,
        scratch_shapes=[
            pltpu.VMEM((particles, 2, rows, cols), BF),
            pltpu.VMEM((particles, 2, rows, cols), BF),
            pltpu.VMEM((particles, min(rows, 64), LANES), F32),
            pltpu.SemaphoreType.DMA((particles,)),
        ],
        compiler_params=params(12),
        name="stein",
    )(ids, coef, whole, *arrived)

    back = []
    for k in range(columns):
        for x in range(2):
            pairs = [(dev(m, c, s), dev(m + k, c ^ x, s)) for m, c, s in devices]
            back.append(move(fields[2 * k + x], pairs))

    steps = max(rows // 32, 1)
    flat_rows = rows * 2 * lane_tiles
    state_spec = pl.BlockSpec((flat_rows // steps, LANES), lambda i: (i, 0))
    outs = pl.pallas_call(
        functools.partial(adam_kernel, particles),
        grid=(steps,),
        out_shape=[jax.ShapeDtypeStruct((flat_rows, LANES), F32)] * 4,
        in_specs=[smem_spec()] + [state_spec] * 3 + [any_spec()] * particles,
        out_specs=[state_spec] * 4,
        scratch_shapes=[pltpu.VMEM((2, rows, hidden), BF), pltpu.SemaphoreType.DMA((particles,))],
        compiler_params=params(20),
        name="adam",
    )(ids, w_flat, first_moment, second_moment, *back)
    return tuple(unflat(x) for x in outs)


def solution(mesh):
    state = P("particle", "shard", None, None)
    return jax.shard_map(
        local,
        mesh=mesh,
        in_specs=(P("shard", None), P("shard"), P(), P("particle", "shard", None), state, state, state),
        out_specs=(state, state, state, state),
        check_vma=False,
    )
```

```python
import functools

import jax
import jax.numpy as jnp
from jax import lax
from jax.experimental import pallas as pl
from jax.experimental.pallas import tpu as pltpu
from jax.sharding import PartitionSpec as P

BF = jnp.bfloat16
F32 = jnp.float32
AXES = ("particle", "shard")
LANES = 128
BLOCK = 256
MIB = 1024 * 1024

COL, CORE, SHARD, PROC, PIECE = range(5)


def any_spec():
    return pl.BlockSpec(memory_space=pl.ANY)


def smem_spec():
    return pl.BlockSpec(memory_space=pltpu.SMEM)


def params(mib):
    return pltpu.CompilerParams(vmem_limit_bytes=mib * MIB)


def run_copies(copies):
    for copy in copies:
        copy.start()
    for copy in copies:
        copy.wait()


def slice_index(ids, column, core, shard, columns):
    return 2 * lax.rem(column - shard + columns * 16, columns) + core


def sent_piece(shards, ids, r):
    if shards != 4:
        return lax.rem(ids[SHARD] - r + shards, shards)
    side = lax.rem(ids[SHARD], 2)
    if r < 2:
        return 2 * (1 - side) + r
    away = lax.rem(ids[PROC] + ids[CORE], 2)
    return 2 * side + lax.rem(r + 1 - away, 2)


def place_pieces(shards, ids, pieces, store):
    if shards != 4:
        for r in range(shards):
            store(pieces[r], lax.rem(ids[PIECE] + r, shards))
        return
    s = ids[SHARD]
    beside = s + 1 - 2 * lax.rem(s, 2)
    across = lax.rem(s + 2, 4)
    for e in range(2):

        @pl.when(ids[CORE] == e)
        def _():
            store(pieces[e], beside)
            store(pieces[2 + e], 3 - s)
            store(pieces[4 + e], across)
            store(pieces[5 - e], s)


def prep_kernel(shards, ids, w, *out):
    pieces, slices = out[:shards], out[shards]
    _, rows, piece = pieces[0].shape
    particles, _, _, cols = slices.shape
    columns = particles // 2
    tiles, per_slice = piece // LANES, cols // LANES
    for r in range(shards):
        q = sent_piece(shards, ids, r)
        for j in range(tiles):
            e = q * (tiles // per_slice) + j // per_slice
            column = lax.rem(lax.div(e, 2) + ids[SHARD], columns)
            p = 2 * column + lax.rem(e, 2)
            at, within = j * LANES, j % per_slice * LANES
            for kind in range(2):
                line = 2 * (q * tiles + j) + kind
                part = w[pl.ds(line, rows, stride=2 * shards * tiles), :].astype(BF)
                pieces[r][kind, :, at : at + LANES] = part
                slices[p, kind, :, within : within + LANES] = part


def up_kernel(shards, scale, ids, tokens, *refs):
    pieces = refs[:-4]
    act_t, slope, down_w, up_w = refs[-4:]
    width, part = up_w.shape
    rows = width // shards

    @pl.when(pl.program_id(0) == 0)
    def _():
        def store(piece, shard):
            at = pl.multiple_of(shard * rows, rows)
            up_w[pl.ds(at, rows), :] = piece[0]
            down_w[pl.ds(at, rows), :] = piece[1]

        place_pieces(shards, ids, pieces, store)

    u = jnp.dot(tokens[...], up_w[...], preferred_element_type=F32) * scale
    cdf = 0.5 * (1.0 + lax.erf(u * 0.7071067811865476))
    density = jnp.exp(-0.5 * u * u) * 0.3989422804014327
    act_t[...] = (u * cdf).astype(BF).T
    slope[...] = (cdf + u * density).astype(BF)


def grad_kernel(shards, particles, up_scale, down_scale, back_scale, pick, ids, normed, act_t, slope_rows, down_w, *refs):
    n_in = len(refs) - particles - 8
    sources, out = refs[:n_in], refs[n_in : n_in + particles]
    c, n, act, slope, grad, down, score, sems = refs[n_in + particles :]
    part, tokens = act.shape
    width = c.shape[1]
    chunk = tokens // shards
    first = [
        pltpu.make_async_copy(down_w, down, sems.at[1]),
        pltpu.make_async_copy(slope_rows, slope, sems.at[2]),
    ]
    later = [
        pltpu.make_async_copy(act_t, act, sems.at[3]),
        pltpu.make_async_copy(normed, n, sems.at[4]),
    ]
    for copy in first:
        copy.start()
    pick(ids, sources, c, sems.at[0])
    for copy in later:
        copy.start()
    for copy in first:
        copy.wait()
    pltpu.make_async_copy(c, c, sems.at[0]).wait()

    def back(i, carry):
        at = pl.multiple_of(i * chunk, chunk)
        b = jnp.dot(c[pl.ds(at, chunk), :], down[...], preferred_element_type=F32)
        b = (b * (slope[pl.ds(at, chunk), :].astype(F32) * back_scale)).astype(BF)
        grad[:, pl.ds(at, chunk)] = b.T
        return carry

    lax.fori_loop(0, shards, back, 0)
    for copy in later:
        copy.wait()

    def gradient(j, carry):
        at = pl.multiple_of(j * BLOCK, BLOCK)
        g = jnp.dot(grad[...], n[:, pl.ds(at, BLOCK)], preferred_element_type=F32)
        score[0, pl.ds(at, BLOCK), :] = (g * up_scale).T.astype(BF)
        g = jnp.dot(act[...], c[:, pl.ds(at, BLOCK)], preferred_element_type=F32)
        score[1, pl.ds(at, BLOCK), :] = (g * down_scale).T.astype(BF)
        return carry

    lax.fori_loop(0, width // BLOCK, gradient, 0)
    rows = width // shards
    ratio = particles // shards
    cols = part // ratio
    mine = 2 * ids[COL] + ids[PROC]
    copies = []
    for t in range(particles):
        u = lax.rem(mine + ratio * ids[PIECE] - t + particles, particles)
        row = pl.multiple_of(lax.div(u, ratio) * rows, rows)
        col = pl.multiple_of(lax.rem(u, ratio) * cols, cols)
        copies.append(pltpu.make_async_copy(score.at[:, pl.ds(row, rows), pl.ds(col, cols)], out[t], sems.at[t]))
    run_copies(copies)


def distance_kernel(whole, out):
    particles, _, rows, cols = whole.shape
    pairs = [(i, j) for i in range(particles) for j in range(i)]
    tiles = cols // LANES

    def body(g, acc):
        kind = lax.div(g, rows // 16)
        row = pl.multiple_of(lax.rem(g, rows // 16) * 16, 16)
        for tile in range(tiles):
            w = [whole[p, kind, pl.ds(row, 16), tile * LANES : (tile + 1) * LANES].astype(F32) for p in range(particles)]
            new = []
            for a, (i, j) in zip(acc, pairs):
                d = w[i] - w[j]
                d = d * d
                new.append(a + (d[:8] + d[8:]))
            acc = tuple(new)
        return acc

    acc = lax.fori_loop(0, 2 * rows // 16, body, tuple(jnp.zeros((8, LANES), F32) for _ in pairs))
    lane = lax.broadcasted_iota(jnp.int32, (8, LANES), 1)
    row = jnp.zeros((8, LANES), F32)
    for i, a in enumerate(acc):
        total = jnp.sum(jnp.sum(a, axis=0, keepdims=True), axis=1, keepdims=True)
        row = row + jnp.where(lane == i, total, 0.0)
    out[...] = row


def stein_kernel(shards, particles, ids, coef, whole, *refs):
    sources, out = refs[:particles], refs[particles : 2 * particles]
    scores, field, pushed, sems = refs[2 * particles :]
    columns = particles // 2
    ratio = particles // shards
    _, _, rows, cols = whole.shape
    e = slice_index(ids, ids[COL], ids[CORE], ids[SHARD], columns)
    u = ids[SHARD] * ratio + lax.rem(e, ratio) + particles * shards - ratio * lax.div(e, ratio)
    run_copies(
        [pltpu.make_async_copy(sources[t], scores.at[lax.rem(u + t, particles)], sems.at[t]) for t in range(particles)]
    )
    repulse = coef[particles * particles + particles]
    chunk = min(rows, 64)
    groups = rows // chunk
    tiles = cols // LANES

    def body(g, carry):
        kind = lax.div(g, groups)
        row = pl.multiple_of(lax.rem(g, groups) * chunk, chunk)
        for tile in range(tiles):
            at = (kind, pl.ds(row, chunk), slice(tile * LANES, (tile + 1) * LANES))
            for p in range(particles):
                pushed[p] = scores[(p,) + at].astype(F32) - repulse * whole[(p,) + at].astype(F32)
            for i in range(particles):
                total = coef[particles * particles + i] * whole[(i,) + at].astype(F32)
                for j in range(particles):
                    total = total + coef[i * particles + j] * pushed[j]
                field[(i,) + at] = total.astype(BF)
        return carry

    lax.fori_loop(0, 2 * groups, body, 0)
    copies = []
    for k in range(columns):
        for x in range(2):
            column = lax.rem(ids[COL] + k, columns)
            core = ids[CORE] if x == 0 else 1 - ids[CORE]
            i = 2 * k + x
            copies.append(pltpu.make_async_copy(field.at[2 * column + core], out[i], sems.at[i]))
    run_copies(copies)


def adam_kernel(particles, ids, w, first, second, *refs):
    sources = refs[:particles]
    new_w, new_first, new_second, transport, field, sems = refs[particles:]
    columns = particles // 2
    _, _, hidden = field.shape
    width = hidden // particles
    step = pl.program_id(0)

    @pl.when(step == 0)
    def _():
        copies = []
        for k in range(columns):
            for x in range(2):
                column = lax.rem(ids[COL] - k + columns, columns)
                core = ids[CORE] if x == 0 else 1 - ids[CORE]
                at = pl.multiple_of(slice_index(ids, column, core, ids[SHARD], columns) * width, width)
                i = 2 * k + x
                copies.append(pltpu.make_async_copy(sources[i], field.at[:, :, pl.ds(at, width)], sems.at[i]))
        run_copies(copies)

    lane_tiles = hidden // LANES
    rows = w.shape[0] // (2 * lane_tiles)
    base = pl.multiple_of(step * rows, rows)
    for kind in range(2):
        for tile in range(lane_tiles):
            part = field[kind, pl.ds(base, rows), tile * LANES : (tile + 1) * LANES]
            transport[pl.ds(2 * tile + kind, rows, stride=2 * lane_tiles), :] = part.astype(F32)
    t = transport[...]
    m = first[...] - 0.1 * t
    v = second[...] + 0.001 * t * t
    new_first[...] = m
    new_second[...] = v
    new_w[...] = w[...] - 0.01 * m / (jnp.sqrt(v) + 1e-08)


def local(pool, batch_index, kernel_scale, cotangent, weights, first_moment, second_moment):
    shards = lax.axis_size("shard")
    particles = lax.axis_size("particle")
    columns, half = particles // 2, shards // 2
    tok_rows = batch_index.shape[0]
    width = pool.shape[1]
    _, rows, _, hidden = weights.shape
    part, cols = hidden // shards, hidden // particles
    tokens = tok_rows * shards
    blocks = tokens // BLOCK
    lane_tiles = hidden // LANES

    own = lax.axis_index("particle")
    shard = lax.axis_index("shard")
    core, column = own % 2, own // 2
    proc = shard // half
    piece = 2 * (shard % half) + core
    ids = jnp.stack([column, core, shard, proc, piece]).astype(jnp.int32)
    devices = [(m, c, s) for m in range(columns) for c in range(2) for s in range(shards)]

    def dev(m, c, s):
        return (2 * (m % columns) + c) * shards + s

    def move(x, pairs):
        if all(a == b for a, b in pairs) and len(pairs) == len(devices):
            return x
        return lax.ppermute(x, AXES, pairs)

    def swap_of(among):
        return [(dev(m, c, s), dev(m, 1 - c, s)) for m, c, s in devices if s in among]

    def flat(x):
        return x[0].reshape(rows, 2, lane_tiles, LANES).transpose(0, 2, 1, 3).reshape(-1, LANES)

    def unflat(x):
        return x.reshape(rows, lane_tiles, 2, LANES).transpose(0, 2, 1, 3).reshape(1, rows, 2, hidden)

    everyone = range(shards)
    half_rows = tok_rows // 2
    share = tok_rows // particles
    index = lax.dynamic_slice(batch_index, (own * share,), (share,))
    picked = jnp.take(pool, index, axis=0).astype(F32)
    normed = (picked * lax.rsqrt(jnp.mean(picked * picked, axis=1, keepdims=True) + 1e-06)).astype(BF)

    def shift_tokens(x):
        shifted = [[(dev(m, c, s), dev(m, c, (s + k) % shards)) for m, c, s in devices] for k in range(shards)]
        return jnp.stack([move(x, pairs) for pairs in shifted])

    w_flat = flat(weights)
    steps = max(rows // 64, 1)
    lines = w_flat.shape[0] // steps
    *prepared, slices = pl.pallas_call(
        functools.partial(prep_kernel, shards),
        grid=(steps,),
        out_shape=[jax.ShapeDtypeStruct((2, rows, part), BF)] * shards
        + [jax.ShapeDtypeStruct((particles, 2, rows, cols), BF)],
        in_specs=[smem_spec(), pl.BlockSpec((lines, LANES), lambda i: (i, 0))],
        out_specs=[pl.BlockSpec((2, rows // steps, part), lambda i: (0, i, 0))] * shards
        + [pl.BlockSpec((particles, 2, rows // steps, cols), lambda i: (0, 0, i, 0))],
        compiler_params=params(56),
        name="prep",
    )(ids, w_flat)

    w_routes = []
    if shards == 4:
        for own, far_by in ((True, 1), (False, 3), (None, 2)):
            for e in range(2):
                pairs = []
                for m, c, s in devices:
                    at_home = c == s // half
                    if own is None and at_home:
                        pairs.append((dev(m, c, s), dev(m, 1 - e, s)))
                    elif own is None or own == at_home:
                        pairs.append((dev(m, c, s), dev(m, e, s ^ far_by)))
                w_routes.append(pairs)
    else:
        for r in range(shards):
            pairs = []
            for m, c, s in devices:
                q = (s - r) % shards
                pairs.append((dev(m, c, s), dev(m, q % 2, c * half + q // 2)))
            w_routes.append(pairs)

    whole = lax.all_to_all(slices, "particle", 0, 0, tiled=True)

    pair_list = [(i, j) for i in range(particles) for j in range(i)]
    hops = []
    for count, stride in ((particles, shards), (shards, 1)):
        hop = 1
        while hop < count:
            hops.append([(d, d + ((d // stride % count ^ hop) - d // stride % count) * stride) for d in range(len(devices))])
            hop *= 2

    def pair_sums(whole):
        return pl.pallas_call(
            distance_kernel,
            out_shape=jax.ShapeDtypeStruct((8, LANES), F32),
            in_specs=[pl.BlockSpec(memory_space=pltpu.VMEM)],
            out_specs=pl.BlockSpec(memory_space=pltpu.VMEM),
            compiler_params=params(8),
                name="distances",
        )(whole)

    def add_over(sums, steps):
        for step in steps:
            sums = sums + move(sums, hops[step])
        return sums

    def gather_row(ids, which, turn):
        k = lax.rem(ids[SHARD] - which + shards, shards)
        return (turn * (particles // 2) * shards + k) * share

    def place(ids, ref, held, sem, which, turn, start=0):
        row = gather_row(ids, which, turn)
        for i in range(particles // 2):
            to = pl.multiple_of(row + i * shards * share, share)
            pltpu.make_async_copy(
                ref.at[pl.ds(start + i * share, share), :], held.at[pl.ds(to, share), :], sem
            ).start()

    if shards == 4:
        cot = cotangent[0]
        inner = jnp.logical_or(shard == 1, shard == 2)
        flip = jnp.where(jnp.logical_or(inner, core == proc), 0, 1)
        first_routes, second_routes = [], []
        for e in range(2):
            one, two = [], []
            for m, c, s in devices:
                at_home, is_inner = c == s // half, s in (1, 2)
                if not at_home:
                    to, turn = (3 - s, e) if is_inner else (1 if s == 3 else 2, 1 - e)
                    one.append((dev(m, c, s), dev(m, c ^ turn, to)))
                elif is_inner:
                    one.append((dev(m, c, s), dev(m, c ^ e, s ^ 1)))
                else:
                    two.append((dev(m, c, s), dev(m, c ^ e, s ^ 1)))
                if is_inner:
                    two.append((dev(m, c, s), dev(m, c, s ^ 1)))
            first_routes.append(one)
            second_routes.append(two)
        halves = [
            lax.dynamic_slice(cot, (((core + e + flip) % 2) * half_rows, 0), (half_rows, width)) for e in range(2)
        ]
        alpha = [move(x, route) for x, route in zip(halves, first_routes)]
        own_c = move(cot, [(dev(m, c, s), dev(m, 1 - c, s)) for m, c, s in devices if c == s // half])
        normed = shift_tokens(normed)
        w_pieces = [move(x, route) for x, route in zip(prepared[:2], w_routes[:2])]
        alpha, own_c, prepared, normed, w_pieces = lax.optimization_barrier((alpha, own_c, prepared, normed, w_pieces))
        normed = lax.all_gather(normed[None], "particle", axis=0, tiled=True)
        w_pieces = w_pieces + [move(x, route) for x, route in zip(prepared, w_routes[2:])]
        beta = [move(jnp.where(inner, a, x), route) for a, x, route in zip(alpha, halves, second_routes)]
        alpha_x = [move(x, swap_of(everyone)) for x in alpha]
        whole, w_pieces[2:5] = lax.optimization_barrier((whole, w_pieces[2:5]))
        sums = add_over(pair_sums(whole), range(len(hops) - 3))
        w_pieces, normed, sums = lax.optimization_barrier((w_pieces, normed, sums))
        beta_x = [move(x, swap_of(everyone)) for x in beta]
        sources = [cot, own_c, *alpha, *alpha_x, *beta, *beta_x]

        def pick(ids, refs, held, sem):
            s, core, proc = ids[SHARD], ids[CORE], ids[PROC]
            low = s < 2
            near, far, pair = jnp.where(low, 2, 1), jnp.where(low, 3, 0), s + 1 - 2 * lax.rem(s, 2)
            side = lax.rem(core + proc, 2)
            is_inner = jnp.logical_or(s == 1, s == 2)

            def own(ref):
                for turn in range(2):
                    place(ids, ref, held, sem, s, turn, turn * half_rows)

            def others(main, main_x, rest, rest_x):
                for e in range(2):
                    same = side == e
                    place(ids, main[e], held, sem, jnp.where(same, near, far), core)
                    place(ids, main_x[e], held, sem, jnp.where(same, far, near), 1 - core)

                    @pl.when(same)
                    def _():
                        place(ids, rest[e], held, sem, pair, core)
                        place(ids, rest_x[1 - e], held, sem, pair, 1 - core)

            @pl.when(side == 0)
            def _():
                own(refs[0])

            @pl.when(side == 1)
            def _():
                own(refs[1])

            @pl.when(is_inner)
            def _():
                others(refs[2:4], refs[4:6], refs[6:8], refs[8:10])

            @pl.when(jnp.logical_not(is_inner))
            def _():
                others(refs[6:8], refs[8:10], refs[2:4], refs[4:6])
    else:
        full = lax.all_gather(cotangent[0], "shard", axis=0, tiled=True)
        sources = [jnp.where(core == proc, full, move(full, swap_of(everyone)))]
        w_pieces = [move(x, route) for x, route in zip(prepared, w_routes)]
        normed = lax.all_gather(shift_tokens(normed)[None], "particle", axis=0, tiled=True)
        sums = add_over(pair_sums(whole), range(len(hops) - 3))

        def pick(ids, refs, held, sem):
            def one(which, carry):
                for turn in range(2):
                    start = pl.multiple_of(which * tok_rows + turn * half_rows, half_rows)
                    place(ids, refs[0], held, sem, which, turn, start)
                return carry

            lax.fori_loop(0, shards, one, 0)

    normed = normed.reshape(tokens, width)
    act_t, slope, down_w = pl.pallas_call(
        functools.partial(up_kernel, shards, width ** (-0.5)),
        grid=(blocks,),
        out_shape=[
            jax.ShapeDtypeStruct((part, tokens), BF),
            jax.ShapeDtypeStruct((tokens, part), BF),
            jax.ShapeDtypeStruct((width, part), BF),
        ],
        in_specs=[smem_spec(), pl.BlockSpec((BLOCK, width), lambda i: (i, 0))]
        + [pl.BlockSpec((2, rows, part), lambda i: (0, 0, 0))] * len(w_pieces),
        out_specs=[
            pl.BlockSpec((part, BLOCK), lambda i: (0, i)),
            pl.BlockSpec((BLOCK, part), lambda i: (i, 0)),
            pl.BlockSpec((width, part), lambda i: (0, 0)),
        ],
        scratch_shapes=[pltpu.VMEM((width, part), BF)],
        compiler_params=params(20),
        name="up",
    )(ids, normed, *w_pieces)

    sums = add_over(sums, [-3])
    sums, act_t, slope = lax.optimization_barrier((sums, act_t, slope))
    grad_scale = 1.0 / (tokens * width)
    held = 2 * (2 * tokens * width + 3 * tokens * part + 3 * width * part)
    scores = pl.pallas_call(
        functools.partial(
            grad_kernel,
            shards,
            particles,
            -(width ** (-0.5)) * grad_scale,
            -(hidden ** (-0.5)) * grad_scale,
            hidden ** (-0.5),
            pick,
        ),
        out_shape=[jax.ShapeDtypeStruct((2, rows, cols), BF)] * particles,
        in_specs=[smem_spec()] + [any_spec()] * (4 + len(sources)),
        out_specs=[any_spec()] * particles,
        scratch_shapes=[
            pltpu.VMEM((tokens, width), BF),
            pltpu.VMEM((tokens, width), BF),
            pltpu.VMEM((part, tokens), BF),
            pltpu.VMEM((tokens, part), BF),
            pltpu.VMEM((part, tokens), BF),
            pltpu.VMEM((width, part), BF),
            pltpu.VMEM((2, width, part), BF),
            pltpu.SemaphoreType.DMA((particles + 5,)),
        ],
        compiler_params=params(held // MIB + 7),
        name="grads",
    )(ids, normed, act_t, slope, down_w, *sources)

    sums = add_over(sums, [-2])
    sums, *scores = lax.optimization_barrier((sums, *scores))

    ratio = particles // shards
    arrived = []
    for t in range(particles):
        pairs = []
        for m, c, s in devices:
            mine, q = 2 * m + s // half, 2 * (s % half) + c
            u = (mine + ratio * q - t) % particles
            z, e = u // ratio, q * ratio + u % ratio
            pairs.append((dev(m, c, s), dev(e // 2 + z, e % 2, z)))
        arrived.append(move(scores[t], pairs))

    sums = add_over(sums, [-1])
    first_moment, second_moment, sums, *arrived[:5] = lax.optimization_barrier(
        (flat(first_moment), flat(second_moment), sums, *arrived[:5])
    )
    first_moment, second_moment = 0.9 * first_moment, 0.999 * second_moment
    sums = sums[0]
    lookup = [
        [pair_list.index((max(i, j), min(i, j))) if i != j else len(pair_list) for j in range(particles)]
        for i in range(particles)
    ]
    table = jnp.concatenate([sums[: len(pair_list)], jnp.zeros((1,), F32)])
    distances = table[jnp.array(lookup, jnp.int32)]
    inverse_band = 1.0 / kernel_scale[0].astype(F32)
    repulse = 2.0 * inverse_band
    kernel = jnp.exp(-distances * inverse_band)
    scale = 2 * width * hidden / particles
    coef = jnp.concatenate(
        [(scale * kernel).reshape(-1), scale * repulse * jnp.sum(kernel, axis=1), repulse[None]]
    )

    fields = pl.pallas_call(
        functools.partial(stein_kernel, shards, particles),
        out_shape=[jax.ShapeDtypeStruct((2, rows, cols), BF)] * particles,
        in_specs=[smem_spec(), smem_spec(), pl.BlockSpec(memory_space=pltpu.VMEM)] + [any_spec()] * particles,
        out_specs=[any_spec()] * particles,
        scratch_shapes=[
            pltpu.VMEM((particles, 2, rows, cols), BF),
            pltpu.VMEM((particles, 2, rows, cols), BF),
            pltpu.VMEM((particles, min(rows, 64), LANES), F32),
            pltpu.SemaphoreType.DMA((particles,)),
        ],
        compiler_params=params(12),
        name="stein",
    )(ids, coef, whole, *arrived)

    back = []
    for k in range(columns):
        for x in range(2):
            pairs = [(dev(m, c, s), dev(m + k, c ^ x, s)) for m, c, s in devices]
            back.append(move(fields[2 * k + x], pairs))

    steps = max(rows // 32, 1)
    flat_rows = rows * 2 * lane_tiles
    state_spec = pl.BlockSpec((flat_rows // steps, LANES), lambda i: (i, 0))
    outs = pl.pallas_call(
        functools.partial(adam_kernel, particles),
        grid=(steps,),
        out_shape=[jax.ShapeDtypeStruct((flat_rows, LANES), F32)] * 4,
        in_specs=[smem_spec()] + [state_spec] * 3 + [any_spec()] * particles,
        out_specs=[state_spec] * 4,
        scratch_shapes=[pltpu.VMEM((2, rows, hidden), BF), pltpu.SemaphoreType.DMA((particles,))],
        compiler_params=params(20),
        name="adam",
    )(ids, w_flat, first_moment, second_moment, *back)
    return tuple(unflat(x) for x in outs)


def solution(mesh):
    state = P("particle", "shard", None, None)
    return jax.shard_map(
        local,
        mesh=mesh,
        in_specs=(P("shard", None), P("shard"), P(), P("particle", "shard", None), state, state, state),
        out_specs=(state, state, state, state),
        check_vma=False,
    )
```

```python
import functools

import jax
import jax.numpy as jnp
from jax import lax
from jax.experimental import pallas as pl
from jax.experimental.pallas import tpu as pltpu
from jax.sharding import PartitionSpec as P

BF = jnp.bfloat16
F32 = jnp.float32
AXES = ("particle", "shard")
LANES = 128
BLOCK = 256
MIB = 1024 * 1024

COL, CORE, SHARD, PROC, PIECE = range(5)


def any_spec():
    return pl.BlockSpec(memory_space=pl.ANY)


def smem_spec():
    return pl.BlockSpec(memory_space=pltpu.SMEM)


def params(mib):
    return pltpu.CompilerParams(vmem_limit_bytes=mib * MIB)


def run_copies(copies):
    for copy in copies:
        copy.start()
    for copy in copies:
        copy.wait()


def slice_index(ids, column, core, shard, columns):
    return 2 * lax.rem(column - shard + columns * 16, columns) + core


def sent_piece(shards, ids, r):
    if shards != 4:
        return lax.rem(ids[SHARD] - r + shards, shards)
    side = lax.rem(ids[SHARD], 2)
    if r < 2:
        return 2 * (1 - side) + r
    away = lax.rem(ids[PROC] + ids[CORE], 2)
    return 2 * side + lax.rem(r + 1 - away, 2)


def place_pieces(shards, ids, pieces, store):
    if shards != 4:
        for r in range(shards):
            store(pieces[r], lax.rem(ids[PIECE] + r, shards))
        return
    s = ids[SHARD]
    beside = s + 1 - 2 * lax.rem(s, 2)
    across = lax.rem(s + 2, 4)
    for e in range(2):

        @pl.when(ids[CORE] == e)
        def _():
            store(pieces[e], beside)
            store(pieces[2 + e], 3 - s)
            store(pieces[4 + e], across)
            store(pieces[5 - e], s)


def prep_kernel(shards, ids, w, *out):
    pieces, slices = out[:shards], out[shards]
    _, rows, piece = pieces[0].shape
    particles, _, _, cols = slices.shape
    columns = particles // 2
    tiles, per_slice = piece // LANES, cols // LANES
    for r in range(shards):
        q = sent_piece(shards, ids, r)
        for j in range(tiles):
            e = q * (tiles // per_slice) + j // per_slice
            column = lax.rem(lax.div(e, 2) + ids[SHARD], columns)
            p = 2 * column + lax.rem(e, 2)
            at, within = j * LANES, j % per_slice * LANES
            for kind in range(2):
                line = 2 * (q * tiles + j) + kind
                part = w[pl.ds(line, rows, stride=2 * shards * tiles), :].astype(BF)
                pieces[r][kind, :, at : at + LANES] = part
                slices[p, kind, :, within : within + LANES] = part


def up_kernel(shards, scale, ids, tokens, *refs):
    pieces = refs[:-4]
    act_t, slope, down_w, up_w = refs[-4:]
    width, part = up_w.shape
    rows = width // shards

    @pl.when(pl.program_id(0) == 0)
    def _():
        def store(piece, shard):
            at = pl.multiple_of(shard * rows, rows)
            up_w[pl.ds(at, rows), :] = piece[0]
            down_w[pl.ds(at, rows), :] = piece[1]

        place_pieces(shards, ids, pieces, store)

    u = jnp.dot(tokens[...], up_w[...], preferred_element_type=F32) * scale
    cdf = 0.5 * (1.0 + lax.erf(u * 0.7071067811865476))
    density = jnp.exp(-0.5 * u * u) * 0.3989422804014327
    act_t[...] = (u * cdf).astype(BF).T
    slope[...] = (cdf + u * density).astype(BF)


def grad_kernel(shards, particles, up_scale, down_scale, back_scale, pick, ids, normed, act_t, slope_rows, down_w, *refs):
    n_in = len(refs) - particles - 8
    sources, out = refs[:n_in], refs[n_in : n_in + particles]
    c, n, act, slope, grad, down, score, sems = refs[n_in + particles :]
    part, tokens = act.shape
    width = c.shape[1]
    chunk = tokens // shards
    first = [
        pltpu.make_async_copy(down_w, down, sems.at[1]),
        pltpu.make_async_copy(slope_rows, slope, sems.at[2]),
    ]
    later = [
        pltpu.make_async_copy(act_t, act, sems.at[3]),
        pltpu.make_async_copy(normed, n, sems.at[4]),
    ]
    for copy in first:
        copy.start()
    pick(ids, sources, c, sems.at[0])
    for copy in later:
        copy.start()
    for copy in first:
        copy.wait()
    pltpu.make_async_copy(c, c, sems.at[0]).wait()

    def back(i, carry):
        at = pl.multiple_of(i * chunk, chunk)
        b = jnp.dot(c[pl.ds(at, chunk), :], down[...], preferred_element_type=F32)
        b = (b * (slope[pl.ds(at, chunk), :].astype(F32) * back_scale)).astype(BF)
        grad[:, pl.ds(at, chunk)] = b.T
        return carry

    lax.fori_loop(0, shards, back, 0)
    for copy in later:
        copy.wait()

    def gradient(j, carry):
        at = pl.multiple_of(j * BLOCK, BLOCK)
        g = jnp.dot(grad[...], n[:, pl.ds(at, BLOCK)], preferred_element_type=F32)
        score[0, pl.ds(at, BLOCK), :] = (g * up_scale).astype(BF).T
        g = jnp.dot(act[...], c[:, pl.ds(at, BLOCK)], preferred_element_type=F32)
        score[1, pl.ds(at, BLOCK), :] = (g * down_scale).astype(BF).T
        return carry

    lax.fori_loop(0, width // BLOCK, gradient, 0)
    rows = width // shards
    ratio = particles // shards
    cols = part // ratio
    mine = 2 * ids[COL] + ids[PROC]
    copies = []
    for t in range(particles):
        u = lax.rem(mine + ratio * ids[PIECE] - t + particles, particles)
        row = pl.multiple_of(lax.div(u, ratio) * rows, rows)
        col = pl.multiple_of(lax.rem(u, ratio) * cols, cols)
        copies.append(pltpu.make_async_copy(score.at[:, pl.ds(row, rows), pl.ds(col, cols)], out[t], sems.at[t]))
    run_copies(copies)


def distance_kernel(whole, out):
    particles, _, rows, cols = whole.shape
    pairs = [(i, j) for i in range(particles) for j in range(i)]
    tiles = cols // LANES

    def body(g, acc):
        kind = lax.div(g, rows // 16)
        row = pl.multiple_of(lax.rem(g, rows // 16) * 16, 16)
        for tile in range(tiles):
            w = [whole[p, kind, pl.ds(row, 16), tile * LANES : (tile + 1) * LANES].astype(F32) for p in range(particles)]
            new = []
            for a, (i, j) in zip(acc, pairs):
                d = w[i] - w[j]
                d = d * d
                new.append(a + (d[:8] + d[8:]))
            acc = tuple(new)
        return acc

    acc = lax.fori_loop(0, 2 * rows // 16, body, tuple(jnp.zeros((8, LANES), F32) for _ in pairs))
    lane = lax.broadcasted_iota(jnp.int32, (8, LANES), 1)
    row = jnp.zeros((8, LANES), F32)
    for i, a in enumerate(acc):
        total = jnp.sum(jnp.sum(a, axis=0, keepdims=True), axis=1, keepdims=True)
        row = row + jnp.where(lane == i, total, 0.0)
    out[...] = row


def stein_kernel(shards, particles, ids, coef, whole, *refs):
    sources, out = refs[:particles], refs[particles : 2 * particles]
    scores, field, pushed, sems = refs[2 * particles :]
    columns = particles // 2
    ratio = particles // shards
    _, _, rows, cols = whole.shape
    e = slice_index(ids, ids[COL], ids[CORE], ids[SHARD], columns)
    u = ids[SHARD] * ratio + lax.rem(e, ratio) + particles * shards - ratio * lax.div(e, ratio)
    run_copies(
        [pltpu.make_async_copy(sources[t], scores.at[lax.rem(u + t, particles)], sems.at[t]) for t in range(particles)]
    )
    repulse = coef[particles * particles + particles]
    chunk = min(rows, 64)
    groups = rows // chunk
    tiles = cols // LANES

    def body(g, carry):
        kind = lax.div(g, groups)
        row = pl.multiple_of(lax.rem(g, groups) * chunk, chunk)
        for tile in range(tiles):
            at = (kind, pl.ds(row, chunk), slice(tile * LANES, (tile + 1) * LANES))
            for p in range(particles):
                pushed[p] = scores[(p,) + at].astype(F32) - repulse * whole[(p,) + at].astype(F32)
            for i in range(particles):
                total = coef[particles * particles + i] * whole[(i,) + at].astype(F32)
                for j in range(particles):
                    total = total + coef[i * particles + j] * pushed[j]
                field[(i,) + at] = total.astype(BF)
        return carry

    lax.fori_loop(0, 2 * groups, body, 0)
    copies = []
    for k in range(columns):
        for x in range(2):
            column = lax.rem(ids[COL] + k, columns)
            core = ids[CORE] if x == 0 else 1 - ids[CORE]
            i = 2 * k + x
            copies.append(pltpu.make_async_copy(field.at[2 * column + core], out[i], sems.at[i]))
    run_copies(copies)


def adam_kernel(particles, ids, w, first, second, *refs):
    sources = refs[:particles]
    new_w, new_first, new_second, transport, field, sems = refs[particles:]
    columns = particles // 2
    _, _, hidden = field.shape
    width = hidden // particles
    step = pl.program_id(0)

    @pl.when(step == 0)
    def _():
        copies = []
        for k in range(columns):
            for x in range(2):
                column = lax.rem(ids[COL] - k + columns, columns)
                core = ids[CORE] if x == 0 else 1 - ids[CORE]
                at = pl.multiple_of(slice_index(ids, column, core, ids[SHARD], columns) * width, width)
                i = 2 * k + x
                copies.append(pltpu.make_async_copy(sources[i], field.at[:, :, pl.ds(at, width)], sems.at[i]))
        run_copies(copies)

    lane_tiles = hidden // LANES
    rows = w.shape[0] // (2 * lane_tiles)
    base = pl.multiple_of(step * rows, rows)
    for kind in range(2):
        for tile in range(lane_tiles):
            part = field[kind, pl.ds(base, rows), tile * LANES : (tile + 1) * LANES]
            transport[pl.ds(2 * tile + kind, rows, stride=2 * lane_tiles), :] = part.astype(F32)
    t = transport[...]
    m = first[...] - 0.1 * t
    v = second[...] + 0.001 * t * t
    new_first[...] = m
    new_second[...] = v
    new_w[...] = w[...] - 0.01 * m / (jnp.sqrt(v) + 1e-08)


def local(pool, batch_index, kernel_scale, cotangent, weights, first_moment, second_moment):
    shards = lax.axis_size("shard")
    particles = lax.axis_size("particle")
    columns, half = particles // 2, shards // 2
    tok_rows = batch_index.shape[0]
    width = pool.shape[1]
    _, rows, _, hidden = weights.shape
    part, cols = hidden // shards, hidden // particles
    tokens = tok_rows * shards
    blocks = tokens // BLOCK
    lane_tiles = hidden // LANES

    own = lax.axis_index("particle")
    shard = lax.axis_index("shard")
    core, column = own % 2, own // 2
    proc = shard // half
    piece = 2 * (shard % half) + core
    ids = jnp.stack([column, core, shard, proc, piece]).astype(jnp.int32)
    devices = [(m, c, s) for m in range(columns) for c in range(2) for s in range(shards)]

    def dev(m, c, s):
        return (2 * (m % columns) + c) * shards + s

    def move(x, pairs):
        if all(a == b for a, b in pairs) and len(pairs) == len(devices):
            return x
        return lax.ppermute(x, AXES, pairs)

    def swap_of(among):
        return [(dev(m, c, s), dev(m, 1 - c, s)) for m, c, s in devices if s in among]

    def flat(x):
        return x[0].reshape(rows, 2, lane_tiles, LANES).transpose(0, 2, 1, 3).reshape(-1, LANES)

    def unflat(x):
        return x.reshape(rows, lane_tiles, 2, LANES).transpose(0, 2, 1, 3).reshape(1, rows, 2, hidden)

    everyone = range(shards)
    half_rows = tok_rows // 2
    share = tok_rows // particles
    index = lax.dynamic_slice(batch_index, (own * share,), (share,))
    picked = jnp.take(pool, index, axis=0).astype(F32)
    normed = (picked * lax.rsqrt(jnp.mean(picked * picked, axis=1, keepdims=True) + 1e-06)).astype(BF)

    def shift_tokens(x):
        shifted = [[(dev(m, c, s), dev(m, c, (s + k) % shards)) for m, c, s in devices] for k in range(shards)]
        return jnp.stack([move(x, pairs) for pairs in shifted])

    w_flat = flat(weights)
    steps = max(rows // 64, 1)
    lines = w_flat.shape[0] // steps
    *prepared, slices = pl.pallas_call(
        functools.partial(prep_kernel, shards),
        grid=(steps,),
        out_shape=[jax.ShapeDtypeStruct((2, rows, part), BF)] * shards
        + [jax.ShapeDtypeStruct((particles, 2, rows, cols), BF)],
        in_specs=[smem_spec(), pl.BlockSpec((lines, LANES), lambda i: (i, 0))],
        out_specs=[pl.BlockSpec((2, rows // steps, part), lambda i: (0, i, 0))] * shards
        + [pl.BlockSpec((particles, 2, rows // steps, cols), lambda i: (0, 0, i, 0))],
        compiler_params=params(56),
        name="prep",
    )(ids, w_flat)

    w_routes = []
    if shards == 4:
        for own, far_by in ((True, 1), (False, 3), (None, 2)):
            for e in range(2):
                pairs = []
                for m, c, s in devices:
                    at_home = c == s // half
                    if own is None and at_home:
                        pairs.append((dev(m, c, s), dev(m, 1 - e, s)))
                    elif own is None or own == at_home:
                        pairs.append((dev(m, c, s), dev(m, e, s ^ far_by)))
                w_routes.append(pairs)
    else:
        for r in range(shards):
            pairs = []
            for m, c, s in devices:
                q = (s - r) % shards
                pairs.append((dev(m, c, s), dev(m, q % 2, c * half + q // 2)))
            w_routes.append(pairs)

    whole = lax.all_to_all(slices, "particle", 0, 0, tiled=True)

    pair_list = [(i, j) for i in range(particles) for j in range(i)]
    hops = []
    for count, stride in ((particles, shards), (shards, 1)):
        hop = 1
        while hop < count:
            hops.append([(d, d + ((d // stride % count ^ hop) - d // stride % count) * stride) for d in range(len(devices))])
            hop *= 2

    def pair_sums(whole):
        return pl.pallas_call(
            distance_kernel,
            out_shape=jax.ShapeDtypeStruct((8, LANES), F32),
            in_specs=[pl.BlockSpec(memory_space=pltpu.VMEM)],
            out_specs=pl.BlockSpec(memory_space=pltpu.VMEM),
            compiler_params=params(8),
                name="distances",
        )(whole)

    def add_over(sums, steps):
        for step in steps:
            sums = sums + move(sums, hops[step])
        return sums

    def gather_row(ids, which, turn):
        k = lax.rem(ids[SHARD] - which + shards, shards)
        return (turn * (particles // 2) * shards + k) * share

    def place(ids, ref, held, sem, which, turn, start=0):
        row = gather_row(ids, which, turn)
        for i in range(particles // 2):
            to = pl.multiple_of(row + i * shards * share, share)
            pltpu.make_async_copy(
                ref.at[pl.ds(start + i * share, share), :], held.at[pl.ds(to, share), :], sem
            ).start()

    if shards == 4:
        cot = cotangent[0]
        inner = jnp.logical_or(shard == 1, shard == 2)
        flip = jnp.where(jnp.logical_or(inner, core == proc), 0, 1)
        first_routes, second_routes = [], []
        for e in range(2):
            one, two = [], []
            for m, c, s in devices:
                at_home, is_inner = c == s // half, s in (1, 2)
                if not at_home:
                    to, turn = (3 - s, e) if is_inner else (1 if s == 3 else 2, 1 - e)
                    one.append((dev(m, c, s), dev(m, c ^ turn, to)))
                elif is_inner:
                    one.append((dev(m, c, s), dev(m, c ^ e, s ^ 1)))
                else:
                    two.append((dev(m, c, s), dev(m, c ^ e, s ^ 1)))
                if is_inner:
                    two.append((dev(m, c, s), dev(m, c, s ^ 1)))
            first_routes.append(one)
            second_routes.append(two)
        halves = [
            lax.dynamic_slice(cot, (((core + e + flip) % 2) * half_rows, 0), (half_rows, width)) for e in range(2)
        ]
        alpha = [move(x, route) for x, route in zip(halves, first_routes)]
        own_c = move(cot, [(dev(m, c, s), dev(m, 1 - c, s)) for m, c, s in devices if c == s // half])
        normed = shift_tokens(normed)
        w_pieces = [move(x, route) for x, route in zip(prepared[:2], w_routes[:2])]
        alpha, own_c, prepared, normed, w_pieces = lax.optimization_barrier((alpha, own_c, prepared, normed, w_pieces))
        normed = lax.all_gather(normed[None], "particle", axis=0, tiled=True)
        w_pieces = w_pieces + [move(x, route) for x, route in zip(prepared, w_routes[2:])]
        beta = [move(jnp.where(inner, a, x), route) for a, x, route in zip(alpha, halves, second_routes)]
        alpha_x = [move(x, swap_of(everyone)) for x in alpha]
        whole, w_pieces[2:4] = lax.optimization_barrier((whole, w_pieces[2:4]))
        sums = add_over(pair_sums(whole), range(len(hops) - 3))
        w_pieces, normed, sums = lax.optimization_barrier((w_pieces, normed, sums))
        beta_x = [move(x, swap_of(everyone)) for x in beta]
        sources = [cot, own_c, *alpha, *alpha_x, *beta, *beta_x]

        def pick(ids, refs, held, sem):
            s, core, proc = ids[SHARD], ids[CORE], ids[PROC]
            low = s < 2
            near, far, pair = jnp.where(low, 2, 1), jnp.where(low, 3, 0), s + 1 - 2 * lax.rem(s, 2)
            side = lax.rem(core + proc, 2)
            is_inner = jnp.logical_or(s == 1, s == 2)

            def own(ref):
                for turn in range(2):
                    place(ids, ref, held, sem, s, turn, turn * half_rows)

            def others(main, main_x, rest, rest_x):
                for e in range(2):
                    same = side == e
                    place(ids, main[e], held, sem, jnp.where(same, near, far), core)
                    place(ids, main_x[e], held, sem, jnp.where(same, far, near), 1 - core)

                    @pl.when(same)
                    def _():
                        place(ids, rest[e], held, sem, pair, core)
                        place(ids, rest_x[1 - e], held, sem, pair, 1 - core)

            @pl.when(side == 0)
            def _():
                own(refs[0])

            @pl.when(side == 1)
            def _():
                own(refs[1])

            @pl.when(is_inner)
            def _():
                others(refs[2:4], refs[4:6], refs[6:8], refs[8:10])

            @pl.when(jnp.logical_not(is_inner))
            def _():
                others(refs[6:8], refs[8:10], refs[2:4], refs[4:6])
    else:
        full = lax.all_gather(cotangent[0], "shard", axis=0, tiled=True)
        sources = [jnp.where(core == proc, full, move(full, swap_of(everyone)))]
        w_pieces = [move(x, route) for x, route in zip(prepared, w_routes)]
        normed = lax.all_gather(shift_tokens(normed)[None], "particle", axis=0, tiled=True)
        sums = add_over(pair_sums(whole), range(len(hops) - 3))

        def pick(ids, refs, held, sem):
            def one(which, carry):
                for turn in range(2):
                    start = pl.multiple_of(which * tok_rows + turn * half_rows, half_rows)
                    place(ids, refs[0], held, sem, which, turn, start)
                return carry

            lax.fori_loop(0, shards, one, 0)

    normed = normed.reshape(tokens, width)
    act_t, slope, down_w = pl.pallas_call(
        functools.partial(up_kernel, shards, width ** (-0.5)),
        grid=(blocks,),
        out_shape=[
            jax.ShapeDtypeStruct((part, tokens), BF),
            jax.ShapeDtypeStruct((tokens, part), BF),
            jax.ShapeDtypeStruct((width, part), BF),
        ],
        in_specs=[smem_spec(), pl.BlockSpec((BLOCK, width), lambda i: (i, 0))]
        + [pl.BlockSpec((2, rows, part), lambda i: (0, 0, 0))] * len(w_pieces),
        out_specs=[
            pl.BlockSpec((part, BLOCK), lambda i: (0, i)),
            pl.BlockSpec((BLOCK, part), lambda i: (i, 0)),
            pl.BlockSpec((width, part), lambda i: (0, 0)),
        ],
        scratch_shapes=[pltpu.VMEM((width, part), BF)],
        compiler_params=params(56),
        name="up",
    )(ids, normed, *w_pieces)

    sums = add_over(sums, [-3])
    sums, act_t, slope = lax.optimization_barrier((sums, act_t, slope))
    grad_scale = 1.0 / (tokens * width)
    scores = pl.pallas_call(
        functools.partial(
            grad_kernel,
            shards,
            particles,
            -(width ** (-0.5)) * grad_scale,
            -(hidden ** (-0.5)) * grad_scale,
            hidden ** (-0.5),
            pick,
        ),
        out_shape=[jax.ShapeDtypeStruct((2, rows, cols), BF)] * particles,
        in_specs=[smem_spec()] + [any_spec()] * (4 + len(sources)),
        out_specs=[any_spec()] * particles,
        scratch_shapes=[
            pltpu.VMEM((tokens, width), BF),
            pltpu.VMEM((tokens, width), BF),
            pltpu.VMEM((part, tokens), BF),
            pltpu.VMEM((tokens, part), BF),
            pltpu.VMEM((part, tokens), BF),
            pltpu.VMEM((width, part), BF),
            pltpu.VMEM((2, width, part), BF),
            pltpu.SemaphoreType.DMA((particles + 5,)),
        ],
        compiler_params=params(56),
        name="grads",
    )(ids, normed, act_t, slope, down_w, *sources)

    sums = add_over(sums, [-2])
    sums, *scores = lax.optimization_barrier((sums, *scores))

    ratio = particles // shards
    arrived = []
    for t in range(particles):
        pairs = []
        for m, c, s in devices:
            mine, q = 2 * m + s // half, 2 * (s % half) + c
            u = (mine + ratio * q - t) % particles
            z, e = u // ratio, q * ratio + u % ratio
            pairs.append((dev(m, c, s), dev(e // 2 + z, e % 2, z)))
        arrived.append(move(scores[t], pairs))

    sums = add_over(sums, [-1])
    first_moment, second_moment, sums, *arrived[:5] = lax.optimization_barrier(
        (flat(first_moment), flat(second_moment), sums, *arrived[:5])
    )
    first_moment, second_moment = 0.9 * first_moment, 0.999 * second_moment
    sums = sums[0]
    lookup = [
        [pair_list.index((max(i, j), min(i, j))) if i != j else len(pair_list) for j in range(particles)]
        for i in range(particles)
    ]
    table = jnp.concatenate([sums[: len(pair_list)], jnp.zeros((1,), F32)])
    distances = table[jnp.array(lookup, jnp.int32)]
    inverse_band = 1.0 / kernel_scale[0].astype(F32)
    repulse = 2.0 * inverse_band
    kernel = jnp.exp(-distances * inverse_band)
    scale = 2 * width * hidden / particles
    coef = jnp.concatenate(
        [(scale * kernel).reshape(-1), scale * repulse * jnp.sum(kernel, axis=1), repulse[None]]
    )

    fields = pl.pallas_call(
        functools.partial(stein_kernel, shards, particles),
        out_shape=[jax.ShapeDtypeStruct((2, rows, cols), BF)] * particles,
        in_specs=[smem_spec(), smem_spec(), pl.BlockSpec(memory_space=pltpu.VMEM)] + [any_spec()] * particles,
        out_specs=[any_spec()] * particles,
        scratch_shapes=[
            pltpu.VMEM((particles, 2, rows, cols), BF),
            pltpu.VMEM((particles, 2, rows, cols), BF),
            pltpu.VMEM((particles, min(rows, 64), LANES), F32),
            pltpu.SemaphoreType.DMA((particles,)),
        ],
        compiler_params=params(12),
        name="stein",
    )(ids, coef, whole, *arrived)

    back = []
    for k in range(columns):
        for x in range(2):
            pairs = [(dev(m, c, s), dev(m + k, c ^ x, s)) for m, c, s in devices]
            back.append(move(fields[2 * k + x], pairs))

    steps = max(rows // 32, 1)
    flat_rows = rows * 2 * lane_tiles
    state_spec = pl.BlockSpec((flat_rows // steps, LANES), lambda i: (i, 0))
    outs = pl.pallas_call(
        functools.partial(adam_kernel, particles),
        grid=(steps,),
        out_shape=[jax.ShapeDtypeStruct((flat_rows, LANES), F32)] * 4,
        in_specs=[smem_spec()] + [state_spec] * 3 + [any_spec()] * particles,
        out_specs=[state_spec] * 4,
        scratch_shapes=[pltpu.VMEM((2, rows, hidden), BF), pltpu.SemaphoreType.DMA((particles,))],
        compiler_params=params(20),
        name="adam",
    )(ids, w_flat, first_moment, second_moment, *back)
    return tuple(unflat(x) for x in outs)


def solution(mesh):
    state = P("particle", "shard", None, None)
    return jax.shard_map(
        local,
        mesh=mesh,
        in_specs=(P("shard", None), P("shard"), P(), P("particle", "shard", None), state, state, state),
        out_specs=(state, state, state, state),
        check_vma=False,
    )
```

```python
import functools

import jax
import jax.numpy as jnp
from jax import lax
from jax.experimental import pallas as pl
from jax.experimental.pallas import tpu as pltpu
from jax.sharding import PartitionSpec as P

BF = jnp.bfloat16
F32 = jnp.float32
AXES = ("particle", "shard")
LANES = 128
BLOCK = 256
MIB = 1024 * 1024

COL, CORE, SHARD, PROC, PIECE = range(5)


def any_spec():
    return pl.BlockSpec(memory_space=pl.ANY)


def smem_spec():
    return pl.BlockSpec(memory_space=pltpu.SMEM)


def params(mib):
    return pltpu.CompilerParams(vmem_limit_bytes=mib * MIB)


def run_copies(copies):
    for copy in copies:
        copy.start()
    for copy in copies:
        copy.wait()


def slice_index(ids, column, core, shard, columns):
    return 2 * lax.rem(column - shard + columns * 16, columns) + core


def sent_piece(shards, ids, r):
    if shards != 4:
        return lax.rem(ids[SHARD] - r + shards, shards)
    side = lax.rem(ids[SHARD], 2)
    if r < 2:
        return 2 * (1 - side) + r
    away = lax.rem(ids[PROC] + ids[CORE], 2)
    return 2 * side + lax.rem(r + 1 - away, 2)


def place_pieces(shards, ids, pieces, store):
    if shards != 4:
        for r in range(shards):
            store(pieces[r], lax.rem(ids[PIECE] + r, shards))
        return
    s = ids[SHARD]
    beside = s + 1 - 2 * lax.rem(s, 2)
    across = lax.rem(s + 2, 4)
    for e in range(2):

        @pl.when(ids[CORE] == e)
        def _():
            store(pieces[e], beside)
            store(pieces[2 + e], 3 - s)
            store(pieces[4 + e], across)
            store(pieces[5 - e], s)


def prep_kernel(shards, ids, w, *out):
    pieces, slices = out[:shards], out[shards]
    _, rows, piece = pieces[0].shape
    particles, _, _, cols = slices.shape
    columns = particles // 2
    tiles, per_slice = piece // LANES, cols // LANES
    for r in range(shards):
        q = sent_piece(shards, ids, r)
        for j in range(tiles):
            e = q * (tiles // per_slice) + j // per_slice
            column = lax.rem(lax.div(e, 2) + ids[SHARD], columns)
            p = 2 * column + lax.rem(e, 2)
            at, within = j * LANES, j % per_slice * LANES
            for kind in range(2):
                line = 2 * (q * tiles + j) + kind
                part = w[pl.ds(line, rows, stride=2 * shards * tiles), :].astype(BF)
                pieces[r][kind, :, at : at + LANES] = part
                slices[p, kind, :, within : within + LANES] = part


def up_kernel(shards, scale, ids, tokens, *refs):
    pieces = refs[:-4]
    act_t, slope, down_w, up_w = refs[-4:]
    width, part = up_w.shape
    rows = width // shards

    @pl.when(pl.program_id(0) == 0)
    def _():
        def store(piece, shard):
            at = pl.multiple_of(shard * rows, rows)
            up_w[pl.ds(at, rows), :] = piece[0]
            down_w[pl.ds(at, rows), :] = piece[1]

        place_pieces(shards, ids, pieces, store)

    u = jnp.dot(tokens[...], up_w[...], preferred_element_type=F32) * scale
    cdf = 0.5 * (1.0 + lax.erf(u * 0.7071067811865476))
    density = jnp.exp(-0.5 * u * u) * 0.3989422804014327
    act_t[...] = (u * cdf).astype(BF).T
    slope[...] = (cdf + u * density).astype(BF)


def grad_kernel(shards, particles, up_scale, down_scale, back_scale, pick, ids, normed, act_t, slope_rows, down_w, *refs):
    n_in = len(refs) - particles - 8
    sources, out = refs[:n_in], refs[n_in : n_in + particles]
    c, n, act, slope, grad, down, score, sems = refs[n_in + particles :]
    part, tokens = act.shape
    width = c.shape[1]
    chunk = tokens // shards
    first = [
        pltpu.make_async_copy(down_w, down, sems.at[1]),
        pltpu.make_async_copy(slope_rows, slope, sems.at[2]),
    ]
    later = [
        pltpu.make_async_copy(act_t, act, sems.at[3]),
        pltpu.make_async_copy(normed, n, sems.at[4]),
    ]
    for copy in first:
        copy.start()
    pick(ids, sources, c, sems.at[0])
    for copy in later:
        copy.start()
    for copy in first:
        copy.wait()
    pltpu.make_async_copy(c, c, sems.at[0]).wait()

    for i in range(shards):
        rows = slice(i * chunk, (i + 1) * chunk)
        b = jnp.dot(c[rows, :], down[...], preferred_element_type=F32)
        b = (b * (slope[rows, :].astype(F32) * back_scale)).astype(BF)
        grad[:, rows] = b.T
    for copy in later:
        copy.wait()
    for j in range(width // BLOCK):
        span = slice(j * BLOCK, (j + 1) * BLOCK)
        g = jnp.dot(grad[...], n[:, span], preferred_element_type=F32)
        score[0, span, :] = (g * up_scale).astype(BF).T
        g = jnp.dot(act[...], c[:, span], preferred_element_type=F32)
        score[1, span, :] = (g * down_scale).astype(BF).T
    rows = width // shards
    ratio = particles // shards
    cols = part // ratio
    mine = 2 * ids[COL] + ids[PROC]
    copies = []
    for t in range(particles):
        u = lax.rem(mine + ratio * ids[PIECE] - t + particles, particles)
        row = pl.multiple_of(lax.div(u, ratio) * rows, rows)
        col = pl.multiple_of(lax.rem(u, ratio) * cols, cols)
        copies.append(pltpu.make_async_copy(score.at[:, pl.ds(row, rows), pl.ds(col, cols)], out[t], sems.at[t]))
    run_copies(copies)


def distance_kernel(whole, out):
    particles, _, rows, cols = whole.shape
    pairs = [(i, j) for i in range(particles) for j in range(i)]
    tiles = cols // LANES

    def body(g, acc):
        kind = lax.div(g, rows // 16)
        row = pl.multiple_of(lax.rem(g, rows // 16) * 16, 16)
        for tile in range(tiles):
            w = [whole[p, kind, pl.ds(row, 16), tile * LANES : (tile + 1) * LANES].astype(F32) for p in range(particles)]
            new = []
            for a, (i, j) in zip(acc, pairs):
                d = w[i] - w[j]
                d = d * d
                new.append(a + (d[:8] + d[8:]))
            acc = tuple(new)
        return acc

    acc = lax.fori_loop(0, 2 * rows // 16, body, tuple(jnp.zeros((8, LANES), F32) for _ in pairs))
    lane = lax.broadcasted_iota(jnp.int32, (8, LANES), 1)
    row = jnp.zeros((8, LANES), F32)
    for i, a in enumerate(acc):
        total = jnp.sum(jnp.sum(a, axis=0, keepdims=True), axis=1, keepdims=True)
        row = row + jnp.where(lane == i, total, 0.0)
    out[...] = row


def stein_kernel(shards, particles, ids, coef, whole, *refs):
    sources, out = refs[:particles], refs[particles : 2 * particles]
    scores, field, pushed, sems = refs[2 * particles :]
    columns = particles // 2
    ratio = particles // shards
    _, _, rows, cols = whole.shape
    e = slice_index(ids, ids[COL], ids[CORE], ids[SHARD], columns)
    u = ids[SHARD] * ratio + lax.rem(e, ratio) + particles * shards - ratio * lax.div(e, ratio)
    run_copies(
        [pltpu.make_async_copy(sources[t], scores.at[lax.rem(u + t, particles)], sems.at[t]) for t in range(particles)]
    )
    repulse = coef[particles * particles + particles]
    chunk = min(rows, 64)
    groups = rows // chunk
    tiles = cols // LANES

    def body(g, carry):
        kind = lax.div(g, groups)
        row = pl.multiple_of(lax.rem(g, groups) * chunk, chunk)
        for tile in range(tiles):
            at = (kind, pl.ds(row, chunk), slice(tile * LANES, (tile + 1) * LANES))
            for p in range(particles):
                pushed[p] = scores[(p,) + at].astype(F32) - repulse * whole[(p,) + at].astype(F32)
            for i in range(particles):
                total = coef[particles * particles + i] * whole[(i,) + at].astype(F32)
                for j in range(particles):
                    total = total + coef[i * particles + j] * pushed[j]
                field[(i,) + at] = total.astype(BF)
        return carry

    lax.fori_loop(0, 2 * groups, body, 0)
    copies = []
    for k in range(columns):
        for x in range(2):
            column = lax.rem(ids[COL] + k, columns)
            core = ids[CORE] if x == 0 else 1 - ids[CORE]
            i = 2 * k + x
            copies.append(pltpu.make_async_copy(field.at[2 * column + core], out[i], sems.at[i]))
    run_copies(copies)


def adam_kernel(particles, ids, w, first, second, *refs):
    sources = refs[:particles]
    new_w, new_first, new_second, transport, field, sems = refs[particles:]
    columns = particles // 2
    _, _, hidden = field.shape
    width = hidden // particles
    step = pl.program_id(0)

    @pl.when(step == 0)
    def _():
        copies = []
        for k in range(columns):
            for x in range(2):
                column = lax.rem(ids[COL] - k + columns, columns)
                core = ids[CORE] if x == 0 else 1 - ids[CORE]
                at = pl.multiple_of(slice_index(ids, column, core, ids[SHARD], columns) * width, width)
                i = 2 * k + x
                copies.append(pltpu.make_async_copy(sources[i], field.at[:, :, pl.ds(at, width)], sems.at[i]))
        run_copies(copies)

    lane_tiles = hidden // LANES
    rows = w.shape[0] // (2 * lane_tiles)
    base = pl.multiple_of(step * rows, rows)
    for kind in range(2):
        for tile in range(lane_tiles):
            part = field[kind, pl.ds(base, rows), tile * LANES : (tile + 1) * LANES]
            transport[pl.ds(2 * tile + kind, rows, stride=2 * lane_tiles), :] = part.astype(F32)
    t = transport[...]
    m = first[...] - 0.1 * t
    v = second[...] + 0.001 * t * t
    new_first[...] = m
    new_second[...] = v
    new_w[...] = w[...] - 0.01 * m / (jnp.sqrt(v) + 1e-08)


def local(pool, batch_index, kernel_scale, cotangent, weights, first_moment, second_moment):
    shards = lax.axis_size("shard")
    particles = lax.axis_size("particle")
    columns, half = particles // 2, shards // 2
    tok_rows = batch_index.shape[0]
    width = pool.shape[1]
    _, rows, _, hidden = weights.shape
    part, cols = hidden // shards, hidden // particles
    tokens = tok_rows * shards
    blocks = tokens // BLOCK
    lane_tiles = hidden // LANES

    own = lax.axis_index("particle")
    shard = lax.axis_index("shard")
    core, column = own % 2, own // 2
    proc = shard // half
    piece = 2 * (shard % half) + core
    ids = jnp.stack([column, core, shard, proc, piece]).astype(jnp.int32)
    devices = [(m, c, s) for m in range(columns) for c in range(2) for s in range(shards)]

    def dev(m, c, s):
        return (2 * (m % columns) + c) * shards + s

    def move(x, pairs):
        if all(a == b for a, b in pairs) and len(pairs) == len(devices):
            return x
        return lax.ppermute(x, AXES, pairs)

    def swap_of(among):
        return [(dev(m, c, s), dev(m, 1 - c, s)) for m, c, s in devices if s in among]

    def flat(x):
        return x[0].reshape(rows, 2, lane_tiles, LANES).transpose(0, 2, 1, 3).reshape(-1, LANES)

    def unflat(x):
        return x.reshape(rows, lane_tiles, 2, LANES).transpose(0, 2, 1, 3).reshape(1, rows, 2, hidden)

    everyone = range(shards)
    half_rows = tok_rows // 2
    share = tok_rows // particles
    index = lax.dynamic_slice(batch_index, (own * share,), (share,))
    picked = jnp.take(pool, index, axis=0).astype(F32)
    normed = (picked * lax.rsqrt(jnp.mean(picked * picked, axis=1, keepdims=True) + 1e-06)).astype(BF)

    def shift_tokens(x):
        shifted = [[(dev(m, c, s), dev(m, c, (s + k) % shards)) for m, c, s in devices] for k in range(shards)]
        return jnp.stack([move(x, pairs) for pairs in shifted])

    w_flat = flat(weights)
    steps = max(rows // 64, 1)
    lines = w_flat.shape[0] // steps
    *prepared, slices = pl.pallas_call(
        functools.partial(prep_kernel, shards),
        grid=(steps,),
        out_shape=[jax.ShapeDtypeStruct((2, rows, part), BF)] * shards
        + [jax.ShapeDtypeStruct((particles, 2, rows, cols), BF)],
        in_specs=[smem_spec(), pl.BlockSpec((lines, LANES), lambda i: (i, 0))],
        out_specs=[pl.BlockSpec((2, rows // steps, part), lambda i: (0, i, 0))] * shards
        + [pl.BlockSpec((particles, 2, rows // steps, cols), lambda i: (0, 0, i, 0))],
        compiler_params=params(56),
        name="prep",
    )(ids, w_flat)

    w_routes = []
    if shards == 4:
        for own, far_by in ((True, 1), (False, 3), (None, 2)):
            for e in range(2):
                pairs = []
                for m, c, s in devices:
                    at_home = c == s // half
                    if own is None and at_home:
                        pairs.append((dev(m, c, s), dev(m, 1 - e, s)))
                    elif own is None or own == at_home:
                        pairs.append((dev(m, c, s), dev(m, e, s ^ far_by)))
                w_routes.append(pairs)
    else:
        for r in range(shards):
            pairs = []
            for m, c, s in devices:
                q = (s - r) % shards
                pairs.append((dev(m, c, s), dev(m, q % 2, c * half + q // 2)))
            w_routes.append(pairs)

    whole = lax.all_to_all(slices, "particle", 0, 0, tiled=True)

    pair_list = [(i, j) for i in range(particles) for j in range(i)]
    hops = []
    for count, stride in ((particles, shards), (shards, 1)):
        hop = 1
        while hop < count:
            hops.append([(d, d + ((d // stride % count ^ hop) - d // stride % count) * stride) for d in range(len(devices))])
            hop *= 2

    def pair_sums(whole):
        return pl.pallas_call(
            distance_kernel,
            out_shape=jax.ShapeDtypeStruct((8, LANES), F32),
            in_specs=[pl.BlockSpec(memory_space=pltpu.VMEM)],
            out_specs=pl.BlockSpec(memory_space=pltpu.VMEM),
            compiler_params=params(8),
                name="distances",
        )(whole)

    def add_over(sums, steps):
        for step in steps:
            sums = sums + move(sums, hops[step])
        return sums

    def gather_row(ids, which, turn):
        k = lax.rem(ids[SHARD] - which + shards, shards)
        return (turn * (particles // 2) * shards + k) * share

    def place(ids, ref, held, sem, which, turn, start=0):
        row = gather_row(ids, which, turn)
        for i in range(particles // 2):
            to = pl.multiple_of(row + i * shards * share, share)
            pltpu.make_async_copy(
                ref.at[pl.ds(start + i * share, share), :], held.at[pl.ds(to, share), :], sem
            ).start()

    if shards == 4:
        cot = cotangent[0]
        inner = jnp.logical_or(shard == 1, shard == 2)
        flip = jnp.where(jnp.logical_or(inner, core == proc), 0, 1)
        first_routes, second_routes = [], []
        for e in range(2):
            one, two = [], []
            for m, c, s in devices:
                at_home, is_inner = c == s // half, s in (1, 2)
                if not at_home:
                    to, turn = (3 - s, e) if is_inner else (1 if s == 3 else 2, 1 - e)
                    one.append((dev(m, c, s), dev(m, c ^ turn, to)))
                elif is_inner:
                    one.append((dev(m, c, s), dev(m, c ^ e, s ^ 1)))
                else:
                    two.append((dev(m, c, s), dev(m, c ^ e, s ^ 1)))
                if is_inner:
                    two.append((dev(m, c, s), dev(m, c, s ^ 1)))
            first_routes.append(one)
            second_routes.append(two)
        halves = [
            lax.dynamic_slice(cot, (((core + e + flip) % 2) * half_rows, 0), (half_rows, width)) for e in range(2)
        ]
        alpha = [move(x, route) for x, route in zip(halves, first_routes)]
        own_c = move(cot, [(dev(m, c, s), dev(m, 1 - c, s)) for m, c, s in devices if c == s // half])
        normed = shift_tokens(normed)
        w_pieces = [move(x, route) for x, route in zip(prepared[:2], w_routes[:2])]
        alpha, own_c, prepared, normed, w_pieces = lax.optimization_barrier((alpha, own_c, prepared, normed, w_pieces))
        normed = lax.all_gather(normed[None], "particle", axis=0, tiled=True)
        w_pieces = w_pieces + [move(x, route) for x, route in zip(prepared, w_routes[2:])]
        beta = [move(jnp.where(inner, a, x), route) for a, x, route in zip(alpha, halves, second_routes)]
        alpha_x = [move(x, swap_of(everyone)) for x in alpha]
        whole, w_pieces[2:4] = lax.optimization_barrier((whole, w_pieces[2:4]))
        sums = add_over(pair_sums(whole), range(len(hops) - 3))
        w_pieces, normed, sums = lax.optimization_barrier((w_pieces, normed, sums))
        beta_x = [move(x, swap_of(everyone)) for x in beta]
        sources = [cot, own_c, *alpha, *alpha_x, *beta, *beta_x]

        def pick(ids, refs, held, sem):
            s, core, proc = ids[SHARD], ids[CORE], ids[PROC]
            low = s < 2
            near, far, pair = jnp.where(low, 2, 1), jnp.where(low, 3, 0), s + 1 - 2 * lax.rem(s, 2)
            side = lax.rem(core + proc, 2)
            is_inner = jnp.logical_or(s == 1, s == 2)

            def own(ref):
                for turn in range(2):
                    place(ids, ref, held, sem, s, turn, turn * half_rows)

            def others(main, main_x, rest, rest_x):
                for e in range(2):
                    same = side == e
                    place(ids, main[e], held, sem, jnp.where(same, near, far), core)
                    place(ids, main_x[e], held, sem, jnp.where(same, far, near), 1 - core)

                    @pl.when(same)
                    def _():
                        place(ids, rest[e], held, sem, pair, core)
                        place(ids, rest_x[1 - e], held, sem, pair, 1 - core)

            @pl.when(side == 0)
            def _():
                own(refs[0])

            @pl.when(side == 1)
            def _():
                own(refs[1])

            @pl.when(is_inner)
            def _():
                others(refs[2:4], refs[4:6], refs[6:8], refs[8:10])

            @pl.when(jnp.logical_not(is_inner))
            def _():
                others(refs[6:8], refs[8:10], refs[2:4], refs[4:6])
    else:
        full = lax.all_gather(cotangent[0], "shard", axis=0, tiled=True)
        sources = [jnp.where(core == proc, full, move(full, swap_of(everyone)))]
        w_pieces = [move(x, route) for x, route in zip(prepared, w_routes)]
        normed = lax.all_gather(shift_tokens(normed)[None], "particle", axis=0, tiled=True)
        sums = add_over(pair_sums(whole), range(len(hops) - 3))

        def pick(ids, refs, held, sem):
            def one(which, carry):
                for turn in range(2):
                    start = pl.multiple_of(which * tok_rows + turn * half_rows, half_rows)
                    place(ids, refs[0], held, sem, which, turn, start)
                return carry

            lax.fori_loop(0, shards, one, 0)

    normed = normed.reshape(tokens, width)
    act_t, slope, down_w = pl.pallas_call(
        functools.partial(up_kernel, shards, width ** (-0.5)),
        grid=(blocks,),
        out_shape=[
            jax.ShapeDtypeStruct((part, tokens), BF),
            jax.ShapeDtypeStruct((tokens, part), BF),
            jax.ShapeDtypeStruct((width, part), BF),
        ],
        in_specs=[smem_spec(), pl.BlockSpec((BLOCK, width), lambda i: (i, 0))]
        + [pl.BlockSpec((2, rows, part), lambda i: (0, 0, 0))] * len(w_pieces),
        out_specs=[
            pl.BlockSpec((part, BLOCK), lambda i: (0, i)),
            pl.BlockSpec((BLOCK, part), lambda i: (i, 0)),
            pl.BlockSpec((width, part), lambda i: (0, 0)),
        ],
        scratch_shapes=[pltpu.VMEM((width, part), BF)],
        compiler_params=params(56),
        name="up",
    )(ids, normed, *w_pieces)

    sums = add_over(sums, [-3])
    sums, act_t, slope = lax.optimization_barrier((sums, act_t, slope))
    grad_scale = 1.0 / (tokens * width)
    scores = pl.pallas_call(
        functools.partial(
            grad_kernel,
            shards,
            particles,
            -(width ** (-0.5)) * grad_scale,
            -(hidden ** (-0.5)) * grad_scale,
            hidden ** (-0.5),
            pick,
        ),
        out_shape=[jax.ShapeDtypeStruct((2, rows, cols), BF)] * particles,
        in_specs=[smem_spec()] + [any_spec()] * (4 + len(sources)),
        out_specs=[any_spec()] * particles,
        scratch_shapes=[
            pltpu.VMEM((tokens, width), BF),
            pltpu.VMEM((tokens, width), BF),
            pltpu.VMEM((part, tokens), BF),
            pltpu.VMEM((tokens, part), BF),
            pltpu.VMEM((part, tokens), BF),
            pltpu.VMEM((width, part), BF),
            pltpu.VMEM((2, width, part), BF),
            pltpu.SemaphoreType.DMA((particles + 5,)),
        ],
        compiler_params=params(56),
        name="grads",
    )(ids, normed, act_t, slope, down_w, *sources)

    sums = add_over(sums, [-2])
    sums, *scores = lax.optimization_barrier((sums, *scores))

    ratio = particles // shards
    arrived = []
    for t in range(particles):
        pairs = []
        for m, c, s in devices:
            mine, q = 2 * m + s // half, 2 * (s % half) + c
            u = (mine + ratio * q - t) % particles
            z, e = u // ratio, q * ratio + u % ratio
            pairs.append((dev(m, c, s), dev(e // 2 + z, e % 2, z)))
        arrived.append(move(scores[t], pairs))

    sums = add_over(sums, [-1])
    first_moment, second_moment, sums, *arrived[:5] = lax.optimization_barrier(
        (flat(first_moment), flat(second_moment), sums, *arrived[:5])
    )
    first_moment, second_moment = 0.9 * first_moment, 0.999 * second_moment
    sums = sums[0]
    lookup = [
        [pair_list.index((max(i, j), min(i, j))) if i != j else len(pair_list) for j in range(particles)]
        for i in range(particles)
    ]
    table = jnp.concatenate([sums[: len(pair_list)], jnp.zeros((1,), F32)])
    distances = table[jnp.array(lookup, jnp.int32)]
    inverse_band = 1.0 / kernel_scale[0].astype(F32)
    repulse = 2.0 * inverse_band
    kernel = jnp.exp(-distances * inverse_band)
    scale = 2 * width * hidden / particles
    coef = jnp.concatenate(
        [(scale * kernel).reshape(-1), scale * repulse * jnp.sum(kernel, axis=1), repulse[None]]
    )

    fields = pl.pallas_call(
        functools.partial(stein_kernel, shards, particles),
        out_shape=[jax.ShapeDtypeStruct((2, rows, cols), BF)] * particles,
        in_specs=[smem_spec(), smem_spec(), pl.BlockSpec(memory_space=pltpu.VMEM)] + [any_spec()] * particles,
        out_specs=[any_spec()] * particles,
        scratch_shapes=[
            pltpu.VMEM((particles, 2, rows, cols), BF),
            pltpu.VMEM((particles, 2, rows, cols), BF),
            pltpu.VMEM((particles, min(rows, 64), LANES), F32),
            pltpu.SemaphoreType.DMA((particles,)),
        ],
        compiler_params=params(12),
        name="stein",
    )(ids, coef, whole, *arrived)

    back = []
    for k in range(columns):
        for x in range(2):
            pairs = [(dev(m, c, s), dev(m + k, c ^ x, s)) for m, c, s in devices]
            back.append(move(fields[2 * k + x], pairs))

    steps = max(rows // 32, 1)
    flat_rows = rows * 2 * lane_tiles
    state_spec = pl.BlockSpec((flat_rows // steps, LANES), lambda i: (i, 0))
    outs = pl.pallas_call(
        functools.partial(adam_kernel, particles),
        grid=(steps,),
        out_shape=[jax.ShapeDtypeStruct((flat_rows, LANES), F32)] * 4,
        in_specs=[smem_spec()] + [state_spec] * 3 + [any_spec()] * particles,
        out_specs=[state_spec] * 4,
        scratch_shapes=[pltpu.VMEM((2, rows, hidden), BF), pltpu.SemaphoreType.DMA((particles,))],
        compiler_params=params(20),
        name="adam",
    )(ids, w_flat, first_moment, second_moment, *back)
    return tuple(unflat(x) for x in outs)


def solution(mesh):
    state = P("particle", "shard", None, None)
    return jax.shard_map(
        local,
        mesh=mesh,
        in_specs=(P("shard", None), P("shard"), P(), P("particle", "shard", None), state, state, state),
        out_specs=(state, state, state, state),
        check_vma=False,
    )
```
